32 devices in a mesh: expert: 8 (over z, y), wshard: 4 (over x, core).
Axes of the slice: x: 2, y: 2, z: 4, core: 2. Of those that a mesh axis runs over, the one named last changes fastest.
Arguments:
- tokens: bfloat16 [4096, 768], P(('expert', 'wshard')), may hold values from -6 to 6
- routes: int32 [4096, 2], P(('expert', 'wshard')), may hold values from 0 to 7, all different within a row; in each aligned block of 128 rows (0 to 127, 128 to 255, ...) at most 48 rows name the same one
- buckets: int32 [4096, 512], P(('expert', 'wshard')), may hold values from 0 to 31
- gain_one: bfloat16 [768], P('wshard'), may hold values from 0.5 to 1.5
- w_query: bfloat16 [768, 768], P('wshard'), may hold values from -0.21875 to 0.21875
- w_key: bfloat16 [768, 768], P('wshard'), may hold values from -0.21875 to 0.21875
- w_value: bfloat16 [768, 768], P('wshard'), may hold values from -0.21875 to 0.21875
- w_output: bfloat16 [768, 768], P('wshard'), may hold values from -1.75 to 1.75
- pos_bias: bfloat16 [12, 32], P('wshard'), may hold values from -3 to 3
- gain_two: bfloat16 [768], P('wshard'), may hold values from 0.5 to 1.5
- w_router: bfloat16 [768, 8], P('wshard'), may hold values from -0.15625 to 0.15625
- expert_in: bfloat16 [8, 768, 3072], P('expert', None, 'wshard'), may hold values from -0.21875 to 0.21875
- expert_out: bfloat16 [8, 3072, 768], P('expert', 'wshard'), may hold values from -0.109375 to 0.109375
- grad_out: bfloat16 [4096, 768], P(('expert', 'wshard')), may hold values from -6 to 6
Outputs:
- block_out: bfloat16 [4096, 768], P(('expert', 'wshard'))
- grad_tokens: float32 [4096, 768], P(('expert', 'wshard'))
- grad_gain_one: float32 [768], P('wshard')
- grad_w_query: float32 [768, 768], P('wshard')
- grad_w_key: float32 [768, 768], P('wshard')
- grad_w_value: float32 [768, 768], P('wshard')
- grad_w_output: float32 [768, 768], P('wshard')
- grad_pos_bias: float32 [12, 32], P('wshard')
- grad_gain_two: float32 [768], P('wshard')
- grad_w_router: float32 [768, 8], P('wshard')
- grad_expert_in: float32 [8, 768, 3072], P('expert', None, 'wshard')
- grad_expert_out: float32 [8, 3072, 768], P('expert', 'wshard')
The draws below stay inside these ranges and needn't reach their ends.
Inputs may be any that keep to these rules, and one draw needn't show every extreme that they name: `routes`: each row names 2 different experts. Among the 128 rows of one device (aligned blocks) no expert is named more than 48 times, a bound that some block reaches.
All inputs are finite; a program needn't handle non-finite values.
Results may differ from the reference program's by a relative error of at most 0.015.
Values may be sent and summed in bfloat16 or wider, within the bound.
No kernel may reach another device: no remote copies, remote signals or barrier semaphores. Data moves between devices by JAX's collectives and lax.ppermute only.
A program may use at most 128 MiB of HBM per device.

```python
import math
import jax
import jax.numpy as jnp
import numpy as np
from jax import lax

D = 768
H = 12
DH = 64
FF = 3072
TOPK = 2
NB = 32
TOK_DEV = 128
EXPERTS = 8
CAP = 48
LEN = 512
SEQS = 8
TOKENS = 4096


def touch_ends(entries, stream_key, smallest, high):
    spot = [jax.random.randint(jax.random.fold_in(stream_key, axis), (), 0, length) for axis, length in enumerate(entries.shape)]
    main_axis = entries.shape.index(max(entries.shape))
    beside = spot[:main_axis] + [(spot[main_axis] + 1) % entries.shape[main_axis]] + spot[main_axis + 1:]
    return entries.at[tuple(spot)].set(smallest).at[tuple(beside)].set(high)


def block_scale(stream_key, dims, split, low, high):
    level = 1.0
    for dim, parts in split:
        draws = jax.random.uniform(jax.random.fold_in(jax.random.fold_in(stream_key, 6), dim), (parts,), jnp.float32, low / len(split), high / len(split))
        level = level * jnp.repeat(jnp.exp(draws), dims[dim] // parts).reshape((-1,) + (1,) * (len(dims) - 1 - dim))
    return level


def routed_block(rng, own, number, rows, count, top, limit, slope):
    sequence = jax.random.permutation(rng, count)
    packed, ordinary = portions_of(count, rows * top, limit, slope, True), portions_of(count, rows * top, limit, slope, False)
    places = jnp.arange(count)

    def named(sizes, turn):
        used = int((sizes > 0).sum())
        fixed = max(1, used // 4)
        moved = fixed + (places - fixed + turn * (used - fixed)) % max(1, count - fixed)
        return jnp.zeros((count,), jnp.int32).at[sequence[jnp.where(places < fixed, places, moved)]].set(jnp.asarray(sizes, jnp.int32))

    sizes = jnp.where(number % 4 == 0, named(packed, number // 4), named(ordinary, number - number // 4 - 1))
    mixed = jax.random.permutation(jax.random.fold_in(own, 3), count)
    giver, receiver = mixed[0:count // 2 * 2:2], mixed[1:count // 2 * 2:2]
    slack = jnp.minimum(sizes[giver] - 1, limit - sizes[receiver]) // 2
    slack = jnp.where((giver == sequence[0]) | (receiver == sequence[0]) | (sizes[receiver] == 0), 0, jnp.maximum(slack, 0))
    moved = jax.random.randint(jax.random.fold_in(own, 4), (count // 2,), 0, 1 << 20) % (slack + 1)
    sizes = sizes.at[giver].add(-moved).at[receiver].add(moved)
    members = jnp.searchsorted(jnp.cumsum(sizes), jnp.arange(rows * top), side="right").astype(jnp.int32)
    grid = members.reshape(top, rows).T
    grid = grid[jax.random.permutation(jax.random.fold_in(own, 1), rows)]
    turn = jax.random.randint(jax.random.fold_in(own, 2), (rows, 1), 0, top)
    return jnp.take_along_axis(grid, (jnp.arange(top)[None, :] + turn) % top, axis=1)


def portions_of(amount, total, bound, skew, full):
    portions = [(1 << 20) // math.isqrt(grade ** skew) + 1 for grade in range(1, amount + 1)]
    largest = bound if full else min(bound, max(-(-total // amount), total * portions[0] // sum(portions)))
    least = 1 if total - largest >= amount - 1 else 0
    given, surplus = [largest] + [least] * (amount - 1), total - largest - least * (amount - 1)
    while surplus > 0:
        candidates = [i for i in range(1, amount) if given[i] < largest] or [i for i in range(1, amount) if given[i] < bound]
        mass, budget = sum([portions[i] for i in candidates]), surplus
        for i in candidates:
            more = min(bound - given[i], max(1, budget * portions[i] // mass), surplus)
            given[i] = given[i] + more
            surplus = surplus - more
    return np.array(given)


def noise(stream_key, extent, deviation, limit, split=(), kind=jnp.bfloat16):
    array = deviation * jax.random.normal(stream_key, extent, jnp.float32)
    if split:
        array = array * block_scale(stream_key, extent, split, -0.22, 0.18)
    return jnp.clip(array, -limit, limit).astype(kind)


def setup_inputs(seed: int = 0) -> dict:
    arg_keys = jax.random.split(jax.random.key(seed), 15)
    tokens = noise(arg_keys[0], (TOKENS, D), 1.0, 6.0, ((0, 32),))
    routes_keys = jax.random.split(jax.random.fold_in(arg_keys[1], 1), TOKENS // TOK_DEV)
    routes_turns = jax.random.permutation(jax.random.fold_in(arg_keys[1], 3), TOKENS // TOK_DEV)
    routes = jax.vmap(lambda own, number: routed_block(jax.random.fold_in(arg_keys[1], 2), own, number, TOK_DEV, EXPERTS, TOPK, CAP, 1))(routes_keys, routes_turns).reshape((TOKENS, TOPK))
    buckets = touch_ends(jax.random.randint(arg_keys[2], (TOKENS, LEN), 0, NB), jax.random.fold_in(arg_keys[2], 1), 0, NB - 1).astype(jnp.int32)
    gain_one = jnp.clip(1.0 + 0.1 * jax.random.normal(arg_keys[3], (D,), jnp.float32), 0.5, 1.5).astype(jnp.bfloat16)
    w_query = noise(arg_keys[4], (D, D), D ** -0.5, 0.21875, ((0, 4),))
    w_key = noise(arg_keys[5], (D, D), D ** -0.5, 0.21875, ((0, 4),))
    w_value = noise(arg_keys[6], (D, D), D ** -0.5, 0.21875, ((0, 4),))
    w_output = noise(arg_keys[7], (D, D), (D // 64) ** -0.5, 1.75, ((0, 4),))
    pos_bias = noise(arg_keys[8], (H, NB), 0.5, 3.0, ((0, 4),))
    gain_two = jnp.clip(1.0 + 0.1 * jax.random.normal(arg_keys[9], (D,), jnp.float32), 0.5, 1.5).astype(jnp.bfloat16)
    w_router = noise(arg_keys[10], (D, EXPERTS), (2 * D) ** -0.5, 0.15625, ((0, 4),))
    expert_in = noise(arg_keys[11], (EXPERTS, D, FF), D ** -0.5, 0.21875, ((0, 8), (2, 4)))
    expert_out = noise(arg_keys[12], (EXPERTS, FF, D), FF ** -0.5, 0.109375, ((0, 8), (1, 4)))
    grad_out = noise(arg_keys[13], (TOKENS, D), 1.0, 6.0, ((0, 32),))
    return {"tokens": tokens, "routes": routes, "buckets": buckets, "gain_one": gain_one, "w_query": w_query, "w_key": w_key, "w_value": w_value, "w_output": w_output, "pos_bias": pos_bias, "gain_two": gain_two, "w_router": w_router, "expert_in": expert_in, "expert_out": expert_out, "grad_out": grad_out}


epsilon = 1e-06
highest = lax.Precision.HIGHEST

@jax.custom_vjp
def low(v):
    return lax.optimization_barrier(v.astype(jnp.bfloat16)).astype(jnp.float32)

@jax.custom_vjp
def low_back(v):
    return v

def low_keep(v):
    return (low(v), None)

def low_pass(kept, grad):
    return (grad,)

def back_keep(v):
    return (v, None)

def back_low(kept, grad):
    return (low(grad),)
low.defvjp(low_keep, low_pass)
low_back.defvjp(back_keep, back_low)

def matmul(left, right):
    return jnp.dot(left, right, precision=highest, preferred_element_type=jnp.float32)

def rms_norm(values, gain):
    scale = lax.rsqrt(lax.optimization_barrier(jnp.mean(values * values, axis=-1, keepdims=True)) + epsilon)
    return values * scale * gain

def softmax_last(scores):
    shifted = scores - lax.optimization_barrier(jnp.max(scores, axis=-1, keepdims=True))
    exp_scores = jnp.exp(shifted)
    return exp_scores / lax.optimization_barrier(jnp.sum(exp_scores, axis=-1, keepdims=True))

def attend_group(bias_table, inputs):
    queries, key_rows, value_rows, bucket_ids = inputs
    group_size = queries.shape[0]
    head_shape = (group_size, LEN, H, DH)
    raw_scores = jnp.einsum('gthd,gshd->ghts', queries.reshape(head_shape), key_rows.reshape(head_shape), precision=highest) * 0.125
    biases = jnp.transpose(bias_table[:, bucket_ids], (1, 0, 2, 3))
    positions = jnp.arange(LEN, dtype=jnp.int32)
    causal = positions[None, :] <= positions[:, None]
    scores = jnp.where(causal[None, None], low_back(raw_scores) + biases, -1000000000.0)
    weights = softmax_last(scores)
    mixed_heads = jnp.einsum('ghts,gshd->gthd', low(weights), value_rows.reshape(head_shape), precision=highest)
    return mixed_heads.reshape(group_size, LEN, D)

def expert_apply(inputs):
    slot_rows, weight_in, weight_out = inputs
    hidden = low(jax.nn.gelu(low_back(matmul(slot_rows, weight_in))))
    return low(low_back(matmul(hidden, weight_out)))

def reference(tokens, routes, buckets, gain_one, w_query, w_key, w_value, w_output, pos_bias, gain_two, w_router, expert_in, expert_out, grad_out):
    blocks = TOKENS // TOK_DEV
    group_size = math.gcd(SEQS, max(1, 4096 // LEN))
    group_count = SEQS // group_size
    chosen = (routes[:, :, None] == jnp.arange(EXPERTS, dtype=jnp.int32)[None, None, :]).astype(jnp.int32)
    chosen_flat = chosen.reshape(blocks, TOK_DEV * TOPK, EXPERTS)
    before = jnp.cumsum(chosen_flat, axis=1) - chosen_flat
    slot_ids = lax.optimization_barrier(jnp.sum(before * chosen_flat, axis=-1)).reshape(TOKENS, TOPK).astype(jnp.int32)
    block_ids = jnp.broadcast_to((jnp.arange(TOKENS, dtype=jnp.int32) // TOK_DEV)[:, None], (TOKENS, TOPK))
    bucket_groups = buckets.reshape(group_count, group_size, LEN, LEN)

    def forward(x_float, gain_a, query_w, key_w, value_w, output_w, bias_w, gain_b, router_w, weights_in, weights_out):
        normed_one = low(rms_norm(x_float, gain_a))
        queries = low(low_back(matmul(normed_one, query_w)))
        key_rows = low(low_back(matmul(normed_one, key_w)))
        value_rows = low(low_back(matmul(normed_one, value_w)))
        grouped = (queries.reshape(group_count, group_size, LEN, D), key_rows.reshape(group_count, group_size, LEN, D), value_rows.reshape(group_count, group_size, LEN, D), bucket_groups)
        mixed = lax.map(jax.checkpoint(lambda inputs: attend_group(bias_w, inputs)), grouped).reshape(TOKENS, D)
        mixed = low(low_back(mixed))
        residual = x_float + low_back(matmul(mixed, output_w))
        normed_two = low(rms_norm(residual, gain_b))
        logits = matmul(normed_two, router_w)
        picked = jnp.take_along_axis(logits, routes, axis=1)
        gate_probs = softmax_last(picked)
        copies = jnp.broadcast_to(normed_two[:, None, :], (TOKENS, TOPK, D))
        buffer = jnp.zeros((EXPERTS, blocks, CAP, D), jnp.float32).at[routes, block_ids, slot_ids].set(copies)
        buffer = low_back(buffer).reshape(EXPERTS, blocks * CAP, D)
        results = lax.map(jax.checkpoint(expert_apply), (buffer, weights_in, weights_out))
        results = results.reshape(EXPERTS, blocks, CAP, D)
        per_choice = results[routes, block_ids, slot_ids]
        return residual + lax.optimization_barrier(jnp.sum(gate_probs[:, :, None] * per_choice, axis=1))
    params = (tokens, gain_one, w_query, w_key, w_value, w_output, pos_bias, gain_two, w_router, expert_in, expert_out)
    params = tuple((item.astype(jnp.float32) for item in params))
    block_out, pullback = jax.vjp(forward, *params)
    grads = pullback(grad_out.astype(jnp.float32))
    return (block_out.astype(jnp.bfloat16), grads[0], grads[1], grads[2], grads[3], grads[4], grads[5], grads[6], grads[7], grads[8], grads[9], grads[10])
```

```python
import functools

import jax
import jax.numpy as jnp
from jax import lax
from jax.experimental import pallas as pl
from jax.experimental.pallas import tpu as pltpu
from jax.sharding import PartitionSpec as P

TOPK = 2
epsilon = 1e-06
bf16 = jnp.bfloat16
f32 = jnp.float32
NN = (((1,), (0,)), ((), ()))
NT = (((1,), (1,)), ((), ()))
TN = (((0,), (0,)), ((), ()))


def mm(left, right, dims=NN):
    return lax.dot_general(left, right, dims, preferred_element_type=f32)


def send_xor(value, axis, k):
    n = lax.axis_size(axis)
    return lax.ppermute(value, axis, [(i, i ^ k) for i in range(n)])


def to_xor(stacked, axis, dim=0):
    n = stacked.shape[dim]
    return jnp.take(stacked, jnp.arange(n) ^ lax.axis_index(axis), axis=dim)


def exchange(parts, axis):
    n = len(parts)
    if n <= 8:
        return [parts[0]] + [send_xor(parts[k], axis, k) for k in range(1, n)]
    got = lax.all_to_all(to_xor(jnp.stack(parts), axis), axis, 0, 0, tiled=True)
    got = to_xor(got, axis)
    return [got[k] for k in range(n)]


def spread(value, axis):
    n = lax.axis_size(axis)
    if n <= 8:
        return [value] + [send_xor(value, axis, k) for k in range(1, n)]
    got = to_xor(lax.all_gather(value, axis), axis)
    return [got[k] for k in range(n)]


def gather_w(value):
    across = send_xor(value, "wshard", 2)
    beside = send_xor(value, "wshard", 1)
    return [value, beside, across, send_xor(across, "wshard", 1)]


def scatter_w(parts):
    other = send_xor(parts[3], "wshard", 1)
    pair = (parts[2].astype(f32) + other.astype(f32)).astype(bf16)
    across = send_xor(pair, "wshard", 2)
    beside = send_xor(parts[1], "wshard", 1)
    return parts[0].astype(f32) + beside.astype(f32) + across.astype(f32)


def attn_forward_kernel(
    w_ref, tok_ref, wqkv_ref, gain_ref, bucket_ref, table_ref,
    mixed_ref, probs_ref, qkv_ref, normed_ref, weight_ref,
):
    w = w_ref[0]
    blocks, rows, width = tok_ref.shape
    shard = width // blocks
    heads = probs_ref.shape[0]
    dim = shard // heads
    for j in range(blocks):
        weight_ref[j * shard : (j + 1) * shard, :] = wqkv_ref[j ^ w]
    for i in range(blocks):
        x = tok_ref[i ^ w].astype(f32)
        scale = lax.rsqrt(jnp.mean(x * x, axis=-1, keepdims=True) + epsilon)
        normed = (x * scale * gain_ref[...]).astype(bf16)
        normed_ref[i * rows : (i + 1) * rows, :] = normed
        qkv_ref[i * rows : (i + 1) * rows, :] = mm(normed, weight_ref[...]).astype(bf16)
    below = lax.broadcasted_iota(jnp.int32, (rows, rows), 1) <= lax.broadcasted_iota(
        jnp.int32, (rows, rows), 0
    )
    for i in range(blocks):
        span = (i + 1) * rows
        ids = bucket_ref[i ^ w].astype(jnp.int32)
        for h in range(heads):
            query = qkv_ref[i * rows : span, h * dim : (h + 1) * dim]
            keys = qkv_ref[:span, shard + h * dim : shard + (h + 1) * dim]
            values = qkv_ref[:span, 2 * shard + h * dim : 2 * shard + (h + 1) * dim]
            raw = mm(query, keys, NT) * 0.125
            table = jnp.broadcast_to(table_ref[h : h + 1, :], (rows, table_ref.shape[1]))
            bias = [
                jnp.take_along_axis(table, ids[:, j * rows : (j + 1) * rows], axis=1)
                for j in range(i + 1)
            ]
            scores = raw + jnp.concatenate(bias, axis=1) if i else raw + bias[0]
            last = jnp.where(below, scores[:, i * rows :], -1000000000.0)
            scores = jnp.concatenate([scores[:, : i * rows], last], axis=1) if i else last
            raised = jnp.exp(scores - jnp.max(scores, axis=-1, keepdims=True))
            probs = raised / jnp.sum(raised, axis=-1, keepdims=True)
            probs_ref[h, i * rows : span, :span] = probs
            mixed_ref[i ^ w, :, h * dim : (h + 1) * dim] = mm(probs.astype(bf16), values).astype(
                bf16
            )


def attn_backward_kernel(
    w_ref, grad_ref, wout_ref, qkv_ref, probs_ref, normed_ref, mixed_ref, wqkv_ref, bucket_ref,
    tok_ref,
    back_ref, gqkv_ref, gout_ref, gbias_ref, ggain_ref,
    weight_ref, gmix_ref, part_ref, grads_ref, scores_ref,
):
    w = w_ref[0]
    blocks, rows, width = grad_ref.shape
    shard = width // blocks
    heads = probs_ref.shape[0]
    dim = shard // heads
    for j in range(blocks):
        weight_ref[j * shard : (j + 1) * shard, :] = wqkv_ref[j ^ w]
    for i in range(blocks):
        grad = grad_ref[i ^ w]
        gmix_ref[i * rows : (i + 1) * rows, :] = mm(grad, wout_ref[...], NT).astype(bf16)
        term = mm(mixed_ref[i ^ w], grad, TN)
        if i == 0:
            gout_ref[...] = term
        else:
            gout_ref[...] += term
    part_ref[...] = jnp.zeros_like(part_ref)
    gbias_ref[...] = jnp.zeros_like(gbias_ref)
    for i in range(blocks):
        span = (i + 1) * rows
        for h in range(heads):
            query = qkv_ref[i * rows : span, h * dim : (h + 1) * dim]
            keys = qkv_ref[:span, shard + h * dim : shard + (h + 1) * dim]
            values = qkv_ref[:span, 2 * shard + h * dim : 2 * shard + (h + 1) * dim]
            gmix = gmix_ref[i * rows : span, h * dim : (h + 1) * dim]
            probs = probs_ref[h, i * rows : span, :span]
            gprobs = mm(gmix, values, NT)
            inner = jnp.sum(probs * gprobs, axis=-1, keepdims=True)
            gscores = probs * (gprobs - inner)
            scores_ref[h, :, :span] = gscores
            low = gscores.astype(bf16)
            grads_ref[i * rows : span, h * dim : (h + 1) * dim] = (mm(low, keys) * 0.125).astype(
                bf16
            )
            part_ref[0, h, :span, :] += mm(low, query, TN)
            part_ref[1, h, :span, :] += mm(probs.astype(bf16), gmix, TN)
        ids = bucket_ref[i ^ w, :, :span].astype(jnp.int32)
        for b in range(32):
            hit = ids == b
            for h in range(heads):
                picked = jnp.where(hit, scores_ref[h, :, :span], 0.0)
                gbias_ref[h, b : b + 1, :] += functools.reduce(
                    lambda p, q: p + q,
                    [
                        jnp.sum(picked[:, j * rows : (j + 1) * rows], axis=0, keepdims=True)
                        for j in range(i + 1)
                    ],
                )
    for h in range(heads):
        grads_ref[:, shard + h * dim : shard + (h + 1) * dim] = (part_ref[0, h] * 0.125).astype(
            bf16
        )
        grads_ref[:, 2 * shard + h * dim : 2 * shard + (h + 1) * dim] = part_ref[1, h].astype(bf16)
    total = jnp.zeros((1, width), f32)
    for i in range(blocks):
        back = mm(grads_ref[i * rows : (i + 1) * rows, :], weight_ref[...], NT)
        back_ref[i ^ w] = back.astype(bf16)
        x = tok_ref[i ^ w].astype(f32)
        scale = lax.rsqrt(jnp.mean(x * x, axis=-1, keepdims=True) + epsilon)
        total += jnp.sum(back * x * scale, axis=0, keepdims=True)
    ggain_ref[...] = total
    gqkv_ref[...] = mm(normed_ref[...], grads_ref[...], TN)


def on_chip(kernel, outs, scratch, scalars, *args):
    return pl.pallas_call(
        kernel,
        out_shape=outs,
        in_specs=[pl.BlockSpec(memory_space=pltpu.SMEM)] * len(scalars)
        + [pl.BlockSpec(memory_space=pltpu.VMEM)] * len(args),
        out_specs=[pl.BlockSpec(memory_space=pltpu.VMEM)] * len(outs),
        scratch_shapes=scratch,
        compiler_params=pltpu.CompilerParams(vmem_limit_bytes=40 * 1024 * 1024),
    )(*scalars, *args)


def body(
    tokens, routes, buckets, gain_one, w_query, w_key, w_value, w_output, pos_bias, gain_two,
    w_router, expert_in, expert_out, grad_out,
):
    rows, width = tokens.shape
    nw, ne = lax.axis_size("wshard"), lax.axis_size("expert")
    w, e = lax.axis_index("wshard"), lax.axis_index("expert")
    w_arr = w.astype(jnp.int32).reshape(1)
    shard = width // nw
    heads, bins = pos_bias.shape
    dim = shard // heads
    seq = rows * nw
    experts = w_router.shape[1]
    cap = 3 * rows * TOPK // (2 * experts)
    slots = experts * cap

    small = jnp.concatenate([gain_one[None], gain_two[None], w_router.T], axis=0)
    small = to_xor(jnp.stack(gather_w(small)), "wshard")
    small = small.transpose(1, 0, 2).reshape(2 + experts, width)
    tok_all = jnp.stack(gather_w(tokens))
    columns = jnp.concatenate(
        [m.reshape(shard, nw, shard) for m in (w_query, w_key, w_value)], axis=2
    ).transpose(1, 0, 2)
    columns = to_xor(columns, "wshard")
    wqkv = jnp.stack(exchange([columns[k] for k in range(nw)], "wshard"))
    bucket_all = jnp.stack(gather_w(buckets.astype(bf16)))
    wout_all = gather_w(w_output)
    gain_a, gain_b = small[0:1].astype(f32), small[1:2].astype(f32)
    router = small[2:]

    chosen = (routes[:, :, None] == jnp.arange(experts, dtype=jnp.int32)).astype(f32)
    both = jnp.sum(chosen, axis=1)
    lower = (
        jnp.arange(rows, dtype=jnp.int32)[None, :] < jnp.arange(rows, dtype=jnp.int32)[:, None]
    )
    before = mm(lower.astype(bf16), both.astype(bf16))
    slot = jnp.sum(before[:, None, :] * chosen, axis=-1).astype(jnp.int32)
    dest = (routes ^ e) * cap + slot
    hot = (dest[:, :, None] == jnp.arange(slots, dtype=jnp.int32)).astype(bf16)
    hot_any = hot[:, 0] + hot[:, 1]
    lane = jnp.zeros((1, 128), f32)
    g_rows = jnp.concatenate(
        [
            mm(hot_any, grad_out, TN),
            mm(hot, routes[:, ::-1].astype(bf16), (((0, 1), (0, 1)), ((), ())))[:, None] + lane,
        ],
        axis=1,
    ).astype(bf16)
    g_rows = g_rows.reshape(experts, cap, width + 128)
    g_mine = jnp.concatenate(exchange([g_rows[k] for k in range(experts)], "expert"))
    g_all = jnp.concatenate(gather_w(g_mine))
    g_in, other = g_all[:, :width], g_all[:, width].astype(jnp.int32)

    table = jnp.zeros((8, 128), f32).at[:heads, :bins].set(pos_bias.astype(f32))
    mixed, probs, qkv, normed_one = on_chip(
        attn_forward_kernel,
        [
            jax.ShapeDtypeStruct((nw, rows, shard), bf16),
            jax.ShapeDtypeStruct((heads, seq, seq), f32),
            jax.ShapeDtypeStruct((seq, 3 * shard), bf16),
            jax.ShapeDtypeStruct((seq, width), bf16),
        ],
        [pltpu.VMEM((width, 3 * shard), bf16)],
        [w_arr],
        tok_all, wqkv, gain_a, bucket_all, table,
    )
    mixed_got = exchange([mixed[k] for k in range(nw)], "wshard")
    x_float = tokens.astype(f32)
    residual = x_float
    for k in range(nw):
        residual = residual + mm(mixed_got[k], wout_all[k])
    scale_two = lax.rsqrt(jnp.mean(residual * residual, axis=-1, keepdims=True) + epsilon)
    normed_two = (residual * scale_two * gain_b).astype(bf16)

    n_rows = mm(hot_any, normed_two, TN).astype(bf16).reshape(experts, cap, width)
    n_mine = jnp.concatenate(exchange([n_rows[k] for k in range(experts)], "expert"))
    n_parts = gather_w(n_mine)
    n_all = jnp.concatenate(n_parts)
    w_in, w_back = expert_in[0], expert_out[0]
    g_hidden = mm(g_in, w_back, NT)
    mine_hot = (jnp.arange(experts) == e).astype(f32)[None, :]
    differ = mine_hot - (jnp.arange(experts)[None, :] == other[:, None]).astype(f32)
    logits = mm(n_all, router, NT)
    gate = jax.nn.sigmoid(jnp.sum(logits * differ, axis=-1, keepdims=True))
    pre = mm(n_all, w_in)
    act, act_back = jax.vjp(jax.nn.gelu, pre)
    hidden = act.astype(bf16)
    g_gate = jnp.sum(act * g_hidden, axis=-1, keepdims=True)
    g_logits = (gate * (1.0 - gate) * g_gate * differ).astype(bf16)
    g_pre = act_back(gate * g_hidden)[0].astype(bf16)
    g_slot = (mm(g_pre, w_in, NT) + mm(g_logits, router)).astype(bf16)
    g_slot = scatter_w([g_slot[k * slots : (k + 1) * slots] for k in range(nw)]).astype(bf16)
    g_slot = g_slot.reshape(experts, cap, width)
    g_back = jnp.concatenate(exchange([g_slot[k] for k in range(experts)], "expert"))

    result = (mm(hidden, w_back) * gate).astype(bf16)
    result = scatter_w([result[k * slots : (k + 1) * slots] for k in range(nw)]).astype(bf16)
    result = result.reshape(experts, cap, width)
    result = jnp.concatenate(exchange([result[k] for k in range(experts)], "expert"))
    block_out = (residual + mm(hot_any, result)).astype(bf16)
    grad_in_w = mm(n_all, g_pre, TN)
    grad_out_w = mm(hidden, (gate * g_in).astype(bf16), TN)
    grad_router = mm(g_logits, n_all, TN)

    grad_float = grad_out.astype(f32)
    g_normed = mm(hot_any, g_back)
    scaled = g_normed * gain_b
    grad_residual = (
        grad_float
        + scale_two * scaled
        - residual * scale_two**3 * jnp.mean(scaled * residual, axis=-1, keepdims=True)
    )
    grad_gain_b = jnp.sum(g_normed * residual * scale_two, axis=0, keepdims=True)
    grad_attn = jnp.stack(gather_w(grad_residual.astype(bf16)))

    back, gqkv, gout, gbias, ggain = on_chip(
        attn_backward_kernel,
        [
            jax.ShapeDtypeStruct((nw, rows, width), bf16),
            jax.ShapeDtypeStruct((width, 3 * shard), f32),
            jax.ShapeDtypeStruct((shard, width), f32),
            jax.ShapeDtypeStruct((heads, bins, 128), f32),
            jax.ShapeDtypeStruct((1, width), f32),
        ],
        [
            pltpu.VMEM((width, 3 * shard), bf16),
            pltpu.VMEM((seq, shard), bf16),
            pltpu.VMEM((2, heads, seq, dim), f32),
            pltpu.VMEM((seq, 3 * shard), bf16),
            pltpu.VMEM((heads, rows, seq), f32),
        ],
        [w_arr],
        grad_attn, w_output, qkv, probs, normed_one, mixed, wqkv, bucket_all, tok_all,
    )
    g_normed_one = scatter_w([back[k] for k in range(nw)])
    scale_one = lax.rsqrt(jnp.mean(x_float * x_float, axis=-1, keepdims=True) + epsilon)
    scaled_one = g_normed_one * gain_a
    grad_tokens = (
        grad_residual
        + scale_one * scaled_one
        - x_float * scale_one**3 * jnp.mean(scaled_one * x_float, axis=-1, keepdims=True)
    )

    piece = shard // ne
    chunks = to_xor(to_xor(gqkv.reshape(nw, ne, piece, 3 * shard), "expert", 1), "wshard")
    chunks = chunks.astype(bf16)
    out_chunks = to_xor(gout.reshape(ne, piece, width), "expert").astype(bf16)
    got = exchange([chunks[:, k] for k in range(ne)], "expert")
    got_out = exchange([out_chunks[k] for k in range(ne)], "expert")
    total = functools.reduce(lambda a, b: a + b, [c.astype(f32) for c in got]).astype(bf16)
    total_out = functools.reduce(lambda a, b: a + b, [c.astype(f32) for c in got_out]).astype(bf16)
    swapped = jnp.stack(exchange([total[k] for k in range(nw)], "wshard"))
    swapped = to_xor(swapped, "wshard").reshape(nw, piece, 3, shard).transpose(1, 2, 0, 3)
    joined = jnp.concatenate([swapped.reshape(piece, 3 * width), total_out], axis=1)
    whole = to_xor(jnp.stack(spread(joined, "expert")), "expert").reshape(shard, 4 * width)
    whole = whole.astype(f32)

    few = jnp.concatenate([ggain, grad_gain_b, grad_router], axis=0)
    few = to_xor(few.reshape(2 + experts, nw, shard).transpose(1, 0, 2), "wshard")
    few = functools.reduce(lambda a, b: a + b, exchange([few[k] for k in range(nw)], "wshard"))
    bias_row = jnp.pad(jnp.sum(gbias, axis=-1), ((0, 0), (0, shard - bins)))
    few = jnp.concatenate([few, bias_row], axis=0)
    if ne <= 8:
        few = functools.reduce(lambda a, b: a + b, spread(few, "expert"))
    else:
        few = lax.psum(few, "expert")
    return (
        block_out,
        grad_tokens,
        few[0],
        whole[:, :width],
        whole[:, width : 2 * width],
        whole[:, 2 * width : 3 * width],
        whole[:, 3 * width :],
        few[2 + experts :, :bins],
        few[1],
        few[2 : 2 + experts].T,
        grad_in_w[None],
        grad_out_w[None],
    )


def solution(mesh):
    placed = (
        P(("expert", "wshard"), None),
        P(("expert", "wshard"), None),
        P(("expert", "wshard"), None),
        P("wshard"),
        P("wshard", None),
        P("wshard", None),
        P("wshard", None),
        P("wshard", None),
        P("wshard", None),
        P("wshard"),
        P("wshard", None),
        P("expert", None, "wshard"),
        P("expert", "wshard", None),
        P(("expert", "wshard"), None),
    )
    return jax.shard_map(
        body,
        mesh=mesh,
        in_specs=placed,
        out_specs=(
            P(("expert", "wshard"), None),
            P(("expert", "wshard"), None),
            P("wshard"),
            P("wshard", None),
            P("wshard", None),
            P("wshard", None),
            P("wshard", None),
            P("wshard", None),
            P("wshard"),
            P("wshard", None),
            P("expert", None, "wshard"),
            P("expert", "wshard", None),
        ),
        check_vma=False,
    )
```

```python
import functools

import jax
import jax.numpy as jnp
from jax import lax
from jax.experimental import pallas as pl
from jax.experimental.pallas import tpu as pltpu
from jax.sharding import PartitionSpec as P

TOPK = 2
epsilon = 1e-06
bf16 = jnp.bfloat16
f32 = jnp.float32
NN = (((1,), (0,)), ((), ()))
NT = (((1,), (1,)), ((), ()))
TN = (((0,), (0,)), ((), ()))


def mm(left, right, dims=NN):
    return lax.dot_general(left, right, dims, preferred_element_type=f32)


def send_xor(value, axis, k):
    n = lax.axis_size(axis)
    return lax.ppermute(value, axis, [(i, i ^ k) for i in range(n)])


def to_xor(stacked, axis, dim=0):
    n = stacked.shape[dim]
    return jnp.take(stacked, jnp.arange(n) ^ lax.axis_index(axis), axis=dim)


def exchange(parts, axis):
    n = len(parts)
    if n <= 8:
        return [parts[0]] + [send_xor(parts[k], axis, k) for k in range(1, n)]
    got = lax.all_to_all(to_xor(jnp.stack(parts), axis), axis, 0, 0, tiled=True)
    got = to_xor(got, axis)
    return [got[k] for k in range(n)]


def spread(value, axis):
    n = lax.axis_size(axis)
    if n <= 8:
        return [value] + [send_xor(value, axis, k) for k in range(1, n)]
    got = to_xor(lax.all_gather(value, axis), axis)
    return [got[k] for k in range(n)]


def gather_w(value):
    across = send_xor(value, "wshard", 2)
    beside = send_xor(value, "wshard", 1)
    return [value, beside, across, send_xor(across, "wshard", 1)]


def after(value, dep):
    return lax.optimization_barrier((value, dep))[0]


def send_rows(parts):
    if len(parts) > 1:
        return exchange(parts, "expert")
    n = lax.axis_size("expert")
    value = parts[0].reshape(n, -1, parts[0].shape[-1])
    got = lax.all_to_all(to_xor(value, "expert"), "expert", 0, 0, tiled=True)
    return [to_xor(got, "expert").reshape(parts[0].shape)]


def store_rows(refs, rows):
    step = rows.shape[0] // len(refs)
    for k, ref in enumerate(refs):
        ref[...] = rows[k * step : (k + 1) * step].astype(ref.dtype)


def load_rows(refs, scratch):
    step = scratch.shape[0] // len(refs)
    for k, ref in enumerate(refs):
        scratch[k * step : (k + 1) * step, :] = ref[...]
    return scratch[...]


def norm_scale(x):
    return lax.rsqrt(jnp.mean(x * x, axis=-1, keepdims=True) + epsilon)


def pack_kernel(w_ref, tok_ref, bucket_ref, small_ref, wq_ref, wk_ref, wv_ref, pack_ref, *col_refs):
    w = w_ref[0]
    rows, width = tok_ref.shape
    shard = wq_ref.shape[0]
    pack_ref[:rows, :width] = tok_ref[...]
    pack_ref[:rows, width:] = bucket_ref[...].astype(f32).astype(bf16)
    pack_ref[rows:, :] = jnp.zeros((pack_ref.shape[0] - rows, pack_ref.shape[1]), bf16)
    pack_ref[rows:, :shard] = small_ref[...]
    blocks = width // shard
    for k in range(blocks):
        for j in range(blocks):

            @pl.when(w ^ k == j)
            def _():
                for i, ref in enumerate((wq_ref, wk_ref, wv_ref)):
                    col_refs[k][:, i * shard : (i + 1) * shard] = ref[
                        :, j * shard : (j + 1) * shard
                    ]


def route_kernel(cap, e_ref, routes_ref, grad_ref, hot_ref, *g_refs):
    e = e_ref[0]
    rows, width = grad_ref.shape
    slots = hot_ref.shape[1]
    first, second = routes_ref[:, 0:1], routes_ref[:, 1:2]
    lanes = lax.broadcasted_iota(jnp.int32, (rows, 128), 1)
    one, two = (lanes == first).astype(f32), (lanes == second).astype(f32)
    lower = lax.broadcasted_iota(jnp.int32, (rows, rows), 1) < lax.broadcasted_iota(
        jnp.int32, (rows, rows), 0
    )
    before = mm(lower.astype(f32).astype(bf16), (one + two).astype(bf16))
    places = lax.broadcasted_iota(jnp.int32, (rows, slots), 1)
    hots = []
    for route, named in ((first, one), (second, two)):
        slot = jnp.sum(before * named, axis=1, keepdims=True).astype(jnp.int32)
        hots.append((places == (route ^ e) * cap + slot).astype(f32))
    hot_ref[...] = (hots[0] + hots[1]).astype(bf16)
    g_rows = mm(hot_ref[...], grad_ref[...], TN)
    wide = jnp.zeros((rows, 128), f32)
    other = mm(hots[0].astype(bf16), (second.astype(f32) + wide).astype(bf16), TN) + mm(
        hots[1].astype(bf16), (first.astype(f32) + wide).astype(bf16), TN
    )
    step = slots // len(g_refs)
    for k, ref in enumerate(g_refs):
        ref[:, :width] = g_rows[k * step : (k + 1) * step].astype(bf16)
        ref[:, width:] = other[k * step : (k + 1) * step].astype(bf16)


def attn_forward_kernel(
    w_ref, pack_a, pack_b, pack_c, pack_d, col_a, col_b, col_c, col_d, table_ref,
    mix_a, mix_b, mix_c, mix_d, probs_ref, qkv_ref, normed_ref, small_ref, weight_ref, ids_ref,
    shift_ref, mixed_ref,
):
    w = w_ref[0]
    packs, cols, mixes = (
        (pack_a, pack_b, pack_c, pack_d), (col_a, col_b, col_c, col_d), (mix_a, mix_b, mix_c, mix_d)
    )
    blocks = len(packs)
    heads, seq, _ = probs_ref.shape
    rows, width = seq // blocks, normed_ref.shape[1]
    shard = width // blocks
    dim = shard // heads
    for k in range(blocks):
        weight_ref[k ^ w] = cols[k][...]
        shift_ref[k ^ w] = packs[k][rows:, :shard]
        ids_ref[k ^ w] = packs[k][:rows, width:].astype(f32).astype(jnp.int32)
    for j in range(blocks):
        small_ref[:, j * shard : (j + 1) * shard] = shift_ref[j]
    gain = small_ref[0:1, :].astype(f32)
    weight = weight_ref[...].reshape(width, 3 * shard)
    for k in range(blocks):
        x = packs[k][:rows, :width].astype(f32)
        normed = (x * norm_scale(x) * gain).astype(bf16)
        place = pl.ds(pl.multiple_of((k ^ w) * rows, rows), rows)
        normed_ref[place, :] = normed
        qkv_ref[place, :] = mm(normed, weight).astype(bf16)
    below = lax.broadcasted_iota(jnp.int32, (rows, rows), 1) <= lax.broadcasted_iota(
        jnp.int32, (rows, rows), 0
    )
    for i in range(blocks):
        span = (i + 1) * rows
        ids = ids_ref[i]
        for h in range(heads):
            query = qkv_ref[i * rows : span, h * dim : (h + 1) * dim]
            keys = qkv_ref[:span, shard + h * dim : shard + (h + 1) * dim]
            values = qkv_ref[:span, 2 * shard + h * dim : 2 * shard + (h + 1) * dim]
            raw = mm(query, keys, NT) * 0.125
            table = jnp.broadcast_to(table_ref[h : h + 1, :], (rows, table_ref.shape[1]))
            bias = [
                jnp.take_along_axis(table, ids[:, j * rows : (j + 1) * rows], axis=1)
                for j in range(i + 1)
            ]
            scores = raw + jnp.concatenate(bias, axis=1) if i else raw + bias[0]
            last = jnp.where(below, scores[:, i * rows :], -1000000000.0)
            scores = jnp.concatenate([scores[:, : i * rows], last], axis=1) if i else last
            raised = jnp.exp(scores - jnp.max(scores, axis=-1, keepdims=True))
            probs = raised / jnp.sum(raised, axis=-1, keepdims=True)
            probs_ref[h, i * rows : span, :span] = probs
            mixed_ref[i, :, h * dim : (h + 1) * dim] = mm(probs.astype(bf16), values).astype(bf16)
    for k in range(blocks):
        mixes[k][...] = mixed_ref[k ^ w]


def project_kernel(
    tok_ref, small_ref, hot_ref, mix_a, mix_b, mix_c, mix_d, out_a, out_b, out_c, out_d,
    residual_ref, *n_refs,
):
    residual = tok_ref[...].astype(f32)
    for mix, out in ((mix_a, out_a), (mix_b, out_b), (mix_c, out_c), (mix_d, out_d)):
        residual = residual + mm(mix[...], out[...])
    residual_ref[...] = residual
    normed = (residual * norm_scale(residual) * small_ref[1:2, :].astype(f32)).astype(bf16)
    store_rows(n_refs, mm(hot_ref[...], normed, TN))


def expert_kernel(
    e_ref, n_ref, g_ref, in_ref, out_ref, small_ref,
    slot_ref, hidden_ref, pre_ref, scaled_ref, logit_ref, gate_ref,
):
    e = e_ref[0]
    rows, width = n_ref.shape
    n, g = n_ref[...], g_ref[:, :width]
    logits = mm(n, small_ref[...], NT)
    lanes = lax.broadcasted_iota(jnp.int32, logits.shape, 1)
    other = g_ref[:, width : width + 1].astype(f32).astype(jnp.int32)
    differ = (lanes == 2 + e).astype(f32) - (lanes == 2 + other).astype(f32)
    gate = 1.0 / (1.0 + jnp.exp(-jnp.sum(logits * differ, axis=-1, keepdims=True)))
    gate_ref[...] = jnp.broadcast_to(gate, gate_ref.shape)
    scaled_ref[...] = (gate * g.astype(f32)).astype(bf16)
    pre = mm(n, in_ref[...])
    back = mm(g, out_ref[...], NT)
    square = pre * pre
    bent = jnp.tanh(0.7978845608028654 * pre * (1.0 + 0.044715 * square))
    hidden = 0.5 * pre * (1.0 + bent)
    hidden_ref[...] = hidden.astype(bf16)
    slope = 0.5 * (1.0 + bent) + 0.5 * pre * (1.0 - bent * bent) * (
        0.7978845608028654 * (1.0 + 3.0 * 0.044715 * square)
    )
    g_gate = jnp.sum(hidden * back, axis=-1, keepdims=True)
    g_logit = (gate * (1.0 - gate) * g_gate * differ).astype(bf16)
    logit_ref[...] = g_logit
    g_pre = (gate * back * slope).astype(bf16)
    pre_ref[...] = g_pre
    slot_ref[...] = (mm(g_pre, in_ref[...], NT) + mm(g_logit, small_ref[...])).astype(bf16)


def result_kernel(*refs):
    parts = (len(refs) - 1) // 3
    for k in range(parts):
        hidden, gate, out = refs[k], refs[parts + k], refs[2 * parts + 1 + k]
        out[...] = (mm(hidden[...], refs[2 * parts][...]) * gate[:, 0:1]).astype(bf16)


def expert_grad_kernel(*refs):
    parts = (len(refs) - 3) // 5
    g_in, g_out, g_router = refs[5 * parts :]
    for k in range(parts):
        n, pre, hidden, scaled, logit = (refs[a * parts + k][...] for a in range(5))
        terms = (mm(n, pre, TN), mm(hidden, scaled, TN), mm(logit, n, TN))
        for ref, term in zip((g_in, g_out, g_router), terms):
            if k == 0:
                ref[...] = term
            else:
                ref[...] += term


def pair_kernel(a_ref, b_ref, out_ref):
    out_ref[...] = (a_ref[...].astype(f32) + b_ref[...].astype(f32)).astype(bf16)


def total_kernel(a_ref, b_ref, c_ref, *out_refs):
    total = a_ref[...].astype(f32) + b_ref[...].astype(f32) + c_ref[...].astype(f32)
    store_rows(out_refs, total)


def second_norm_kernel(*refs):
    residual_ref, small_ref, hot_ref, grad_ref = refs[:4]
    grad_residual_ref, low_ref, gain_ref, scratch = refs[-4:]
    g_normed = mm(hot_ref[...], load_rows(refs[4:-4], scratch))
    residual = residual_ref[...]
    scale = norm_scale(residual)
    scaled = g_normed * small_ref[1:2, :].astype(f32)
    grad = (
        grad_ref[...].astype(f32)
        + scale * scaled
        - residual * scale * scale * scale * jnp.mean(scaled * residual, axis=-1, keepdims=True)
    )
    grad_residual_ref[...] = grad
    low_ref[...] = grad.astype(bf16)
    gain_ref[...] = jnp.sum(g_normed * residual * scale, axis=0, keepdims=True)


def block_out_kernel(*refs):
    residual_ref, hot_ref = refs[:2]
    out_ref, scratch = refs[-2:]
    out_ref[...] = (
        residual_ref[...] + mm(hot_ref[...], load_rows(refs[2:-2], scratch))
    ).astype(bf16)


def attn_backward_kernel(
    w_ref, grad_a, grad_b, grad_c, grad_d, wout_ref, qkv_ref, probs_ref,
    grads_ref, scores_ref, gmix_ref, part_ref,
):
    w = w_ref[0]
    packs = (grad_a, grad_b, grad_c, grad_d)
    blocks = len(packs)
    rows, width = grad_a.shape
    shard = width // blocks
    heads = probs_ref.shape[0]
    dim = shard // heads
    for k in range(blocks):
        place = pl.ds(pl.multiple_of((k ^ w) * rows, rows), rows)
        gmix_ref[place, :] = mm(packs[k][...], wout_ref[...], NT).astype(bf16)
    part_ref[...] = jnp.zeros_like(part_ref)
    for i in range(blocks):
        span = (i + 1) * rows
        for h in range(heads):
            query = qkv_ref[i * rows : span, h * dim : (h + 1) * dim]
            keys = qkv_ref[:span, shard + h * dim : shard + (h + 1) * dim]
            values = qkv_ref[:span, 2 * shard + h * dim : 2 * shard + (h + 1) * dim]
            gmix = gmix_ref[i * rows : span, h * dim : (h + 1) * dim]
            probs = probs_ref[h, i * rows : span, :span]
            gprobs = mm(gmix, values, NT)
            inner = jnp.sum(probs * gprobs, axis=-1, keepdims=True)
            gscores = probs * (gprobs - inner)
            scores_ref[h, i * rows : span, :span] = gscores
            low = gscores.astype(bf16)
            grads_ref[i * rows : span, h * dim : (h + 1) * dim] = (mm(low, keys) * 0.125).astype(
                bf16
            )
            part_ref[0, h, :span, :] += mm(low, query, TN)
            part_ref[1, h, :span, :] += mm(probs.astype(bf16), gmix, TN)
    for h in range(heads):
        grads_ref[:, shard + h * dim : shard + (h + 1) * dim] = (part_ref[0, h] * 0.125).astype(
            bf16
        )
        grads_ref[:, 2 * shard + h * dim : 2 * shard + (h + 1) * dim] = part_ref[1, h].astype(bf16)


def weight_grad_kernel(
    ids_ref, grad_a, grad_b, grad_c, grad_d, mix_a, mix_b, mix_c, mix_d, normed_ref, grads_ref,
    *out_refs,
):
    gqkv = mm(normed_ref[...], grads_ref[...], TN)
    gout = functools.reduce(
        lambda p, q: p + q,
        [
            mm(mix[...], grad[...], TN)
            for mix, grad in (
                (mix_a, grad_a), (mix_b, grad_b), (mix_c, grad_c), (mix_d, grad_d)
            )
        ],
    )
    if len(out_refs) == 2:
        out_refs[0][...] = gqkv
        out_refs[1][...] = gout
        return
    w, e = ids_ref[0], ids_ref[1]
    stage_ref, outs = out_refs[-1], out_refs[:-1]
    ne = len(outs)
    shard, width = gout.shape
    nw = width // shard
    piece = shard // ne
    for j in range(nw):
        for s in range(ne):
            row = j * shard + s * piece
            stage_ref[s, j ^ w, :, : 3 * shard] = gqkv[row : row + piece].astype(bf16)
            stage_ref[s, j, :, 3 * shard :] = gout[
                s * piece : (s + 1) * piece, j * shard : (j + 1) * shard
            ].astype(bf16)
    for k in range(ne):
        outs[k][...] = stage_ref[k ^ e]


def weight_sum_kernel(*refs):
    outs, gout_ref, ins = refs[-5:-1], refs[-1], refs[:-5]
    for k in range(4):
        total = functools.reduce(lambda p, q: p + q, [ref[k].astype(f32) for ref in ins])
        cut = outs[k].shape[1]
        outs[k][...] = total[:, :cut].astype(bf16)
        gout_ref[k] = total[:, cut:].astype(bf16)


def weight_pack_kernel(a_ref, b_ref, c_ref, d_ref, gout_ref, out_ref):
    for k, ref in enumerate((a_ref, b_ref, c_ref, d_ref)):
        cut = ref.shape[1]
        out_ref[k, :, :cut] = ref[...]
        out_ref[k, :, cut:] = gout_ref[k]


def weight_join_kernel(ids_ref, *refs):
    w, e = ids_ref[0], ids_ref[1]
    outs, ins = refs[-4:], refs[:-4]
    nw, piece, width = ins[0].shape
    shard = width // nw
    for k, ref in enumerate(ins):
        place = pl.ds(pl.multiple_of((k ^ e) * piece, piece), piece)
        for j in range(nw):
            mine = ref[j ^ w].astype(f32)
            for i in range(3):
                outs[i][place, j * shard : (j + 1) * shard] = mine[:, i * shard : (i + 1) * shard]
            outs[3][place, j * shard : (j + 1) * shard] = ref[j].astype(f32)[:, 3 * shard :]


def input_grad_kernel(
    w_ref, grads_ref, col_a, col_b, col_c, col_d, pack_a, pack_b, pack_c, pack_d,
    back_a, back_b, back_c, back_d, gain_ref, weight_ref,
):
    w = w_ref[0]
    cols, packs, backs = (
        (col_a, col_b, col_c, col_d),
        (pack_a, pack_b, pack_c, pack_d),
        (back_a, back_b, back_c, back_d),
    )
    blocks = len(cols)
    rows, width = back_a.shape
    for k in range(blocks):
        weight_ref[k ^ w] = cols[k][...]
    weight = weight_ref[...].reshape(width, cols[0].shape[1])
    total = jnp.zeros((1, width), f32)
    for k in range(blocks):
        place = pl.ds(pl.multiple_of((k ^ w) * rows, rows), rows)
        back = mm(grads_ref[place, :], weight, NT)
        backs[k][...] = back.astype(bf16)
        x = packs[k][:rows, :width].astype(f32)
        total += jnp.sum(back * x * norm_scale(x), axis=0, keepdims=True)
    gain_ref[...] = total


def bias_grad_kernel(pack_a, pack_b, pack_c, pack_d, w_ref, scores_ref, out_ref, ids_ref):
    w = w_ref[0]
    packs = (pack_a, pack_b, pack_c, pack_d)
    heads, seq, _ = scores_ref.shape
    blocks = len(packs)
    rows = seq // blocks
    width = pack_a.shape[1] - seq
    for k in range(blocks):
        ids_ref[k ^ w] = packs[k][:rows, width:].astype(f32).astype(jnp.int32)
    bins = out_ref.shape[1]
    out_ref[...] = jnp.zeros_like(out_ref)
    for i in range(blocks):
        span = (i + 1) * rows
        ids = ids_ref[i, :, :span]
        for b in range(bins):
            hit = ids == b
            for h in range(heads):
                picked = jnp.where(hit, scores_ref[h, i * rows : span, :span], 0.0)
                out_ref[h, b : b + 1, :] += functools.reduce(
                    lambda p, q: p + q,
                    [
                        jnp.sum(picked[:, j * rows : (j + 1) * rows], axis=0, keepdims=True)
                        for j in range(i + 1)
                    ],
                )


def tokens_grad_kernel(tok_ref, small_ref, residual_ref, a_ref, b_ref, c_ref, out_ref):
    grad = a_ref[...].astype(f32) + b_ref[...].astype(f32) + c_ref[...].astype(f32)
    x = tok_ref[...].astype(f32)
    scale = norm_scale(x)
    scaled = grad * small_ref[0:1, :].astype(f32)
    out_ref[...] = (
        residual_ref[...]
        + scale * scaled
        - x * scale * scale * scale * jnp.mean(scaled * x, axis=-1, keepdims=True)
    )


def shaped(shape, dtype=bf16):
    return jax.ShapeDtypeStruct(shape, dtype)


def on_chip(kernel, outs, scratch, *args, scalars=(0,), flops=0):
    specs = [
        pl.BlockSpec(memory_space=pltpu.SMEM if i in scalars else pltpu.VMEM)
        for i in range(len(args))
    ]
    size = sum(a.size * a.dtype.itemsize for a in (*args, *outs))
    return pl.pallas_call(
        kernel,
        out_shape=outs,
        in_specs=specs,
        out_specs=[pl.BlockSpec(memory_space=pltpu.VMEM)] * len(outs),
        scratch_shapes=scratch,
        compiler_params=pltpu.CompilerParams(vmem_limit_bytes=40 * 1024 * 1024),
        cost_estimate=pl.CostEstimate(
            flops=flops + 1000 * size, bytes_accessed=size, transcendentals=0
        ),
    )(*args)


def run_expert(e_arr, n, g, w_in, w_out, small):
    slots, width = n.shape
    hidden = w_in.shape[1]
    tile = slots // 2
    rows = lambda cols: pl.BlockSpec((tile, cols), lambda i: (i, 0))
    whole = lambda a: pl.BlockSpec(a.shape, lambda i: (0, 0))
    widths = [(width, bf16), (hidden, bf16), (hidden, bf16), (width, bf16), (small.shape[0], bf16), (128, f32)]
    return pl.pallas_call(
        expert_kernel,
        grid=(2,),
        out_shape=[shaped((slots, c), t) for c, t in widths],
        in_specs=[
            pl.BlockSpec(memory_space=pltpu.SMEM),
            rows(width), rows(width + 128), whole(w_in), whole(w_out), whole(small),
        ],
        out_specs=[rows(c) for c, _ in widths],
        compiler_params=pltpu.CompilerParams(vmem_limit_bytes=40 * 1024 * 1024),
        cost_estimate=pl.CostEstimate(
            flops=6 * slots * width * hidden, bytes_accessed=8 * slots * width * 2, transcendentals=0
        ),
    )(e_arr, n, g, w_in, w_out, small)


def scatter_parts(parts):
    other = send_xor(parts[3], "wshard", 1)
    pair = on_chip(pair_kernel, [shaped(other.shape)], [], parts[2], other, scalars=())[0]
    across = send_xor(pair, "wshard", 2)
    beside = send_xor(parts[1], "wshard", 1)
    return parts[0], beside, across


def body(
    tokens, routes, buckets, gain_one, w_query, w_key, w_value, w_output, pos_bias, gain_two,
    w_router, expert_in, expert_out, grad_out,
):
    rows, width = tokens.shape
    nw, ne = lax.axis_size("wshard"), lax.axis_size("expert")
    w, e = lax.axis_index("wshard"), lax.axis_index("expert")
    w_arr, e_arr = w.astype(jnp.int32).reshape(1), e.astype(jnp.int32).reshape(1)
    ids = jnp.concatenate([w_arr, e_arr])
    shard = width // nw
    heads, bins = pos_bias.shape
    dim = shard // heads
    seq = rows * nw
    experts = w_router.shape[1]
    cap = 3 * rows * TOPK // (2 * experts)
    slots = experts * cap
    pieces = ne if ne <= 8 else 1
    few_rows = -(-(2 + experts) // 16) * 16

    small = jnp.concatenate([gain_one[None], gain_two[None], w_router.T], axis=0)
    small = jnp.pad(small, ((0, few_rows - 2 - experts), (0, 0)))
    pack, *cols = on_chip(
        pack_kernel,
        [shaped((rows + few_rows, width + seq))] + [shaped((shard, 3 * shard))] * nw,
        [],
        w_arr, tokens, buckets, small, w_query, w_key, w_value,
    )
    packs = gather_w(pack)
    cols = exchange(cols, "wshard")
    hot, *g_rows = on_chip(
        functools.partial(route_kernel, cap),
        [shaped((rows, slots))] + [shaped((slots // pieces, width + 128))] * pieces,
        [],
        e_arr, routes, grad_out,
    )
    g_mine = jnp.concatenate(send_rows(g_rows))
    wout_all = gather_w(after(w_output, packs[2]))

    table = jnp.zeros((8, 128), f32).at[:heads, :bins].set(pos_bias.astype(f32))
    *mixed, probs, qkv, normed_one, small = on_chip(
        attn_forward_kernel,
        [shaped((rows, shard))] * nw
        + [
            shaped((heads, seq, seq), f32),
            shaped((seq, 3 * shard)),
            shaped((seq, width)),
            shaped((few_rows, width)),
        ],
        [
            pltpu.VMEM((nw, shard, 3 * shard), bf16),
            pltpu.VMEM((nw, rows, seq), jnp.int32),
            pltpu.VMEM((nw, few_rows, shard), bf16),
            pltpu.VMEM((nw, rows, shard), bf16),
        ],
        w_arr, *packs, *cols, table,
    )
    mixed_got = exchange(mixed, "wshard")
    residual, *n_rows = on_chip(
        project_kernel,
        [shaped((rows, width), f32)] + [shaped((slots // pieces, width))] * pieces,
        [],
        tokens, small, hot, *mixed_got, *wout_all, scalars=(),
    )

    g_parts = gather_w(after(g_mine, mixed_got[2]))
    n_mine = jnp.concatenate(send_rows(n_rows))
    n_parts = gather_w(after(n_mine, g_parts[2]))
    w_in, w_back = expert_in[0], expert_out[0]
    runs = [run_expert(e_arr, n_parts[k], g_parts[k], w_in, w_back, small) for k in range(nw)]
    slot, hidden, g_pre, scaled, g_logit, gate = zip(*runs)
    g_total = on_chip(
        total_kernel, [shaped((slots // pieces, width))] * pieces, [], *scatter_parts(slot),
        scalars=(),
    )
    g_back = send_rows(g_total)

    result = on_chip(
        result_kernel, [shaped((slots, width))] * nw, [], *hidden, *gate,
        after(w_back, g_total[0]), scalars=(),
    )
    r_total = on_chip(
        total_kernel, [shaped((slots // pieces, width))] * pieces, [],
        *after(scatter_parts(result), g_back[-1]), scalars=(),
    )
    g_in_w, g_out_w, g_router = on_chip(
        expert_grad_kernel,
        [
            shaped((width, w_in.shape[1]), f32),
            shaped((w_in.shape[1], width), f32),
            shaped((few_rows, width), f32),
        ],
        [],
        *after(n_parts, g_total[0]), *g_pre, *hidden, *scaled, *g_logit, scalars=(),
        flops=4 * 4 * slots * width * width,
    )

    grad_residual, grad_low, grad_gain_b = on_chip(
        second_norm_kernel,
        [shaped((rows, width), f32), shaped((rows, width)), shaped((1, width), f32)],
        [pltpu.VMEM((slots, width), bf16)],
        residual, small, hot, grad_out, *g_back, scalars=(),
    )
    grad_all = gather_w(grad_low)
    result_back = send_rows(after(r_total, grad_low))
    block_out = on_chip(
        block_out_kernel, [shaped((rows, width))], [pltpu.VMEM((slots, width), bf16)],
        residual, hot, *result_back, scalars=(),
    )[0]

    grads, scores = on_chip(
        attn_backward_kernel,
        [shaped((seq, 3 * shard)), shaped((heads, seq, seq), f32)],
        [pltpu.VMEM((seq, shard), bf16), pltpu.VMEM((2, heads, seq, dim), f32)],
        w_arr, *grad_all, w_output, qkv, probs,
    )
    fast = ne <= 8 and shard % (8 * ne) == 0
    piece = shard // ne
    if fast:
        weight_outs = [shaped((nw, piece, width))] * ne
        weight_scratch = [pltpu.VMEM((ne, nw, piece, width), bf16)]
    else:
        weight_outs = [shaped((width, 3 * shard), f32), shaped((shard, width), f32)]
        weight_scratch = []
    chunks = on_chip(
        weight_grad_kernel, weight_outs, weight_scratch,
        ids, *grad_all, *mixed, normed_one, grads,
    )
    *back, grad_gain_a = on_chip(
        input_grad_kernel,
        [shaped((rows, width))] * nw + [shaped((1, width), f32)],
        [pltpu.VMEM((nw, shard, 3 * shard), bf16)],
        w_arr, grads, *cols, *packs,
    )
    if fast:
        got = exchange(chunks, "expert")
        *sums, gout = on_chip(
            weight_sum_kernel,
            [shaped((piece, 3 * shard))] * nw + [shaped((nw, piece, shard))],
            [],
            *got, scalars=(),
        )
        swapped = exchange(sums, "wshard")
        joined = on_chip(
            weight_pack_kernel, [shaped((nw, piece, width))], [], *swapped, gout, scalars=()
        )[0]
        weights = on_chip(
            weight_join_kernel, [shaped((shard, width), f32)] * 4, [], ids,
            *spread(joined, "expert"),
        )
    else:
        gqkv, gout = chunks
        cut = to_xor(to_xor(gqkv.reshape(nw, ne, piece, 3 * shard), "expert", 1), "wshard")
        cut = cut.astype(bf16)
        out_cut = to_xor(gout.reshape(ne, piece, width), "expert").astype(bf16)
        add = lambda parts: functools.reduce(lambda a, b: a + b, [c.astype(f32) for c in parts])
        total = add(exchange([cut[:, k] for k in range(ne)], "expert")).astype(bf16)
        total_out = add(exchange([out_cut[k] for k in range(ne)], "expert")).astype(bf16)
        swapped = jnp.stack(exchange([total[k] for k in range(nw)], "wshard"))
        swapped = to_xor(swapped, "wshard").reshape(nw, piece, 3, shard).transpose(1, 2, 0, 3)
        joined = jnp.concatenate([swapped.reshape(piece, 3 * width), total_out], axis=1)
        whole = to_xor(jnp.stack(spread(joined, "expert")), "expert").reshape(shard, 4 * width)
        whole = whole.astype(f32)
        weights = [whole[:, i * width : (i + 1) * width] for i in range(4)]
    grad_tokens = on_chip(
        tokens_grad_kernel, [shaped((rows, width), f32)], [], tokens, small, grad_residual,
        *scatter_parts(back), scalars=(),
    )[0]
    gbias = on_chip(
        bias_grad_kernel, [shaped((heads, bins, 128), f32)],
        [pltpu.VMEM((nw, rows, seq), jnp.int32)],
        *packs, w_arr, scores, scalars=(4,),
    )[0]

    few = jnp.concatenate([grad_gain_a, grad_gain_b, g_router[2 : 2 + experts]], axis=0)
    few = to_xor(few.reshape(2 + experts, nw, shard).transpose(1, 0, 2), "wshard")
    few = functools.reduce(lambda a, b: a + b, exchange([few[k] for k in range(nw)], "wshard"))
    bias_row = jnp.pad(jnp.sum(gbias, axis=-1), ((0, 0), (0, shard - bins)))
    few = jnp.concatenate([few, bias_row], axis=0)
    if ne <= 8:
        few = functools.reduce(lambda a, b: a + b, spread(few, "expert"))
    else:
        few = lax.psum(few, "expert")
    return (
        block_out,
        grad_tokens,
        few[0],
        *weights,
        few[2 + experts :, :bins],
        few[1],
        few[2 : 2 + experts].T,
        g_in_w[None],
        g_out_w[None],
    )


def solution(mesh):
    placed = (
        P(("expert", "wshard"), None),
        P(("expert", "wshard"), None),
        P(("expert", "wshard"), None),
        P("wshard"),
        P("wshard", None),
        P("wshard", None),
        P("wshard", None),
        P("wshard", None),
        P("wshard", None),
        P("wshard"),
        P("wshard", None),
        P("expert", None, "wshard"),
        P("expert", "wshard", None),
        P(("expert", "wshard"), None),
    )
    return jax.shard_map(
        body,
        mesh=mesh,
        in_specs=placed,
        out_specs=(
            P(("expert", "wshard"), None),
            P(("expert", "wshard"), None),
            P("wshard"),
            P("wshard", None),
            P("wshard", None),
            P("wshard", None),
            P("wshard", None),
            P("wshard", None),
            P("wshard"),
            P("wshard", None),
            P("expert", None, "wshard"),
            P("expert", "wshard", None),
        ),
        check_vma=False,
    )
```

```python
import functools

import jax
import jax.numpy as jnp
from jax import lax
from jax.experimental import pallas as pl
from jax.experimental.pallas import tpu as pltpu
from jax.sharding import PartitionSpec as P

TOPK = 2
epsilon = 1e-06
bf16 = jnp.bfloat16
f32 = jnp.float32
NN = (((1,), (0,)), ((), ()))
NT = (((1,), (1,)), ((), ()))
TN = (((0,), (0,)), ((), ()))


def mm(left, right, dims=NN):
    return lax.dot_general(left, right, dims, preferred_element_type=f32)


def send_xor(value, axis, k):
    n = lax.axis_size(axis)
    return lax.ppermute(value, axis, [(i, i ^ k) for i in range(n)])


def to_xor(stacked, axis, dim=0):
    n = stacked.shape[dim]
    return jnp.take(stacked, jnp.arange(n) ^ lax.axis_index(axis), axis=dim)


def exchange(parts, axis):
    n = len(parts)
    if n <= 8:
        got = [send_xor(parts[k], axis, k) for k in range(n - 1, 0, -1)]
        return [parts[0]] + got[::-1]
    got = lax.all_to_all(to_xor(jnp.stack(parts), axis), axis, 0, 0, tiled=True)
    got = to_xor(got, axis)
    return [got[k] for k in range(n)]


def spread(value, axis):
    n = lax.axis_size(axis)
    if n <= 8:
        return exchange([value] * n, axis)
    got = to_xor(lax.all_gather(value, axis), axis)
    return [got[k] for k in range(n)]


def gather_w(value):
    across = send_xor(value, "wshard", 2)
    beside = send_xor(value, "wshard", 1)
    return [value, beside, across, send_xor(across, "wshard", 1)]


def send_rows(value, experts):
    blocks = value.reshape(experts, -1, value.shape[-1])
    return lax.all_to_all(blocks, "expert", 0, 0, tiled=True).reshape(value.shape)


def start_copies(pairs, sems, first=0):
    copies = [
        pltpu.make_async_copy(src, dst, sems.at[first + i]) for i, (src, dst) in enumerate(pairs)
    ]
    for copy in copies:
        copy.start()
    return copies


def wait_copies(copies):
    for copy in copies:
        copy.wait()


def norm_scale(x):
    return lax.rsqrt(jnp.mean(x * x, axis=-1, keepdims=True) + epsilon)


def pack_kernel(
    w_ref, one_ref, two_ref, router_ref, tok_ref, bucket_ref, wq_ref, wk_ref, wv_ref,
    far_ref, pack_ref, own_ref, near_ref,
    tok, bucket, wq, wk, wv, one, two, router, sems,
):
    w = w_ref[0]
    copies = start_copies(
        [
            (tok_ref, tok), (bucket_ref, bucket), (wq_ref, wq), (wk_ref, wk), (wv_ref, wv),
            (one_ref, one), (two_ref, two), (router_ref, router),
        ],
        sems,
    )
    wait_copies(copies)
    experts = router.shape[0]
    few_rows = pack_ref.shape[0] - tok.shape[0]
    small = jnp.concatenate(
        [
            one[...].astype(f32).reshape(1, -1),
            two[...].astype(f32).reshape(1, -1),
            router[...].astype(f32),
            jnp.zeros((few_rows - 2 - experts, router.shape[1]), f32),
        ],
        axis=0,
    ).astype(bf16)
    rows, width = tok.shape
    shard = wq.shape[0]
    blocks = width // shard
    half = shard // 2
    pack_ref[:rows, :width] = tok[...]
    pack_ref[:rows, width:] = bucket[...].astype(f32).astype(bf16)
    pack_ref[rows:, :] = jnp.zeros((pack_ref.shape[0] - rows, pack_ref.shape[1]), bf16)
    pack_ref[rows:, :shard] = small
    middle = far_ref.shape[1] // 2
    far_ref[: 2 * half, :] = jnp.zeros((2 * half, far_ref.shape[1]), bf16)
    far_ref[2 * half :, :] = pack_ref[...]
    for j in range(blocks):
        for i, ref in enumerate((wq, wk, wv)):
            at = slice(i * shard, (i + 1) * shard)
            block = ref[:, j * shard : (j + 1) * shard]

            @pl.when(w == j)
            def _():
                own_ref[:, at] = block

            @pl.when(w ^ 1 == j)
            def _():
                near_ref[:, at] = block

            for k in (2, 3):

                @pl.when(w ^ k == j)
                def _():
                    place = slice((k - 2) * half, (k - 1) * half)
                    far_ref[place, i * shard : (i + 1) * shard] = block[:half]
                    far_ref[place, middle + i * shard : middle + (i + 1) * shard] = block[half:]


def route_kernel(cap, routes_ref, grad_ref, hot_ref, g_ref):
    rows, width = grad_ref.shape
    slots = hot_ref.shape[1]
    first, second = routes_ref[:, 0:1], routes_ref[:, 1:2]
    lanes = lax.broadcasted_iota(jnp.int32, (rows, 128), 1)
    one, two = (lanes == first).astype(f32), (lanes == second).astype(f32)
    lower = lax.broadcasted_iota(jnp.int32, (rows, rows), 1) < lax.broadcasted_iota(
        jnp.int32, (rows, rows), 0
    )
    before = mm(lower.astype(f32).astype(bf16), (one + two).astype(bf16))
    places = lax.broadcasted_iota(jnp.int32, (rows, slots), 1)
    hots = []
    for route, named in ((first, one), (second, two)):
        slot = jnp.sum(before * named, axis=1, keepdims=True).astype(jnp.int32)
        hots.append((places == route * cap + slot).astype(f32))
    hot_ref[...] = (hots[0] + hots[1]).astype(bf16)
    g_ref[:, :width] = mm(hot_ref[...], grad_ref[...], TN).astype(bf16)
    wide = jnp.zeros((rows, 128), f32)
    other = mm(hots[0].astype(bf16), (second.astype(f32) + wide).astype(bf16), TN) + mm(
        hots[1].astype(bf16), (first.astype(f32) + wide).astype(bf16), TN
    )
    g_ref[:, width:] = other.astype(bf16)


def forward_kernel(far_ref, out_ref):
    out_ref[...] = far_ref[far_ref.shape[0] - out_ref.shape[0] :, :]


def attn_forward_kernel(
    w_ref, pack_a, pack_b, far_c, far_d, col_a, col_b, table_ref,
    mix_a, mix_b, mix_c, mix_d, small_ref, small_out, probs_out, qkv_out, normed_out, weight_out, token_out,
    ids_out,
    probs_ref, qkv_ref, normed_ref, weight_ref, token_ref, ids_ref, shift_ref, mixed_ref, sems,
):
    w = w_ref[0]
    mixes = (mix_a, mix_b, mix_c, mix_d)
    blocks = len(mixes)
    heads, seq, _ = probs_ref.shape
    rows, width = seq // blocks, normed_ref.shape[1]
    shard = width // blocks
    dim = shard // heads
    half, middle = shard // 2, far_c.shape[1] // 2
    weight_ref[w] = col_a[...]
    weight_ref[1 ^ w] = col_b[...]
    weight_ref[2 ^ w, :half] = far_c[:half, : 3 * shard]
    weight_ref[2 ^ w, half:] = far_c[:half, middle : middle + 3 * shard]
    weight_ref[3 ^ w, :half] = far_d[:half, : 3 * shard]
    weight_ref[3 ^ w, half:] = far_d[:half, middle : middle + 3 * shard]
    packs = ((pack_a, 0), (pack_b, 0), (far_c, 2 * half), (far_d, half))
    for k, (ref, at) in enumerate(packs):
        shift_ref[k ^ w] = ref[at + rows :, :shard]
        ids_ref[k ^ w] = ref[at : at + rows, width:]
    for j in range(blocks):
        small_ref[:, j * shard : (j + 1) * shard] = shift_ref[j]
    gain = small_ref[0:1, :].astype(f32)
    weight = weight_ref[...].reshape(width, 3 * shard)
    for k, (ref, at) in enumerate(packs):
        token_ref[k ^ w] = ref[at : at + rows, :width]
        x = ref[at : at + rows, :width].astype(f32)
        normed = (x * norm_scale(x) * gain).astype(bf16)
        place = pl.ds(pl.multiple_of((k ^ w) * rows, rows), rows)
        normed_ref[place, :] = normed
        qkv_ref[place, :] = mm(normed, weight).astype(bf16)
    copies = start_copies(
        [
            (qkv_ref, qkv_out),
            (normed_ref, normed_out),
            (weight_ref, weight_out),
            (token_ref, token_out),
            (ids_ref, ids_out),
            (small_ref, small_out),
        ],
        sems,
    )
    below = lax.broadcasted_iota(jnp.int32, (rows, rows), 1) <= lax.broadcasted_iota(
        jnp.int32, (rows, rows), 0
    )
    for i in range(blocks):
        span = (i + 1) * rows
        ids = ids_ref[i].astype(f32).astype(jnp.int32)
        for h in range(heads):
            query = qkv_ref[i * rows : span, h * dim : (h + 1) * dim]
            keys = qkv_ref[:span, shard + h * dim : shard + (h + 1) * dim]
            values = qkv_ref[:span, 2 * shard + h * dim : 2 * shard + (h + 1) * dim]
            raw = mm(query, keys, NT) * 0.125
            table = jnp.broadcast_to(table_ref[h : h + 1, :], (rows, table_ref.shape[1]))
            bias = [
                jnp.take_along_axis(table, ids[:, j * rows : (j + 1) * rows], axis=1)
                for j in range(i + 1)
            ]
            scores = raw + jnp.concatenate(bias, axis=1) if i else raw + bias[0]
            last = jnp.where(below, scores[:, i * rows :], -1000000000.0)
            scores = jnp.concatenate([scores[:, : i * rows], last], axis=1) if i else last
            raised = jnp.exp(scores - jnp.max(scores, axis=-1, keepdims=True))
            probs = raised / jnp.sum(raised, axis=-1, keepdims=True)
            probs_ref[h, i * rows : span, :span] = probs
            mixed_ref[i, :, h * dim : (h + 1) * dim] = mm(probs.astype(bf16), values).astype(bf16)
        done = slice(i * rows, span)
        copies += start_copies(
            [(probs_ref.at[:, done, :span], probs_out.at[:, done, :span])], sems, 6 + i
        )
    for k in range(blocks):
        mixes[k][...] = mixed_ref[k ^ w]
    wait_copies(copies)


def project_kernel(
    tok_in, small_ref, hot_in, g_in, mix_a, mix_b, mix_c, mix_d, out_a, out_b, out_c, out_d,
    n_ref, residual_out, g_out, tok_ref, hot_ref, residual_ref, g_ref, sems,
):
    copies = start_copies([(tok_in, tok_ref), (hot_in, hot_ref), (g_in, g_ref)], sems)
    residual = 0.0
    for mix, out in ((mix_a, out_a), (mix_b, out_b), (mix_c, out_c), (mix_d, out_d)):
        residual = residual + mm(mix[...], out[...])
    copies[0].wait()
    residual = residual + tok_ref[...].astype(f32)
    residual_ref[...] = residual
    copies += start_copies([(residual_ref, residual_out)], sems, 3)
    copies[2].wait()
    copies += start_copies([(g_ref, g_out)], sems, 4)
    normed = (residual * norm_scale(residual) * small_ref[1:2, :].astype(f32)).astype(bf16)
    copies[1].wait()
    n_ref[...] = mm(hot_ref[...], normed, TN).astype(bf16)
    wait_copies(copies[3:])


def expert_kernel(firsts, e_ref, *refs):
    e = e_ref[0]
    count = len(firsts)
    n_refs, g_refs, refs = refs[:count], refs[count : 2 * count], refs[2 * count :]
    (in_ref, out_ref, small_ref), slot_refs, refs = refs[:3], refs[3 : 3 + count], refs[3 + count :]
    hidden_out, pre_out, router_out, hidden_ref, pre_ref, router_ref, sems = refs
    rows, width = n_refs[0].shape
    n = jnp.concatenate([ref[...] for ref in n_refs], axis=0)
    g_all = jnp.concatenate(
        [ref[first : first + rows, :] for first, ref in zip(firsts, g_refs)], axis=0
    )
    g = g_all[:, :width]
    logits = mm(n, small_ref[...], NT)
    lanes = lax.broadcasted_iota(jnp.int32, logits.shape, 1)
    other = g_all[:, width : width + 1].astype(f32).astype(jnp.int32)
    differ = (lanes == 2 + e).astype(f32) - (lanes == 2 + other).astype(f32)
    gate = 1.0 / (1.0 + jnp.exp(-jnp.sum(logits * differ, axis=-1, keepdims=True)))
    pre = mm(n, in_ref[...])
    back = mm(g, out_ref[...], NT)
    square = pre * pre
    bent = jnp.tanh(0.7978845608028654 * pre * (1.0 + 0.044715 * square))
    hidden = 0.5 * pre * (1.0 + bent)
    hidden_ref[...] = (gate * hidden).astype(bf16)
    slope = 0.5 * (1.0 + bent) + 0.5 * pre * (1.0 - bent * bent) * (
        0.7978845608028654 * (1.0 + 3.0 * 0.044715 * square)
    )
    g_gate = jnp.sum(hidden * back, axis=-1, keepdims=True)
    g_logit = (gate * (1.0 - gate) * g_gate * differ).astype(bf16)
    router_ref[...] = mm(g_logit, n, TN)
    g_pre = (gate * back * slope).astype(bf16)
    pre_ref[...] = g_pre
    copies = start_copies(
        [(hidden_ref, hidden_out), (pre_ref, pre_out), (router_ref, router_out)], sems
    )
    slot = mm(g_pre, in_ref[...], NT) + mm(g_logit, small_ref[...])
    for i, ref in enumerate(slot_refs):
        ref[...] = slot[i * rows : (i + 1) * rows].astype(bf16)
    wait_copies(copies)


def result_kernel(in_a, in_b, in_c, in_d, w_ref, *refs):
    outs, held, sems = refs[:4], refs[4:8], refs[8]
    copies = start_copies(list(zip((in_a, in_b, in_c, in_d), held)), sems)
    half = outs[0].shape[0] // 2
    for i in range(4):
        copies[i].wait()
        value = mm(held[i][...], w_ref[...]).astype(bf16)
        if i < 2:
            outs[i][...] = value
        else:
            at = slice((i - 2) * half, (i - 1) * half)
            outs[2][at, :] = value[:half]
            outs[3][at, :] = value[half:]


def expert_grad_kernel(plan, *refs):
    n_count = 1 + max(n for pieces in plan for n, _, _ in pieces)
    g_count = 1 + max(g for pieces in plan for _, g, _ in pieces)
    runs = len(plan)
    n_refs, g_refs, refs = refs[:n_count], refs[n_count : n_count + g_count], refs[n_count + g_count :]
    ins, (g_in, g_out, token_ref), refs = refs[: 2 * runs], refs[2 * runs : 2 * runs + 3], refs[2 * runs + 3 :]
    held, sems = refs[: 2 * runs], refs[-1]
    token_ref[...] = jnp.zeros_like(token_ref)
    copies = start_copies(list(zip(ins, held)), sems)
    width = n_refs[0].shape[1]
    first_term = True
    for i, pieces in enumerate(plan):
        copies[i].wait()
        copies[runs + i].wait()
        at = 0
        for n_at, g_at, first in pieces:
            n = n_refs[n_at][...]
            rows = n.shape[0]
            pre, hidden = held[i][at : at + rows, :], held[runs + i][at : at + rows, :]
            g = g_refs[g_at][first : first + rows, :width]
            at += rows
            for ref, term in ((g_in, mm(n, pre, TN)), (g_out, mm(hidden, g, TN))):
                if first_term:
                    ref[...] = term
                else:
                    ref[...] += term
            first_term = False


def pair_kernel(a_ref, b_ref, out_ref):
    out_ref[...] = (a_ref[...].astype(f32) + b_ref[...].astype(f32)).astype(bf16)


def total_kernel(own_ref, beside_ref, *refs):
    across, out_ref = refs[:-1], refs[-1]
    step = out_ref.shape[0] // len(across)
    for a, ref in enumerate(across):
        at = slice(a * step, (a + 1) * step)
        total = own_ref[at, :].astype(f32) + beside_ref[at, :].astype(f32) + ref[...].astype(f32)
        out_ref[at, :] = total.astype(bf16)


def second_norm_kernel(
    residual_in, small_in, hot_in, grad_in, got_ref, low_ref, gain_ref, grad_residual_out,
    residual_ref, small_ref, hot_ref, grad_ref, grad_residual_ref, sems,
):
    copies = start_copies(
        [(hot_in, hot_ref), (residual_in, residual_ref), (small_in, small_ref), (grad_in, grad_ref)],
        sems,
    )
    wait_copies(copies)
    g_normed = mm(hot_ref[...], got_ref[...])
    residual = residual_ref[...]
    scale = norm_scale(residual)
    scaled = g_normed * small_ref[1:2, :].astype(f32)
    grad = (
        grad_ref[...].astype(f32)
        + scale * scaled
        - residual * scale * scale * scale * jnp.mean(scaled * residual, axis=-1, keepdims=True)
    )
    grad_residual_ref[...] = grad
    stores = start_copies([(grad_residual_ref, grad_residual_out)], sems, 4)
    low_ref[...] = grad.astype(bf16)
    gain_ref[...] = jnp.sum(g_normed * residual * scale, axis=0, keepdims=True)
    wait_copies(stores)


def block_out_kernel(residual_ref, hot_ref, got_ref, out_ref):
    out_ref[...] = (residual_ref[...] + mm(hot_ref[...], got_ref[...])).astype(bf16)


def attn_backward_kernel(
    w_ref, grad_a, grad_b, grad_c, grad_d, wout_in, qkv_in, probs_in,
    grads_ref, scores_out,
    wout_ref, qkv_ref, probs_ref, scores_ref, gmix_ref, part_ref, sems,
):
    w = w_ref[0]
    packs = (grad_a, grad_b, grad_c, grad_d)
    blocks = len(packs)
    rows = grad_a.shape[0]
    spans = [(slice(i * rows, (i + 1) * rows), (i + 1) * rows) for i in range(blocks)]
    copies = start_copies(
        [(wout_in, wout_ref), (qkv_in, qkv_ref)]
        + [(probs_in.at[:, at, :span], probs_ref.at[:, at, :span]) for at, span in spans],
        sems,
    )
    copies[0].wait()
    rows, width = grad_a.shape
    shard = width // blocks
    heads = probs_ref.shape[0]
    dim = shard // heads
    for k in range(blocks):
        place = pl.ds(pl.multiple_of((k ^ w) * rows, rows), rows)
        gmix_ref[place, :] = mm(packs[k][...], wout_ref[...], NT).astype(bf16)
    part_ref[...] = jnp.zeros_like(part_ref)
    copies[1].wait()
    stores = []
    for i in range(blocks):
        span = (i + 1) * rows
        copies[2 + i].wait()
        for h in range(heads):
            query = qkv_ref[i * rows : span, h * dim : (h + 1) * dim]
            keys = qkv_ref[:span, shard + h * dim : shard + (h + 1) * dim]
            values = qkv_ref[:span, 2 * shard + h * dim : 2 * shard + (h + 1) * dim]
            gmix = gmix_ref[i * rows : span, h * dim : (h + 1) * dim]
            probs = probs_ref[h, i * rows : span, :span]
            gprobs = mm(gmix, values, NT)
            inner = jnp.sum(probs * gprobs, axis=-1, keepdims=True)
            gscores = probs * (gprobs - inner)
            scores_ref[h, i * rows : span, :span] = gscores
            low = gscores.astype(bf16)
            grads_ref[i * rows : span, h * dim : (h + 1) * dim] = (mm(low, keys) * 0.125).astype(
                bf16
            )
            part_ref[0, h, :span, :] += mm(low, query, TN)
            part_ref[1, h, :span, :] += mm(probs.astype(bf16), gmix, TN)
        at = slice(i * rows, span)
        stores += start_copies(
            [(scores_ref.at[:, at, :span], scores_out.at[:, at, :span])], sems, 2 + blocks + i
        )
    for h in range(heads):
        grads_ref[:, shard + h * dim : shard + (h + 1) * dim] = (part_ref[0, h] * 0.125).astype(
            bf16
        )
        grads_ref[:, 2 * shard + h * dim : 2 * shard + (h + 1) * dim] = part_ref[1, h].astype(bf16)
    wait_copies(stores)


def weight_grad_kernel(
    ids_ref, grad_a, grad_b, grad_c, grad_d, in_a, in_b, in_c, in_d, normed_in, grads_ref,
    *out_refs,
):
    *out_refs, mix_a, mix_b, mix_c, mix_d, normed_ref, sems = out_refs
    copies = start_copies(
        [(normed_in, normed_ref), (in_a, mix_a), (in_b, mix_b), (in_c, mix_c), (in_d, mix_d)], sems
    )
    wait_copies(copies)
    gqkv = mm(normed_ref[...], grads_ref[...], TN)
    gout = functools.reduce(
        lambda p, q: p + q,
        [
            mm(mix[...], grad[...], TN)
            for mix, grad in (
                (mix_a, grad_a), (mix_b, grad_b), (mix_c, grad_c), (mix_d, grad_d)
            )
        ],
    )
    if len(out_refs) == 2:
        out_refs[0][...] = gqkv
        out_refs[1][...] = gout
        return
    w = ids_ref[0]
    stage_ref = out_refs[0]
    ne = stage_ref.shape[0]
    shard, width = gout.shape
    nw = width // shard
    piece = shard // ne
    for j in range(nw):
        for s in range(ne):
            row = j * shard + s * piece
            stage_ref[s, j ^ w, :, : 3 * shard] = gqkv[row : row + piece].astype(bf16)
            stage_ref[s, j, :, 3 * shard :] = gout[
                s * piece : (s + 1) * piece, j * shard : (j + 1) * shard
            ].astype(bf16)


def weight_sum_kernel(in_ref, *refs):
    outs, gout_ref = refs[:-1], refs[-1]
    for k, out in enumerate(outs):
        total = functools.reduce(
            lambda p, q: p + q, [in_ref[i, k].astype(f32) for i in range(in_ref.shape[0])]
        )
        cut = out.shape[1]
        out[...] = total[:, :cut].astype(bf16)
        gout_ref[k] = total[:, cut:].astype(bf16)


def weight_pack_kernel(a_ref, b_ref, c_ref, d_ref, gout_ref, few_ref, bias_ref, out_ref, stage):
    piece, cut = a_ref.shape
    width = stage.shape[1]
    shard = width - cut
    stage[...] = jnp.zeros_like(stage)
    for k, ref in enumerate((a_ref, b_ref, c_ref, d_ref)):
        stage[k * piece : (k + 1) * piece, :cut] = ref[...].astype(f32)
        stage[k * piece : (k + 1) * piece, cut:] = gout_ref[k].astype(f32)
    at = 4 * piece
    few = few_ref[...]
    high = few.astype(bf16).astype(f32)
    stage[at:, :shard] = high
    stage[at:, shard : 2 * shard] = few - high
    bias = bias_ref[...]
    high = bias.astype(bf16).astype(f32)
    stage[at : at + 8, 2 * shard : 2 * shard + 128] = high
    stage[at : at + 8, 2 * shard + 128 : 2 * shard + 256] = bias - high
    out_ref[...] = stage[...].astype(bf16)


def weight_join_kernel(ids_ref, *refs):
    w, e = ids_ref[0], ids_ref[1]
    ins, outs, one_ref, two_ref, router_ref, bias_ref, stage = (
        refs[:-9], refs[-9:-5], refs[-5], refs[-4], refs[-3], refs[-2], refs[-1]
    )
    shard, width = outs[0].shape
    nw, piece = width // shard, stage.shape[1]
    at = nw * piece
    few, bias = 0.0, 0.0
    for k, ref in enumerate(ins):
        place = pl.ds(pl.multiple_of((k ^ e) * piece, piece), piece)
        value = ref[...].astype(f32)
        for j in range(nw):
            mine = value[j * piece : (j + 1) * piece]
            stage[j ^ w] = mine
            outs[3][place, j * shard : (j + 1) * shard] = mine[:, 3 * shard :]
        for j in range(nw):
            mine = stage[j]
            for i in range(3):
                outs[i][place, j * shard : (j + 1) * shard] = mine[:, i * shard : (i + 1) * shard]
        few += value[at:, :shard] + value[at:, shard : 2 * shard]
        bias += (
            value[at : at + 8, 2 * shard : 2 * shard + 128]
            + value[at : at + 8, 2 * shard + 128 : 2 * shard + 256]
        )
    one_ref[...] = few[0:1]
    two_ref[...] = few[1:2]
    router_ref[...] = few[2 : 2 + router_ref.shape[0]]
    heads, bins = bias_ref.shape
    for h in range(heads):
        bias_ref[h : h + 1, :] = bias[0:1, h * bins : (h + 1) * bins]


def input_grad_kernel(
    w_ref, grads_ref, weight_in, token_in, gain_ref, *refs,
):
    *router_in, back_a, back_b, back_c, back_d, few_ref, weight_ref, token_ref, router_ref, sems = (
        refs
    )
    w = w_ref[0]
    wait_copies(
        start_copies(
            [(weight_in, weight_ref), (token_in, token_ref)]
            + [(ref, router_ref.at[i]) for i, ref in enumerate(router_in)],
            sems,
        )
    )
    backs = (back_a, back_b, back_c, back_d)
    blocks, rows, width = token_ref.shape
    shard = width // blocks
    weight = weight_ref[...].reshape(width, 3 * shard)
    total = jnp.zeros((1, width), f32)
    for k in range(blocks):
        place = pl.ds(pl.multiple_of((k ^ w) * rows, rows), rows)
        back = mm(grads_ref[place, :], weight, NT)
        backs[k][:rows, :] = back.astype(bf16)
        x = token_ref[k ^ w].astype(f32)
        total += jnp.sum(back * x * norm_scale(x), axis=0, keepdims=True)
    few = jnp.sum(router_ref[...], axis=0)
    line = lax.broadcasted_iota(jnp.int32, few.shape, 0)
    few = jnp.where(line == 0, total, jnp.where(line == 1, gain_ref[...], few))
    for j in range(blocks):
        few_ref[j] = few[:, j * shard : (j + 1) * shard].astype(bf16)
    for k in range(blocks):
        backs[k][rows:, :] = jnp.zeros((few.shape[0], width), bf16)
        backs[k][rows:, :shard] = few_ref[k ^ w]


def bias_grad_kernel(ids_in, scores_in, out_ref, part_ref, ids_ref, scores_ref, sems):
    wait_copies(start_copies([(ids_in, ids_ref), (scores_in, scores_ref)], sems))
    heads, seq, _ = scores_ref.shape
    blocks, rows, _ = ids_ref.shape
    bins = part_ref.shape[0] // heads
    part_ref[...] = jnp.zeros_like(part_ref)
    for i in range(blocks):
        span = (i + 1) * rows
        ids = ids_ref[i, :, :span].astype(f32).astype(jnp.int32)
        for b in range(bins):
            hit = ids == b
            for h in range(heads):
                picked = jnp.where(hit, scores_ref[h, i * rows : span, :span], 0.0)
                part_ref[h * bins + b : h * bins + b + 1, :] += functools.reduce(
                    lambda p, q: p + q,
                    [
                        jnp.sum(picked[:, j * rows : (j + 1) * rows], axis=0, keepdims=True)
                        for j in range(i + 1)
                    ],
                )
    spread_out = jnp.concatenate(
        [part_ref[...], jnp.zeros((128 - part_ref.shape[0], 128), f32)], axis=0
    )
    out_ref[...] = lax.dot_general(
        jnp.ones((8, 128), f32), spread_out, NT, precision=lax.Precision.HIGHEST,
        preferred_element_type=f32,
    )


def tokens_grad_kernel(
    tok_ref, small_ref, residual_ref, a_ref, b_ref, c_ref, out_ref, few_ref
):
    rows = tok_ref.shape[0]
    shard = few_ref.shape[1]
    total = a_ref[...].astype(f32) + b_ref[...].astype(f32) + c_ref[...].astype(f32)
    grad = total[:rows]
    few_ref[...] = total[rows:, :shard]
    x = tok_ref[...].astype(f32)
    scale = norm_scale(x)
    scaled = grad * small_ref[0:1, :].astype(f32)
    out_ref[...] = (
        residual_ref[...]
        + scale * scaled
        - x * scale * scale * scale * jnp.mean(scaled * x, axis=-1, keepdims=True)
    )


def shaped(shape, dtype=bf16):
    return jax.ShapeDtypeStruct(shape, dtype)


def on_chip(
    kernel, outs, scratch, *args, scalars=(0,), flops=0, stay=(), leave=(), deps=(), limit=32
):
    count = len(args)
    args = [
        pltpu.with_memory_space_constraint(a, pltpu.HBM) if i in stay else a
        for i, a in enumerate(args)
    ]
    places = [
        pltpu.SMEM if i in scalars else pltpu.HBM if i in stay else pltpu.VMEM
        for i in range(count)
    ] + [pl.ANY] * len(deps)

    def run(*refs):
        kernel(*refs[:count], *refs[count + len(deps) :])

    size = sum(a.size * a.dtype.itemsize for a in (*args, *outs))
    return pl.pallas_call(
        run,
        out_shape=[
            pltpu.HBM(a.shape, a.dtype) if i in leave else a for i, a in enumerate(outs)
        ],
        in_specs=[pl.BlockSpec(memory_space=place) for place in places],
        out_specs=[
            pl.BlockSpec(memory_space=pltpu.HBM if i in leave else pltpu.VMEM)
            for i in range(len(outs))
        ],
        scratch_shapes=scratch,
        compiler_params=pltpu.CompilerParams(vmem_limit_bytes=limit * 1024 * 1024),
        cost_estimate=pl.CostEstimate(
            flops=flops + 1000 * size, bytes_accessed=size, transcendentals=0
        ),
    )(*args, *deps)


def run_expert(pieces, e_arr, w_in, w_out, small, deps=()):
    rows, width = pieces[0][0].shape
    hidden = w_in.shape[1]
    count = len(pieces)
    kept = [
        shaped((rows * count, hidden)), shaped((rows * count, hidden)),
        shaped((small.shape[0], width), f32),
    ]
    return on_chip(
        functools.partial(expert_kernel, [first for _, _, first in pieces]),
        [shaped((rows, width))] * count + kept,
        [pltpu.VMEM(a.shape, a.dtype) for a in kept] + [pltpu.SemaphoreType.DMA((3,))],
        e_arr, *[n for n, _, _ in pieces], *[g for _, g, _ in pieces], w_in, w_out, small,
        leave=range(count, count + 3), deps=deps,
    )


def add_pair(mine, other, deps=()):
    other = send_xor(other, "wshard", 1)
    return on_chip(
        pair_kernel, [shaped(other.shape)], [], mine, other, scalars=(), deps=deps
    )[0]


def scatter_parts(parts, deps=()):
    across = send_xor(add_pair(parts[2], parts[3], deps), "wshard", 2)
    beside = send_xor(parts[1], "wshard", 1)
    return parts[0], beside, across


def body(
    tokens, routes, buckets, gain_one, w_query, w_key, w_value, w_output, pos_bias, gain_two,
    w_router, expert_in, expert_out, grad_out,
):
    rows, width = tokens.shape
    nw, ne = lax.axis_size("wshard"), lax.axis_size("expert")
    w, e = lax.axis_index("wshard"), lax.axis_index("expert")
    w_arr, e_arr = w.astype(jnp.int32).reshape(1), e.astype(jnp.int32).reshape(1)
    ids = jnp.concatenate([w_arr, e_arr])
    shard = width // nw
    heads, bins = pos_bias.shape
    dim = shard // heads
    seq = rows * nw
    experts = w_router.shape[1]
    cap = 3 * rows * TOPK // (2 * experts)
    slots = experts * cap
    few_rows = -(-(2 + experts) // 16) * 16

    far, pack, col_own, col_near = on_chip(
        pack_kernel,
        [
            shaped((shard + rows + few_rows, width + seq)),
            shaped((rows + few_rows, width + seq)),
            shaped((shard, 3 * shard)),
            shaped((shard, 3 * shard)),
        ],
        [
            pltpu.VMEM((rows, width), bf16),
            pltpu.VMEM((rows, seq), jnp.int32),
            pltpu.VMEM((shard, width), bf16),
            pltpu.VMEM((shard, width), bf16),
            pltpu.VMEM((shard, width), bf16),
            pltpu.VMEM((shard,), bf16),
            pltpu.VMEM((shard,), bf16),
            pltpu.VMEM((experts, shard), bf16),
            pltpu.SemaphoreType.DMA((8,)),
        ],
        w_arr, gain_one, gain_two, w_router.T, tokens, buckets, w_query, w_key, w_value,
        stay=range(1, 9),
    )
    far_c = send_xor(far, "wshard", 2)
    pack_b, col_b = send_xor(pack, "wshard", 1), send_xor(col_near, "wshard", 1)
    hot, g_rows = on_chip(
        functools.partial(route_kernel, cap),
        [shaped((rows, slots)), shaped((slots, width + 128))],
        [],
        routes, grad_out, scalars=(), deps=(pack_b, col_b),
    )
    g_got = send_rows(g_rows, experts)
    far_rest = on_chip(
        forward_kernel, [shaped((far.shape[0] - shard // 2, far.shape[1]))], [], far_c,
        scalars=(),
    )[0]
    far_d = send_xor(far_rest, "wshard", 1)
    wout_far, wout_near = send_xor(w_output, "wshard", 2), send_xor(w_output, "wshard", 1)

    table = jnp.zeros((8, 128), f32).at[:heads, :bins].set(pos_bias.astype(f32))
    kept = [
        shaped((few_rows, width)),
        shaped((heads, seq, seq), f32),
        shaped((seq, 3 * shard)),
        shaped((seq, width)),
        shaped((nw, shard, 3 * shard)),
        shaped((nw, rows, width)),
        shaped((nw, rows, seq)),
    ]
    *mixed, small, small_far, probs, qkv, normed_one, weight, tok_all, bucket_all = on_chip(
        attn_forward_kernel,
        [shaped((rows, shard))] * nw + [shaped((few_rows, width))] + kept,
        [pltpu.VMEM(a.shape, a.dtype) for a in kept[1:]]
        + [
            pltpu.VMEM((nw, few_rows, shard), bf16),
            pltpu.VMEM((nw, rows, shard), bf16),
            pltpu.SemaphoreType.DMA((6 + nw,)),
        ],
        w_arr, pack, pack_b, far_c, far_d, col_own, col_b, table,
        leave=range(nw + 1, nw + 8), deps=(g_got,),
    )
    mixed_got = exchange(mixed, "wshard")
    wout_rest = on_chip(
        forward_kernel, [shaped(w_output.shape)], [], wout_far, scalars=(), deps=(mixed[0],)
    )[0]
    wout_all = [w_output, wout_near, wout_far, send_xor(wout_rest, "wshard", 1)]
    n_rows, residual, g_mine = on_chip(
        project_kernel,
        [shaped((slots, width)), shaped((rows, width), f32), shaped(g_got.shape)],
        [
            pltpu.VMEM((rows, width), bf16),
            pltpu.VMEM((rows, slots), bf16),
            pltpu.VMEM((rows, width), f32),
            pltpu.VMEM(g_got.shape, bf16),
            pltpu.SemaphoreType.DMA((5,)),
        ],
        tokens, small, hot, g_got, *mixed_got, *wout_all,
        scalars=(), stay=(0, 2, 3), leave=(1, 2),
    )

    w_in, w_back = expert_in[0], expert_out[0]
    half = slots // 2
    g_parts = gather_w(g_mine)
    n_got = send_rows(n_rows, experts)
    n_far = [send_xor(n_got[a * half : (a + 1) * half], "wshard", 2) for a in range(2)]
    n_near = send_xor(n_got, "wshard", 1)
    n_rest = [send_xor(n, "wshard", 1) for n in n_far]
    n_all = [n_got, n_near, n_far[0], n_rest[0], n_far[1], n_rest[1]]
    plan = [
        [(0, 0, 0)], [(1, 1, 0)], [(2, 2, 0), (3, 3, 0)], [(4, 2, half), (5, 3, half)]
    ]
    runs, pairs, order = [], [], ()
    for pieces in plan:
        run = run_expert(
            [(n_all[n], g_parts[g], first) for n, g, first in pieces], e_arr, w_in, w_back, small, order
        )
        runs.append(run)
        order = run[:1]
        if len(pieces) == 2:
            pairs.append(add_pair(run[0], run[1]))
            order = pairs[-1:]
    hidden, g_pre, g_router = zip(*(run[-3:] for run in runs))
    across = [send_xor(pair, "wshard", 2) for pair in pairs]
    beside = send_xor(runs[1][0], "wshard", 1)
    parts = len(runs)
    result = on_chip(
        result_kernel, [shaped((slots, width))] * parts,
        [pltpu.VMEM((slots, width), bf16)] * parts + [pltpu.SemaphoreType.DMA((parts,))],
        *hidden, w_back, scalars=(), stay=range(parts),
    )
    g_total = on_chip(
        total_kernel, [shaped((slots, width))], [], runs[0][0], beside, *across,
        scalars=(), deps=(result[0],),
    )[0]
    g_back = send_rows(g_total, experts)

    result_total = on_chip(
        total_kernel, [shaped((slots, width))], [], *scatter_parts(result, deps=pairs[1:]),
        scalars=(), deps=(g_back,),
    )[0]
    g_in_w, g_out_w, token = on_chip(
        functools.partial(expert_grad_kernel, plan),
        [
            shaped((width, w_in.shape[1]), f32),
            shaped((w_in.shape[1], width), f32),
            shaped((8, 128), f32),
        ],
        [pltpu.VMEM((slots, w_in.shape[1]), bf16)] * (2 * parts)
        + [pltpu.SemaphoreType.DMA((2 * parts,))],
        *n_all, *g_parts, *g_pre, *hidden,
        scalars=(), stay=range(6 + nw, 6 + nw + 2 * parts), deps=(g_total,), limit=40,
        flops=4 * 4 * slots * width * width,
    )

    grad_low, grad_gain_b, grad_residual = on_chip(
        second_norm_kernel,
        [shaped((rows, width)), shaped((1, width), f32), shaped((rows, width), f32)],
        [
            pltpu.VMEM((rows, width), f32),
            pltpu.VMEM((few_rows, width), bf16),
            pltpu.VMEM((rows, slots), bf16),
            pltpu.VMEM((rows, width), bf16),
            pltpu.VMEM((rows, width), f32),
            pltpu.SemaphoreType.DMA((5,)),
        ],
        residual, small_far, hot, grad_out, g_back,
        scalars=(), stay=range(4), leave=(2,), deps=(token,),
    )
    grad_all = gather_w(grad_low)
    result_got = send_rows(result_total, experts)

    grads, scores = on_chip(
        attn_backward_kernel,
        [shaped((seq, 3 * shard)), shaped((heads, seq, seq), f32)],
        [
            pltpu.VMEM((shard, width), bf16),
            pltpu.VMEM((seq, 3 * shard), bf16),
            pltpu.VMEM((heads, seq, seq), f32),
            pltpu.VMEM((heads, seq, seq), f32),
            pltpu.VMEM((seq, shard), bf16),
            pltpu.VMEM((2, heads, seq, dim), f32),
            pltpu.SemaphoreType.DMA((2 + 2 * nw,)),
        ],
        w_arr, *grad_all, w_output, qkv, probs, stay=range(1 + nw, 4 + nw), leave=(1,),
    )
    block_out = on_chip(
        block_out_kernel, [shaped((rows, width))], [], residual, hot, result_got, scalars=()
    )[0]
    fast = ne <= 8 and shard % (8 * ne) == 0
    piece = shard // ne
    if fast:
        weight_outs = [shaped((ne, nw, piece, width))]
    else:
        weight_outs = [shaped((width, 3 * shard), f32), shaped((shard, width), f32)]
    chunks = on_chip(
        weight_grad_kernel,
        weight_outs,
        [pltpu.VMEM((rows, shard), bf16)] * nw
        + [pltpu.VMEM((seq, width), bf16), pltpu.SemaphoreType.DMA((1 + nw,))],
        ids, *grad_all, *mixed, normed_one, grads,
        stay=(1 + 2 * nw,), deps=(result_got,),
    )
    back = on_chip(
        input_grad_kernel,
        [shaped((rows + few_rows, width))] * nw,
        [
            pltpu.VMEM((nw, few_rows, shard), bf16),
            pltpu.VMEM((nw, shard, 3 * shard), bf16),
            pltpu.VMEM((nw, rows, width), bf16),
            pltpu.VMEM((parts, few_rows, width), f32),
            pltpu.SemaphoreType.DMA((2 + parts,)),
        ],
        w_arr, grads, weight, tok_all, grad_gain_b, *g_router,
        stay=(2, 3, *range(5, 5 + parts)), deps=chunks[:1],
    )
    bias = on_chip(
        bias_grad_kernel,
        [shaped((8, 128), f32)],
        [
            pltpu.VMEM((heads * bins, 128), f32),
            pltpu.VMEM((nw, rows, seq), bf16),
            pltpu.VMEM((heads, seq, seq), f32),
            pltpu.SemaphoreType.DMA((2,)),
        ],
        bucket_all, scores, scalars=(), stay=(0, 1), deps=chunks[:1],
    )[0]
    grad_tokens, few = on_chip(
        tokens_grad_kernel, [shaped((rows, width), f32), shaped((few_rows, shard), f32)], [],
        tokens, small, grad_residual, *scatter_parts(back), scalars=(),
    )
    if fast:
        got = lax.all_to_all(chunks[0], "expert", 0, 0, tiled=True)
        *sums, gout = on_chip(
            weight_sum_kernel,
            [shaped((piece, 3 * shard))] * nw + [shaped((nw, piece, shard))],
            [],
            got, scalars=(),
        )
        swapped = exchange(sums, "wshard")
        joined = on_chip(
            weight_pack_kernel, [shaped((nw * piece + few_rows, width))],
            [pltpu.VMEM((nw * piece + few_rows, width), f32)],
            *swapped, gout, few, bias, scalars=(),
        )[0]
        *weights, gain_a, gain_b, router, bias = on_chip(
            weight_join_kernel,
            [shaped((shard, width), f32)] * 4
            + [shaped(shape, f32) for shape in ((1, shard), (1, shard), (experts, shard), (heads, bins))],
            [pltpu.VMEM((nw, piece, width), f32)],
            ids, *spread(joined, "expert"),
        )
    else:
        gqkv, gout = chunks
        pieces_w = to_xor(to_xor(gqkv.reshape(nw, ne, piece, 3 * shard), "expert", 1), "wshard")
        pieces_w = pieces_w.astype(bf16)
        pieces_o = to_xor(gout.reshape(ne, piece, width), "expert").astype(bf16)
        add = lambda parts: functools.reduce(lambda a, b: a + b, [c.astype(f32) for c in parts])
        total = add(exchange([pieces_w[:, k] for k in range(ne)], "expert")).astype(bf16)
        total_out = add(exchange([pieces_o[k] for k in range(ne)], "expert")).astype(bf16)
        swapped = jnp.stack(exchange([total[k] for k in range(nw)], "wshard"))
        swapped = to_xor(swapped, "wshard").reshape(nw, piece, 3, shard).transpose(1, 2, 0, 3)
        joined = jnp.concatenate([swapped.reshape(piece, 3 * width), total_out], axis=1)
        whole = to_xor(jnp.stack(spread(joined, "expert")), "expert").reshape(shard, 4 * width)
        whole = whole.astype(f32)
        weights = [whole[:, i * width : (i + 1) * width] for i in range(4)]
        few, bias = lax.psum((few, bias), "expert")
        gain_a, gain_b, router = few[0], few[1], few[2 : 2 + experts]
        bias = bias[0, : heads * bins].reshape(heads, bins)
    return (
        block_out,
        grad_tokens,
        gain_a.reshape(shard),
        *weights,
        bias,
        gain_b.reshape(shard),
        router.T,
        g_in_w[None],
        g_out_w[None],
    )


def solution(mesh):
    placed = (
        P(("expert", "wshard"), None),
        P(("expert", "wshard"), None),
        P(("expert", "wshard"), None),
        P("wshard"),
        P("wshard", None),
        P("wshard", None),
        P("wshard", None),
        P("wshard", None),
        P("wshard", None),
        P("wshard"),
        P("wshard", None),
        P("expert", None, "wshard"),
        P("expert", "wshard", None),
        P(("expert", "wshard"), None),
    )
    return jax.shard_map(
        body,
        mesh=mesh,
        in_specs=placed,
        out_specs=(
            P(("expert", "wshard"), None),
            P(("expert", "wshard"), None),
            P("wshard"),
            P("wshard", None),
            P("wshard", None),
            P("wshard", None),
            P("wshard", None),
            P("wshard", None),
            P("wshard"),
            P("wshard", None),
            P("expert", None, "wshard"),
            P("expert", "wshard", None),
        ),
        check_vma=False,
    )
```

```python
import functools

import jax
import jax.numpy as jnp
from jax import lax
from jax.experimental import pallas as pl
from jax.experimental.pallas import tpu as pltpu
from jax.sharding import PartitionSpec as P

TOPK = 2
epsilon = 1e-06
bf16 = jnp.bfloat16
f32 = jnp.float32
NN = (((1,), (0,)), ((), ()))
NT = (((1,), (1,)), ((), ()))
TN = (((0,), (0,)), ((), ()))


def mm(left, right, dims=NN):
    return lax.dot_general(left, right, dims, preferred_element_type=f32)


def send_xor(value, axis, k):
    n = lax.axis_size(axis)
    return lax.ppermute(value, axis, [(i, i ^ k) for i in range(n)])


def to_xor(stacked, axis, dim=0):
    n = stacked.shape[dim]
    return jnp.take(stacked, jnp.arange(n) ^ lax.axis_index(axis), axis=dim)


def exchange(parts, axis):
    n = len(parts)
    if n <= 8:
        got = [send_xor(parts[k], axis, k) for k in range(n - 1, 0, -1)]
        return [parts[0]] + got[::-1]
    got = lax.all_to_all(to_xor(jnp.stack(parts), axis), axis, 0, 0, tiled=True)
    got = to_xor(got, axis)
    return [got[k] for k in range(n)]


def spread(value, axis):
    n = lax.axis_size(axis)
    if n <= 8:
        return exchange([value] * n, axis)
    got = to_xor(lax.all_gather(value, axis), axis)
    return [got[k] for k in range(n)]


def gather_w(value):
    across = send_xor(value, "wshard", 2)
    beside = send_xor(value, "wshard", 1)
    return [value, beside, across, send_xor(across, "wshard", 1)]


def send_rows(value, experts):
    blocks = value.reshape(experts, -1, value.shape[-1])
    return lax.all_to_all(blocks, "expert", 0, 0, tiled=True).reshape(value.shape)


def start_copies(pairs, sems, first=0):
    copies = [
        pltpu.make_async_copy(src, dst, sems.at[first + i]) for i, (src, dst) in enumerate(pairs)
    ]
    for copy in copies:
        copy.start()
    return copies


def wait_copies(copies):
    for copy in copies:
        copy.wait()


def norm_scale(x):
    return lax.rsqrt(jnp.mean(x * x, axis=-1, keepdims=True) + epsilon)


def pack_kernel(
    w_ref, one_ref, two_ref, router_ref, tok_ref, bucket_ref, wq_ref, wk_ref, wv_ref,
    far_ref, pack_ref, own_out, near_ref,
    tok, bucket, wq, wk, wv, one, two, router, own_ref, sems,
):
    w = w_ref[0]
    copies = start_copies(
        [
            (tok_ref, tok), (bucket_ref, bucket), (wq_ref, wq), (wk_ref, wk), (wv_ref, wv),
            (one_ref, one), (two_ref, two), (router_ref, router),
        ],
        sems,
    )
    wait_copies(copies)
    experts = router.shape[0]
    few_rows = pack_ref.shape[0] - tok.shape[0]
    small = jnp.concatenate(
        [
            one[...].astype(f32).reshape(1, -1),
            two[...].astype(f32).reshape(1, -1),
            router[...].astype(f32),
            jnp.zeros((few_rows - 2 - experts, router.shape[1]), f32),
        ],
        axis=0,
    ).astype(bf16)
    rows, width = tok.shape
    shard = wq.shape[0]
    blocks = width // shard
    half = shard // 2
    parts = [
        (j, slice(i * shard, (i + 1) * shard), ref[:, j * shard : (j + 1) * shard])
        for j in range(blocks)
        for i, ref in enumerate((wq, wk, wv))
    ]
    for j, at, block in parts:

        @pl.when(w == j)
        def _():
            own_ref[:, at] = block

    stores = start_copies([(own_ref, own_out)], sems, 8)
    pack_ref[:rows, :width] = tok[...]
    pack_ref[:rows, width:] = bucket[...].astype(f32).astype(bf16)
    pack_ref[rows:, :] = jnp.zeros((pack_ref.shape[0] - rows, pack_ref.shape[1]), bf16)
    pack_ref[rows:, :shard] = small
    middle = far_ref.shape[1] // 2
    far_ref[: 2 * half, :] = jnp.zeros((2 * half, far_ref.shape[1]), bf16)
    far_ref[2 * half :, :] = pack_ref[...]
    for j, at, block in parts:

        @pl.when(w ^ 1 == j)
        def _():
            near_ref[:, at] = block

        for k in (2, 3):

            @pl.when(w ^ k == j)
            def _():
                place = slice((k - 2) * half, (k - 1) * half)
                far_ref[place, at] = block[:half]
                far_ref[place, middle + at.start : middle + at.stop] = block[half:]

    wait_copies(stores)


def route_kernel(cap, routes_ref, grad_ref, hot_ref, g_ref):
    rows, width = grad_ref.shape
    slots = hot_ref.shape[1]
    first, second = routes_ref[:, 0:1], routes_ref[:, 1:2]
    lanes = lax.broadcasted_iota(jnp.int32, (rows, 128), 1)
    one, two = (lanes == first).astype(f32), (lanes == second).astype(f32)
    lower = lax.broadcasted_iota(jnp.int32, (rows, rows), 1) < lax.broadcasted_iota(
        jnp.int32, (rows, rows), 0
    )
    before = mm(lower.astype(f32).astype(bf16), (one + two).astype(bf16))
    places = lax.broadcasted_iota(jnp.int32, (rows, slots), 1)
    hots = []
    for route, named in ((first, one), (second, two)):
        slot = jnp.sum(before * named, axis=1, keepdims=True).astype(jnp.int32)
        hots.append((places == route * cap + slot).astype(f32))
    hot_ref[...] = (hots[0] + hots[1]).astype(bf16)
    g_ref[:, :width] = mm(hot_ref[...], grad_ref[...], TN).astype(bf16)
    wide = jnp.zeros((rows, 128), f32)
    other = mm(hots[0].astype(bf16), (second.astype(f32) + wide).astype(bf16), TN) + mm(
        hots[1].astype(bf16), (first.astype(f32) + wide).astype(bf16), TN
    )
    g_ref[:, width:] = other.astype(bf16)


def forward_kernel(far_ref, out_ref):
    out_ref[...] = far_ref[far_ref.shape[0] - out_ref.shape[0] :, :]


def attn_forward_kernel(
    w_ref, pack_a_in, pack_b_in, far_c, far_d, col_a_in, col_b_in, table_ref,
    mix_a, mix_b, mix_c, mix_d, small_ref, small_out, mixed_out, probs_out, qkv_out, normed_out, weight_out, token_out,
    ids_out,
    mixed_ref, probs_ref, qkv_ref, normed_ref, weight_ref, token_ref, ids_ref, shift_ref,
    pack_a, pack_b, col_a, col_b, sems, in_sems,
):
    w = w_ref[0]
    fetches = start_copies(
        [(pack_a_in, pack_a), (pack_b_in, pack_b), (col_a_in, col_a), (col_b_in, col_b)], in_sems
    )
    wait_copies(fetches)
    mixes = (mix_a, mix_b, mix_c, mix_d)
    blocks = len(mixes)
    heads, seq, _ = probs_ref.shape
    rows, width = seq // blocks, normed_ref.shape[1]
    shard = width // blocks
    dim = shard // heads
    half, middle = shard // 2, far_c.shape[1] // 2
    weight_ref[w] = col_a[...]
    weight_ref[1 ^ w] = col_b[...]
    weight_ref[2 ^ w, :half] = far_c[:half, : 3 * shard]
    weight_ref[2 ^ w, half:] = far_c[:half, middle : middle + 3 * shard]
    weight_ref[3 ^ w, :half] = far_d[:half, : 3 * shard]
    weight_ref[3 ^ w, half:] = far_d[:half, middle : middle + 3 * shard]
    packs = ((pack_a, 0), (pack_b, 0), (far_c, 2 * half), (far_d, half))
    for k, (ref, at) in enumerate(packs):
        shift_ref[k ^ w] = ref[at + rows :, :shard]
        ids_ref[k ^ w] = ref[at : at + rows, width:]
    for j in range(blocks):
        small_ref[:, j * shard : (j + 1) * shard] = shift_ref[j]
    gain = small_ref[0:1, :].astype(f32)
    weight = weight_ref[...].reshape(width, 3 * shard)
    for k, (ref, at) in enumerate(packs):
        token_ref[k ^ w] = ref[at : at + rows, :width]
        x = ref[at : at + rows, :width].astype(f32)
        normed = (x * norm_scale(x) * gain).astype(bf16)
        place = pl.ds(pl.multiple_of((k ^ w) * rows, rows), rows)
        normed_ref[place, :] = normed
        qkv_ref[place, :] = mm(normed, weight).astype(bf16)
    copies = start_copies(
        [
            (qkv_ref, qkv_out),
            (normed_ref, normed_out),
            (weight_ref, weight_out),
            (token_ref, token_out),
            (ids_ref, ids_out),
            (small_ref, small_out),
        ],
        sems,
    )
    below = lax.broadcasted_iota(jnp.int32, (rows, rows), 1) <= lax.broadcasted_iota(
        jnp.int32, (rows, rows), 0
    )
    for i in range(blocks):
        span = (i + 1) * rows
        ids = ids_ref[i].astype(f32).astype(jnp.int32)
        for h in range(heads):
            query = qkv_ref[i * rows : span, h * dim : (h + 1) * dim]
            keys = qkv_ref[:span, shard + h * dim : shard + (h + 1) * dim]
            values = qkv_ref[:span, 2 * shard + h * dim : 2 * shard + (h + 1) * dim]
            raw = mm(query, keys, NT) * 0.125
            table = jnp.broadcast_to(table_ref[h : h + 1, :], (rows, table_ref.shape[1]))
            bias = [
                jnp.take_along_axis(table, ids[:, j * rows : (j + 1) * rows], axis=1)
                for j in range(i + 1)
            ]
            scores = raw + jnp.concatenate(bias, axis=1) if i else raw + bias[0]
            last = jnp.where(below, scores[:, i * rows :], -1000000000.0)
            scores = jnp.concatenate([scores[:, : i * rows], last], axis=1) if i else last
            raised = jnp.exp(scores - jnp.max(scores, axis=-1, keepdims=True))
            probs = raised / jnp.sum(raised, axis=-1, keepdims=True)
            probs_ref[h, i * rows : span, :span] = probs
            mixed_ref[i, :, h * dim : (h + 1) * dim] = mm(probs.astype(bf16), values).astype(bf16)
        done = slice(i * rows, span)
        copies += start_copies(
            [(probs_ref.at[:, done, :span], probs_out.at[:, done, :span])], sems, 6 + i
        )
    copies += start_copies([(mixed_ref, mixed_out)], sems, 6 + blocks)
    for k in range(blocks):
        mixes[k][...] = mixed_ref[k ^ w]
    wait_copies(copies)


def project_kernel(
    tok_in, small_ref, hot_in, g_in, mix_a, mix_b, mix_c, mix_d, out_a, out_b, out_c, out_d,
    n_ref, residual_out, g_out, tok_ref, hot_ref, residual_ref, sems,
):
    copies = start_copies([(tok_in, tok_ref), (hot_in, hot_ref)], sems)
    g_out[...] = g_in[...]
    residual = 0.0
    for mix, out in ((mix_a, out_a), (mix_b, out_b), (mix_c, out_c), (mix_d, out_d)):
        residual = residual + mm(mix[...], out[...])
    copies[0].wait()
    residual = residual + tok_ref[...].astype(f32)
    residual_ref[...] = residual
    copies += start_copies([(residual_ref, residual_out)], sems, 2)
    normed = (residual * norm_scale(residual) * small_ref[1:2, :].astype(f32)).astype(bf16)
    copies[1].wait()
    n_ref[...] = mm(hot_ref[...], normed, TN).astype(bf16)
    wait_copies(copies[2:])


def expert_kernel(firsts, e_ref, *refs):
    e = e_ref[0]
    count = len(firsts)
    n_refs, g_refs, refs = refs[:count], refs[count : 2 * count], refs[2 * count :]
    (in_ref, out_ref, small_ref), slot_refs, refs = refs[:3], refs[3 : 3 + count], refs[3 + count :]
    hidden_out, pre_out, router_out, hidden_ref, pre_ref, router_ref, sems = refs
    rows, width = n_refs[0].shape
    n = jnp.concatenate([ref[...] for ref in n_refs], axis=0)
    g_all = jnp.concatenate(
        [ref[first : first + rows, :] for first, ref in zip(firsts, g_refs)], axis=0
    )
    g = g_all[:, :width]
    logits = mm(n, small_ref[...], NT)
    lanes = lax.broadcasted_iota(jnp.int32, logits.shape, 1)
    other = g_all[:, width : width + 1].astype(f32).astype(jnp.int32)
    differ = (lanes == 2 + e).astype(f32) - (lanes == 2 + other).astype(f32)
    gate = 1.0 / (1.0 + jnp.exp(-jnp.sum(logits * differ, axis=-1, keepdims=True)))
    pre = mm(n, in_ref[...])
    back = mm(g, out_ref[...], NT)
    square = pre * pre
    bent = jnp.tanh(0.7978845608028654 * pre * (1.0 + 0.044715 * square))
    hidden = 0.5 * pre * (1.0 + bent)
    hidden_ref[...] = (gate * hidden).astype(bf16)
    slope = 0.5 * (1.0 + bent) + 0.5 * pre * (1.0 - bent * bent) * (
        0.7978845608028654 * (1.0 + 3.0 * 0.044715 * square)
    )
    g_gate = jnp.sum(hidden * back, axis=-1, keepdims=True)
    g_logit = (gate * (1.0 - gate) * g_gate * differ).astype(bf16)
    router_ref[...] = mm(g_logit, n, TN)
    g_pre = (gate * back * slope).astype(bf16)
    pre_ref[...] = g_pre
    copies = start_copies(
        [(hidden_ref, hidden_out), (pre_ref, pre_out), (router_ref, router_out)], sems
    )
    slot = mm(g_pre, in_ref[...], NT) + mm(g_logit, small_ref[...])
    for i, ref in enumerate(slot_refs):
        ref[...] = slot[i * rows : (i + 1) * rows].astype(bf16)
    wait_copies(copies)


def result_kernel(in_a, in_b, in_c, in_d, w_ref, *refs):
    outs, held, sems = refs[:4], refs[4:8], refs[8]
    copies = start_copies(list(zip((in_a, in_b, in_c, in_d), held)), sems)
    half = outs[0].shape[0] // 2
    for i in range(4):
        copies[i].wait()
        value = mm(held[i][...], w_ref[...]).astype(bf16)
        if i < 2:
            outs[i][...] = value
        else:
            at = slice((i - 2) * half, (i - 1) * half)
            outs[2][at, :] = value[:half]
            outs[3][at, :] = value[half:]


def expert_grad_kernel(plan, *refs):
    n_count = 1 + max(n for pieces in plan for n, _, _ in pieces)
    g_count = 1 + max(g for pieces in plan for _, g, _ in pieces)
    runs = len(plan)
    n_refs, g_refs, refs = refs[:n_count], refs[n_count : n_count + g_count], refs[n_count + g_count :]
    ins, (g_in, g_out, token_ref), refs = refs[: 2 * runs], refs[2 * runs : 2 * runs + 3], refs[2 * runs + 3 :]
    held, sems = refs[: 2 * runs], refs[-1]
    token_ref[...] = jnp.zeros_like(token_ref)
    copies = start_copies(list(zip(ins, held)), sems)
    width = n_refs[0].shape[1]
    first_term = True
    for i, pieces in enumerate(plan):
        copies[i].wait()
        copies[runs + i].wait()
        at = 0
        for n_at, g_at, first in pieces:
            n = n_refs[n_at][...]
            rows = n.shape[0]
            pre, hidden = held[i][at : at + rows, :], held[runs + i][at : at + rows, :]
            g = g_refs[g_at][first : first + rows, :width]
            at += rows
            for ref, term in ((g_in, mm(n, pre, TN)), (g_out, mm(hidden, g, TN))):
                if first_term:
                    ref[...] = term
                else:
                    ref[...] += term
            first_term = False


def pair_kernel(*refs):
    count = (len(refs) - 1) // 2
    step = refs[0].shape[0]
    for i in range(count):
        total = refs[i][...].astype(f32) + refs[count + i][...].astype(f32)
        refs[-1][i * step : (i + 1) * step, :] = total.astype(bf16)


def total_kernel(own_ref, beside_ref, *refs):
    across, out_ref = refs[:-1], refs[-1]
    step = out_ref.shape[0] // len(across)
    for a, ref in enumerate(across):
        at = slice(a * step, (a + 1) * step)
        total = own_ref[at, :].astype(f32) + beside_ref[at, :].astype(f32) + ref[...].astype(f32)
        out_ref[at, :] = total.astype(bf16)


def second_norm_kernel(
    residual_in, small_in, hot_in, grad_in, got_ref, low_ref, gain_ref, grad_residual_out,
    residual_ref, small_ref, hot_ref, grad_ref, grad_residual_ref, sems,
):
    copies = start_copies(
        [(hot_in, hot_ref), (residual_in, residual_ref), (small_in, small_ref), (grad_in, grad_ref)],
        sems,
    )
    wait_copies(copies)
    g_normed = mm(hot_ref[...], got_ref[...])
    residual = residual_ref[...]
    scale = norm_scale(residual)
    scaled = g_normed * small_ref[1:2, :].astype(f32)
    grad = (
        grad_ref[...].astype(f32)
        + scale * scaled
        - residual * scale * scale * scale * jnp.mean(scaled * residual, axis=-1, keepdims=True)
    )
    grad_residual_ref[...] = grad
    stores = start_copies([(grad_residual_ref, grad_residual_out)], sems, 4)
    low_ref[...] = grad.astype(bf16)
    gain_ref[...] = jnp.sum(g_normed * residual * scale, axis=0, keepdims=True)
    wait_copies(stores)


def block_out_kernel(residual_ref, hot_ref, got_ref, out_ref):
    out_ref[...] = (residual_ref[...] + mm(hot_ref[...], got_ref[...])).astype(bf16)


def attn_backward_kernel(
    ids_ref, grad_a, grad_b, grad_c, grad_d, wout_in, qkv_in, probs_in,
    grads_ref, scores_out, wout_ref, qkv_ref, probs_ref, scores_ref, gmix_ref, part_ref, sems,
):
    w = ids_ref[0]
    packs = (grad_a, grad_b, grad_c, grad_d)
    blocks = len(packs)
    rows = grad_a.shape[0]
    spans = [(slice(i * rows, (i + 1) * rows), (i + 1) * rows) for i in range(blocks)]
    copies = start_copies(
        [(wout_in, wout_ref), (qkv_in, qkv_ref)]
        + [(probs_in.at[:, at, :span], probs_ref.at[:, at, :span]) for at, span in spans],
        sems,
    )
    copies[0].wait()
    rows, width = grad_a.shape
    shard = width // blocks
    heads = probs_ref.shape[0]
    dim = shard // heads
    for k in range(blocks):
        place = pl.ds(pl.multiple_of((k ^ w) * rows, rows), rows)
        gmix_ref[place, :] = mm(packs[k][...], wout_ref[...], NT).astype(bf16)
    part_ref[...] = jnp.zeros_like(part_ref)
    copies[1].wait()
    stores = []
    for i in range(blocks):
        span = (i + 1) * rows
        copies[2 + i].wait()
        for h in range(heads):
            query = qkv_ref[i * rows : span, h * dim : (h + 1) * dim]
            keys = qkv_ref[:span, shard + h * dim : shard + (h + 1) * dim]
            values = qkv_ref[:span, 2 * shard + h * dim : 2 * shard + (h + 1) * dim]
            gmix = gmix_ref[i * rows : span, h * dim : (h + 1) * dim]
            probs = probs_ref[h, i * rows : span, :span]
            gprobs = mm(gmix, values, NT)
            inner = jnp.sum(probs * gprobs, axis=-1, keepdims=True)
            gscores = probs * (gprobs - inner)
            scores_ref[h, i * rows : span, :span] = gscores
            low = gscores.astype(bf16)
            grads_ref[i * rows : span, h * dim : (h + 1) * dim] = (mm(low, keys) * 0.125).astype(
                bf16
            )
            part_ref[0, h, :span, :] += mm(low, query, TN)
            part_ref[1, h, :span, :] += mm(probs.astype(bf16), gmix, TN)
        at = slice(i * rows, span)
        stores += start_copies(
            [(scores_ref.at[:, at, :span], scores_out.at[:, at, :span])], sems, 2 + blocks + i
        )
    for h in range(heads):
        grads_ref[:, shard + h * dim : shard + (h + 1) * dim] = (part_ref[0, h] * 0.125).astype(
            bf16
        )
        grads_ref[:, 2 * shard + h * dim : 2 * shard + (h + 1) * dim] = part_ref[1, h].astype(bf16)
    wait_copies(stores)


def weight_grad_kernel(
    ids_ref, grad_a, grad_b, grad_c, grad_d, normed_in, mixed_in, grads_ref, *refs
):
    *outs, normed_ref, mixed_ref, sems = refs
    w = ids_ref[0]
    copies = start_copies([(mixed_in, mixed_ref), (normed_in, normed_ref)], sems)
    copies[0].wait()
    gout = functools.reduce(
        lambda p, q: p + q,
        [
            mm(mixed_ref[k ^ w], ref[...], TN)
            for k, ref in enumerate((grad_a, grad_b, grad_c, grad_d))
        ],
    )
    copies[1].wait()
    gqkv = mm(normed_ref[...], grads_ref[...], TN)
    if len(outs) == 2:
        outs[0][...] = gqkv
        outs[1][...] = gout
        return
    stage_ref = outs[0]
    ne = stage_ref.shape[0]
    shard, width = gout.shape
    nw = width // shard
    piece = shard // ne
    for j in range(nw):
        for s in range(ne):
            row = j * shard + s * piece
            stage_ref[s, j ^ w, :, : 3 * shard] = gqkv[row : row + piece].astype(bf16)
            stage_ref[s, j, :, 3 * shard :] = gout[
                s * piece : (s + 1) * piece, j * shard : (j + 1) * shard
            ].astype(bf16)


def weight_sum_kernel(in_ref, *refs):
    outs, gout_ref = refs[:-1], refs[-1]
    for k, out in enumerate(outs):
        total = functools.reduce(
            lambda p, q: p + q, [in_ref[i, k].astype(f32) for i in range(in_ref.shape[0])]
        )
        cut = out.shape[1]
        out[...] = total[:, :cut].astype(bf16)
        gout_ref[k] = total[:, cut:].astype(bf16)


def weight_pack_kernel(a_ref, b_ref, c_ref, d_ref, gout_ref, few_ref, bias_ref, out_ref, stage):
    piece, cut = a_ref.shape
    width = stage.shape[1]
    shard = width - cut
    stage[...] = jnp.zeros_like(stage)
    for k, ref in enumerate((a_ref, b_ref, c_ref, d_ref)):
        stage[k * piece : (k + 1) * piece, :cut] = ref[...].astype(f32)
        stage[k * piece : (k + 1) * piece, cut:] = gout_ref[k].astype(f32)
    at = 4 * piece
    few = few_ref[...]
    high = few.astype(bf16).astype(f32)
    for i, part in enumerate((high[:8], high[8:], (few - high)[:8], (few - high)[8:])):
        if i % 2 == 0:
            stage[at : at + 8, i * shard : (i + 1) * shard] = part
        else:
            stage[at : at + 4, i * shard : (i + 1) * shard] = part[:4]
    bias = bias_ref[...]
    high = bias.astype(bf16).astype(f32)
    stage[at + 4 : at + 8, shard : shard + 128] = high[:4]
    stage[at + 4 : at + 8, 3 * shard : 3 * shard + 128] = (bias - high)[:4]
    out_ref[...] = stage[...].astype(bf16)


def weight_join_kernel(ids_ref, *refs):
    w, e = ids_ref[0], ids_ref[1]
    ins, outs, one_ref, two_ref, router_ref, bias_ref, stage = (
        refs[:-9], refs[-9:-5], refs[-5], refs[-4], refs[-3], refs[-2], refs[-1]
    )
    shard, width = outs[0].shape
    nw, piece = width // shard, stage.shape[1]
    at = nw * piece
    few = 0.0
    for k, ref in enumerate(ins):
        place = pl.ds(pl.multiple_of((k ^ e) * piece, piece), piece)
        value = ref[...].astype(f32)
        for j in range(nw):
            mine = value[j * piece : (j + 1) * piece]
            stage[j ^ w] = mine
            outs[3][place, j * shard : (j + 1) * shard] = mine[:, 3 * shard :]
        for j in range(nw):
            mine = stage[j]
            for i in range(3):
                outs[i][place, j * shard : (j + 1) * shard] = mine[:, i * shard : (i + 1) * shard]
        few += value[at:, : 2 * shard] + value[at:, 2 * shard :]
    one_ref[...] = few[0:1, :shard]
    two_ref[...] = few[1:2, :shard]
    bias = few[4:5, shard:]
    experts = router_ref.shape[0]
    router_ref[:6, :] = few[2:8, :shard]
    router_ref[6:, :] = few[: experts - 6, shard:]
    heads, bins = bias_ref.shape
    for h in range(heads):
        bias_ref[h : h + 1, :] = bias[:, h * bins : (h + 1) * bins]


def input_grad_kernel(
    w_ref, grads_ref, weight_in, token_in, gain_ref, *refs,
):
    *router_in, back_a, back_b, back_c, back_d, few_ref, weight_ref, token_ref, router_ref, sems = (
        refs
    )
    w = w_ref[0]
    wait_copies(
        start_copies(
            [(weight_in, weight_ref), (token_in, token_ref)]
            + [(ref, router_ref.at[i]) for i, ref in enumerate(router_in)],
            sems,
        )
    )
    backs = (back_a, back_b, back_c, back_d)
    blocks, rows, width = token_ref.shape
    shard = width // blocks
    weight = weight_ref[...].reshape(width, 3 * shard)
    total = jnp.zeros((1, width), f32)
    for k in range(blocks):
        place = pl.ds(pl.multiple_of((k ^ w) * rows, rows), rows)
        back = mm(grads_ref[place, :], weight, NT)
        backs[k][:rows, :] = back.astype(bf16)
        x = token_ref[k ^ w].astype(f32)
        total += jnp.sum(back * x * norm_scale(x), axis=0, keepdims=True)
    few = jnp.sum(router_ref[...], axis=0)
    line = lax.broadcasted_iota(jnp.int32, few.shape, 0)
    few = jnp.where(line == 0, total, jnp.where(line == 1, gain_ref[...], few))
    for j in range(blocks):
        few_ref[j] = few[:, j * shard : (j + 1) * shard].astype(bf16)
    for k in range(blocks):
        backs[k][rows:, :] = jnp.zeros((few.shape[0], width), bf16)
        backs[k][rows:, :shard] = few_ref[k ^ w]


def bias_grad_kernel(ids_in, scores_in, out_ref, part_ref, ids_ref, scores_ref, sems):
    wait_copies(start_copies([(ids_in, ids_ref), (scores_in, scores_ref)], sems))
    heads, seq, _ = scores_ref.shape
    blocks, rows, _ = ids_ref.shape
    bins = part_ref.shape[0] // heads
    part_ref[...] = jnp.zeros_like(part_ref)
    for i in range(blocks):
        span = (i + 1) * rows
        ids = ids_ref[i, :, :span].astype(f32).astype(jnp.int32)
        for b in range(bins):
            hit = ids == b
            for h in range(heads):
                picked = jnp.where(hit, scores_ref[h, i * rows : span, :span], 0.0)
                part_ref[h * bins + b : h * bins + b + 1, :] += functools.reduce(
                    lambda p, q: p + q,
                    [
                        jnp.sum(picked[:, j * rows : (j + 1) * rows], axis=0, keepdims=True)
                        for j in range(i + 1)
                    ],
                )
    spread_out = jnp.concatenate(
        [part_ref[...], jnp.zeros((128 - part_ref.shape[0], 128), f32)], axis=0
    )
    out_ref[...] = lax.dot_general(
        jnp.ones((8, 128), f32), spread_out, NT, precision=lax.Precision.HIGHEST,
        preferred_element_type=f32,
    )


def tokens_grad_kernel(
    tok_ref, small_ref, residual_ref, a_ref, b_ref, c_ref, out_ref, few_ref
):
    rows = tok_ref.shape[0]
    shard = few_ref.shape[1]
    total = a_ref[...].astype(f32) + b_ref[...].astype(f32) + c_ref[...].astype(f32)
    grad = total[:rows]
    few_ref[...] = total[rows:, :shard]
    x = tok_ref[...].astype(f32)
    scale = norm_scale(x)
    scaled = grad * small_ref[0:1, :].astype(f32)
    out_ref[...] = (
        residual_ref[...]
        + scale * scaled
        - x * scale * scale * scale * jnp.mean(scaled * x, axis=-1, keepdims=True)
    )


def shaped(shape, dtype=bf16):
    return jax.ShapeDtypeStruct(shape, dtype)


def on_chip(
    kernel, outs, scratch, *args, scalars=(0,), flops=0, stay=(), leave=(), deps=(), limit=32,
    weight=1000,
):
    count = len(args)
    args = [
        pltpu.with_memory_space_constraint(a, pltpu.HBM) if i in stay else a
        for i, a in enumerate(args)
    ]
    places = [
        pltpu.SMEM if i in scalars else pltpu.HBM if i in stay else pltpu.VMEM
        for i in range(count)
    ] + [pl.ANY] * len(deps)

    def run(*refs):
        kernel(*refs[:count], *refs[count + len(deps) :])

    size = sum(a.size * a.dtype.itemsize for a in (*args, *outs))
    return pl.pallas_call(
        run,
        out_shape=[
            pltpu.HBM(a.shape, a.dtype) if i in leave else a for i, a in enumerate(outs)
        ],
        in_specs=[pl.BlockSpec(memory_space=place) for place in places],
        out_specs=[
            pl.BlockSpec(memory_space=pltpu.HBM if i in leave else pltpu.VMEM)
            for i in range(len(outs))
        ],
        scratch_shapes=scratch,
        compiler_params=pltpu.CompilerParams(vmem_limit_bytes=limit * 1024 * 1024),
        cost_estimate=pl.CostEstimate(
            flops=flops + weight * size, bytes_accessed=size * weight // 1000, transcendentals=0
        ),
    )(*args, *deps)


def run_expert(pieces, e_arr, w_in, w_out, small, deps=()):
    rows, width = pieces[0][0].shape
    hidden = w_in.shape[1]
    count = len(pieces)
    kept = [
        shaped((rows * count, hidden)), shaped((rows * count, hidden)),
        shaped((small.shape[0], width), f32),
    ]
    return on_chip(
        functools.partial(expert_kernel, [first for _, _, first in pieces]),
        [shaped((rows, width))] * count + kept,
        [pltpu.VMEM(a.shape, a.dtype) for a in kept] + [pltpu.SemaphoreType.DMA((3,))],
        e_arr, *[n for n, _, _ in pieces], *[g for _, g, _ in pieces], w_in, w_out, small,
        leave=range(count, count + 3), deps=deps,
    )


def add_pair(mine, other, deps=()):
    other = send_xor(other, "wshard", 1)
    return on_chip(
        pair_kernel, [shaped(other.shape)], [], mine, other, scalars=(), deps=deps
    )[0]


def scatter_parts(parts, deps=()):
    across = send_xor(add_pair(parts[2], parts[3], deps), "wshard", 2)
    beside = send_xor(parts[1], "wshard", 1)
    return parts[0], beside, across


def body(
    tokens, routes, buckets, gain_one, w_query, w_key, w_value, w_output, pos_bias, gain_two,
    w_router, expert_in, expert_out, grad_out,
):
    rows, width = tokens.shape
    nw, ne = lax.axis_size("wshard"), lax.axis_size("expert")
    w, e = lax.axis_index("wshard"), lax.axis_index("expert")
    w_arr, e_arr = w.astype(jnp.int32).reshape(1), e.astype(jnp.int32).reshape(1)
    ids = jnp.concatenate([w_arr, e_arr])
    shard = width // nw
    heads, bins = pos_bias.shape
    dim = shard // heads
    seq = rows * nw
    experts = w_router.shape[1]
    cap = 3 * rows * TOPK // (2 * experts)
    slots = experts * cap
    few_rows = -(-(2 + experts) // 16) * 16

    far, pack, col_own, col_near = on_chip(
        pack_kernel,
        [
            shaped((shard + rows + few_rows, width + seq)),
            shaped((rows + few_rows, width + seq)),
            shaped((shard, 3 * shard)),
            shaped((shard, 3 * shard)),
        ],
        [
            pltpu.VMEM((rows, width), bf16),
            pltpu.VMEM((rows, seq), jnp.int32),
            pltpu.VMEM((shard, width), bf16),
            pltpu.VMEM((shard, width), bf16),
            pltpu.VMEM((shard, width), bf16),
            pltpu.VMEM((shard,), bf16),
            pltpu.VMEM((shard,), bf16),
            pltpu.VMEM((experts, shard), bf16),
            pltpu.VMEM((shard, 3 * shard), bf16),
            pltpu.SemaphoreType.DMA((9,)),
        ],
        w_arr, gain_one, gain_two, w_router.T, tokens, buckets, w_query, w_key, w_value,
        stay=range(1, 9), leave=(2,),
    )
    far_c = send_xor(far, "wshard", 2)
    pack_b, col_b = send_xor(pack, "wshard", 1), send_xor(col_near, "wshard", 1)
    hot, g_rows = on_chip(
        functools.partial(route_kernel, cap),
        [shaped((rows, slots)), shaped((slots, width + 128))],
        [],
        routes, grad_out, scalars=(), deps=(pack_b, col_b),
    )
    g_got = send_rows(g_rows, experts)
    far_rest = on_chip(
        forward_kernel, [shaped((far.shape[0] - shard // 2, far.shape[1]))], [], far_c,
        scalars=(),
    )[0]
    far_d = send_xor(far_rest, "wshard", 1)
    wout_far, wout_near = send_xor(w_output, "wshard", 2), send_xor(w_output, "wshard", 1)

    table = jnp.zeros((8, 128), f32).at[:heads, :bins].set(pos_bias.astype(f32))
    kept = [
        shaped((few_rows, width)),
        shaped((nw, rows, shard)),
        shaped((heads, seq, seq), f32),
        shaped((seq, 3 * shard)),
        shaped((seq, width)),
        shaped((nw, shard, 3 * shard)),
        shaped((nw, rows, width)),
        shaped((nw, rows, seq)),
    ]
    *mixed, small, small_far, mixed_far, probs, qkv, normed_one, weight, tok_all, bucket_all = on_chip(
        attn_forward_kernel,
        [shaped((rows, shard))] * nw + [shaped((few_rows, width))] + kept,
        [pltpu.VMEM(a.shape, a.dtype) for a in kept[1:]]
        + [
            pltpu.VMEM((nw, few_rows, shard), bf16),
            pltpu.VMEM(pack.shape, bf16),
            pltpu.VMEM(pack.shape, bf16),
            pltpu.VMEM(col_own.shape, bf16),
            pltpu.VMEM(col_own.shape, bf16),
            pltpu.SemaphoreType.DMA((7 + nw,)),
            pltpu.SemaphoreType.DMA((4,)),
        ],
        w_arr, pack, pack_b, far_c, far_d, col_own, col_b, table,
        stay=(1, 2, 5, 6), leave=range(nw + 1, nw + 9), deps=(g_got,),
    )
    mixed_got = exchange(mixed, "wshard")
    wout_rest = on_chip(
        forward_kernel, [shaped(w_output.shape)], [], wout_far, scalars=(), deps=(mixed[0],)
    )[0]
    wout_all = [w_output, wout_near, wout_far, send_xor(wout_rest, "wshard", 1)]
    n_rows, residual, g_mine = on_chip(
        project_kernel,
        [shaped((slots, width)), shaped((rows, width), f32), shaped(g_got.shape)],
        [
            pltpu.VMEM((rows, width), bf16),
            pltpu.VMEM((rows, slots), bf16),
            pltpu.VMEM((rows, width), f32),
            pltpu.SemaphoreType.DMA((3,)),
        ],
        tokens, small, hot, g_got, *mixed_got, *wout_all,
        scalars=(), stay=(0, 2), leave=(1,),
    )

    w_in, w_back = expert_in[0], expert_out[0]
    half = slots // 2
    g_parts = gather_w(g_mine)
    n_got = send_rows(n_rows, experts)
    n_far = [send_xor(n_got[a * half : (a + 1) * half], "wshard", 2) for a in range(2)]
    n_near = send_xor(n_got, "wshard", 1)
    plan = [
        [(0, 0, 0)], [(1, 1, 0)], [(2, 2, 0), (3, 3, 0)], [(4, 2, half), (5, 3, half)]
    ]
    n_all = [n_got, n_near]
    runs, order = [], ()
    for step, pieces in enumerate(plan):
        if step >= 2:
            n = n_far[step - 2]
            if step == 2:
                rest = on_chip(forward_kernel, [shaped(n.shape)], [], n, scalars=(), deps=order)[0]
            else:
                rest = n
            n_all += [n, send_xor(rest, "wshard", 1)]
        run = run_expert(
            [(n_all[n], g_parts[g], first) for n, g, first in pieces], e_arr, w_in, w_back, small, order
        )
        runs.append(run)
        order = run[:1]
    hidden, g_pre, g_router = zip(*(run[-3:] for run in runs))
    other = [send_xor(run[1], "wshard", 1) for run in runs[2:]]
    pair = on_chip(
        pair_kernel, [shaped((slots, width))], [], runs[2][0], runs[3][0], *other, scalars=()
    )[0]
    across = send_xor(pair, "wshard", 2)
    beside = send_xor(runs[1][0], "wshard", 1)
    parts = len(runs)
    result = on_chip(
        result_kernel, [shaped((slots, width))] * parts,
        [pltpu.VMEM((slots, width), bf16)] * parts + [pltpu.SemaphoreType.DMA((parts,))],
        *hidden, w_back, scalars=(), stay=range(parts),
    )
    g_total = on_chip(
        total_kernel, [shaped((slots, width))], [], runs[0][0], beside, across,
        scalars=(),
    )[0]
    g_back = send_rows(g_total, experts)

    result_total = on_chip(
        total_kernel, [shaped((slots, width))], [], *scatter_parts(result, deps=(g_total,)),
        scalars=(), deps=(g_back,),
    )[0]
    g_in_w, g_out_w, token = on_chip(
        functools.partial(expert_grad_kernel, plan),
        [
            shaped((width, w_in.shape[1]), f32),
            shaped((w_in.shape[1], width), f32),
            shaped((8, 128), f32),
        ],
        [pltpu.VMEM((slots, w_in.shape[1]), bf16)] * (2 * parts)
        + [pltpu.SemaphoreType.DMA((2 * parts,))],
        *n_all, *g_parts, *g_pre, *hidden,
        scalars=(), stay=range(6 + nw, 6 + nw + 2 * parts), deps=(g_total,), limit=40,
        flops=4 * 4 * slots * width * width,
    )

    grad_low, grad_gain_b, grad_residual = on_chip(
        second_norm_kernel,
        [shaped((rows, width)), shaped((1, width), f32), shaped((rows, width), f32)],
        [
            pltpu.VMEM((rows, width), f32),
            pltpu.VMEM((few_rows, width), bf16),
            pltpu.VMEM((rows, slots), bf16),
            pltpu.VMEM((rows, width), bf16),
            pltpu.VMEM((rows, width), f32),
            pltpu.SemaphoreType.DMA((5,)),
        ],
        residual, small_far, hot, grad_out, g_back,
        scalars=(), stay=range(4), leave=(2,), deps=(token,),
    )
    grad_all = gather_w(grad_low)
    result_got = send_rows(result_total, experts)

    block_out = on_chip(
        block_out_kernel, [shaped((rows, width))], [], residual, hot, result_got, scalars=()
    )[0]
    fast = ne <= 8 and shard % (8 * ne) == 0 and few_rows == 16 and 6 < experts <= 10
    piece = shard // ne
    if fast:
        weight_outs = [shaped((ne, nw, piece, width))]
    else:
        weight_outs = [shaped((width, 3 * shard), f32), shaped((shard, width), f32)]
    grads, scores = on_chip(
        attn_backward_kernel,
        [shaped((seq, 3 * shard)), shaped((heads, seq, seq), f32)],
        [
            pltpu.VMEM((shard, width), bf16),
            pltpu.VMEM((seq, 3 * shard), bf16),
            pltpu.VMEM((heads, seq, seq), f32),
            pltpu.VMEM((heads, seq, seq), f32),
            pltpu.VMEM((seq, shard), bf16),
            pltpu.VMEM((2, heads, seq, dim), f32),
            pltpu.SemaphoreType.DMA((2 + 2 * nw,)),
        ],
        ids, *grad_all, w_output, qkv, probs, stay=range(1 + nw, 4 + nw), leave=(1,),
    )
    chunks = on_chip(
        weight_grad_kernel,
        weight_outs,
        [
            pltpu.VMEM((seq, width), bf16),
            pltpu.VMEM((nw, rows, shard), bf16),
            pltpu.SemaphoreType.DMA((2,)),
        ],
        ids, *grad_all, normed_one, mixed_far, grads, stay=(1 + nw, 2 + nw), deps=(result_got,),
    )
    back = on_chip(
        input_grad_kernel,
        [shaped((rows + few_rows, width))] * nw,
        [
            pltpu.VMEM((nw, few_rows, shard), bf16),
            pltpu.VMEM((nw, shard, 3 * shard), bf16),
            pltpu.VMEM((nw, rows, width), bf16),
            pltpu.VMEM((parts, few_rows, width), f32),
            pltpu.SemaphoreType.DMA((2 + parts,)),
        ],
        w_arr, grads, weight, tok_all, grad_gain_b, *g_router,
        stay=(2, 3, *range(5, 5 + parts)), deps=chunks[:1],
    )
    bias = on_chip(
        bias_grad_kernel,
        [shaped((8, 128), f32)],
        [
            pltpu.VMEM((heads * bins, 128), f32),
            pltpu.VMEM((nw, rows, seq), bf16),
            pltpu.VMEM((heads, seq, seq), f32),
            pltpu.SemaphoreType.DMA((2,)),
        ],
        bucket_all, scores, scalars=(), stay=(0, 1), deps=chunks[:1],
    )[0]
    grad_tokens, few = on_chip(
        tokens_grad_kernel, [shaped((rows, width), f32), shaped((few_rows, shard), f32)], [],
        tokens, small, grad_residual, *scatter_parts(back), scalars=(),
    )
    if fast:
        got = lax.all_to_all(chunks[0], "expert", 0, 0, tiled=True)
        *sums, gout = on_chip(
            weight_sum_kernel,
            [shaped((piece, 3 * shard))] * nw + [shaped((nw, piece, shard))],
            [],
            got, scalars=(),
        )
        swapped = exchange(sums, "wshard")
        joined = on_chip(
            weight_pack_kernel, [shaped((nw * piece + 8, width))],
            [pltpu.VMEM((nw * piece + 8, width), f32)],
            *swapped, gout, few, bias, scalars=(),
        )[0]
        *weights, gain_a, gain_b, router, bias = on_chip(
            weight_join_kernel,
            [shaped((shard, width), f32)] * 4
            + [shaped(shape, f32) for shape in ((1, shard), (1, shard), (experts, shard), (heads, bins))],
            [pltpu.VMEM((nw, piece, width), f32)],
            ids, *spread(joined, "expert"),
        )
    else:
        gqkv, gout = chunks
        pieces_w = to_xor(to_xor(gqkv.reshape(nw, ne, piece, 3 * shard), "expert", 1), "wshard")
        pieces_w = pieces_w.astype(bf16)
        pieces_o = to_xor(gout.reshape(ne, piece, width), "expert").astype(bf16)
        add = lambda parts: functools.reduce(lambda a, b: a + b, [c.astype(f32) for c in parts])
        total = add(exchange([pieces_w[:, k] for k in range(ne)], "expert")).astype(bf16)
        total_out = add(exchange([pieces_o[k] for k in range(ne)], "expert")).astype(bf16)
        swapped = jnp.stack(exchange([total[k] for k in range(nw)], "wshard"))
        swapped = to_xor(swapped, "wshard").reshape(nw, piece, 3, shard).transpose(1, 2, 0, 3)
        joined = jnp.concatenate([swapped.reshape(piece, 3 * width), total_out], axis=1)
        whole = to_xor(jnp.stack(spread(joined, "expert")), "expert").reshape(shard, 4 * width)
        whole = whole.astype(f32)
        weights = [whole[:, i * width : (i + 1) * width] for i in range(4)]
        few, bias = lax.psum((few, bias), "expert")
        gain_a, gain_b, router = few[0], few[1], few[2 : 2 + experts]
        bias = bias[0, : heads * bins].reshape(heads, bins)
    return (
        block_out,
        grad_tokens,
        gain_a.reshape(shard),
        *weights,
        bias,
        gain_b.reshape(shard),
        router.T,
        g_in_w[None],
        g_out_w[None],
    )


def solution(mesh):
    placed = (
        P(("expert", "wshard"), None),
        P(("expert", "wshard"), None),
        P(("expert", "wshard"), None),
        P("wshard"),
        P("wshard", None),
        P("wshard", None),
        P("wshard", None),
        P("wshard", None),
        P("wshard", None),
        P("wshard"),
        P("wshard", None),
        P("expert", None, "wshard"),
        P("expert", "wshard", None),
        P(("expert", "wshard"), None),
    )
    return jax.shard_map(
        body,
        mesh=mesh,
        in_specs=placed,
        out_specs=(
            P(("expert", "wshard"), None),
            P(("expert", "wshard"), None),
            P("wshard"),
            P("wshard", None),
            P("wshard", None),
            P("wshard", None),
            P("wshard", None),
            P("wshard", None),
            P("wshard"),
            P("wshard", None),
            P("expert", None, "wshard"),
            P("expert", "wshard", None),
        ),
        check_vma=False,
    )
```

```python
import functools

import jax
import jax.numpy as jnp
from jax import lax
from jax.experimental import pallas as pl
from jax.experimental.pallas import tpu as pltpu
from jax.sharding import PartitionSpec as P

TOPK = 2
epsilon = 1e-06
bf16 = jnp.bfloat16
f32 = jnp.float32
NN = (((1,), (0,)), ((), ()))
NT = (((1,), (1,)), ((), ()))
TN = (((0,), (0,)), ((), ()))


def mm(left, right, dims=NN):
    return lax.dot_general(left, right, dims, preferred_element_type=f32)


def send_xor(value, axis, k):
    n = lax.axis_size(axis)
    return lax.ppermute(value, axis, [(i, i ^ k) for i in range(n)])


def to_xor(stacked, axis, dim=0):
    n = stacked.shape[dim]
    return jnp.take(stacked, jnp.arange(n) ^ lax.axis_index(axis), axis=dim)


def exchange(parts, axis):
    n = len(parts)
    if n <= 8:
        got = [send_xor(parts[k], axis, k) for k in range(n - 1, 0, -1)]
        return [parts[0]] + got[::-1]
    got = lax.all_to_all(to_xor(jnp.stack(parts), axis), axis, 0, 0, tiled=True)
    got = to_xor(got, axis)
    return [got[k] for k in range(n)]


def spread(value, axis):
    n = lax.axis_size(axis)
    if n <= 8:
        return exchange([value] * n, axis)
    got = to_xor(lax.all_gather(value, axis), axis)
    return [got[k] for k in range(n)]


def gather_w(value):
    across = send_xor(value, "wshard", 2)
    beside = send_xor(value, "wshard", 1)
    return [value, beside, across, send_xor(across, "wshard", 1)]


def send_rows(value, experts):
    blocks = value.reshape(experts, -1, value.shape[-1])
    return lax.all_to_all(blocks, "expert", 0, 0, tiled=True).reshape(value.shape)


def start_copies(pairs, sems, first=0):
    copies = [
        pltpu.make_async_copy(src, dst, sems.at[first + i]) for i, (src, dst) in enumerate(pairs)
    ]
    for copy in copies:
        copy.start()
    return copies


def wait_copies(copies):
    for copy in copies:
        copy.wait()


def norm_scale(x):
    return lax.rsqrt(jnp.mean(x * x, axis=-1, keepdims=True) + epsilon)


def pack_kernel(
    w_ref, one_ref, two_ref, router_ref, tok_ref, bucket_ref, wq_ref, wk_ref, wv_ref,
    far_ref, pack_ref, own_out, near_ref,
    tok, bucket, wq, wk, wv, one, two, router, own_ref, sems,
):
    w = w_ref[0]
    copies = start_copies(
        [
            (tok_ref, tok), (bucket_ref, bucket), (wq_ref, wq), (wk_ref, wk), (wv_ref, wv),
            (one_ref, one), (two_ref, two), (router_ref, router),
        ],
        sems,
    )
    wait_copies(copies)
    experts = router.shape[0]
    few_rows = pack_ref.shape[0] - tok.shape[0]
    small = jnp.concatenate(
        [
            one[...].astype(f32).reshape(1, -1),
            two[...].astype(f32).reshape(1, -1),
            router[...].astype(f32),
            jnp.zeros((few_rows - 2 - experts, router.shape[1]), f32),
        ],
        axis=0,
    ).astype(bf16)
    rows, width = tok.shape
    shard = wq.shape[0]
    blocks = width // shard
    half = shard // 2
    parts = [
        (j, slice(i * shard, (i + 1) * shard), ref[:, j * shard : (j + 1) * shard])
        for j in range(blocks)
        for i, ref in enumerate((wq, wk, wv))
    ]
    for j, at, block in parts:

        @pl.when(w == j)
        def _():
            own_ref[:, at] = block

    stores = start_copies([(own_ref, own_out)], sems, 8)
    pack_ref[:rows, :width] = tok[...]
    pack_ref[:rows, width:] = bucket[...].astype(f32).astype(bf16)
    pack_ref[rows:, :] = jnp.zeros((pack_ref.shape[0] - rows, pack_ref.shape[1]), bf16)
    pack_ref[rows:, :shard] = small
    middle = far_ref.shape[1] // 2
    far_ref[: 2 * half, :] = jnp.zeros((2 * half, far_ref.shape[1]), bf16)
    far_ref[2 * half :, :] = pack_ref[...]
    for j, at, block in parts:

        @pl.when(w ^ 1 == j)
        def _():
            near_ref[:, at] = block

        for k in (2, 3):

            @pl.when(w ^ k == j)
            def _():
                place = slice((k - 2) * half, (k - 1) * half)
                far_ref[place, at] = block[:half]
                far_ref[place, middle + at.start : middle + at.stop] = block[half:]

    wait_copies(stores)


def route_kernel(cap, routes_ref, grad_ref, hot_ref, g_ref):
    rows, width = grad_ref.shape
    slots = hot_ref.shape[1]
    first, second = routes_ref[:, 0:1], routes_ref[:, 1:2]
    lanes = lax.broadcasted_iota(jnp.int32, (rows, 128), 1)
    one, two = (lanes == first).astype(f32), (lanes == second).astype(f32)
    lower = lax.broadcasted_iota(jnp.int32, (rows, rows), 1) < lax.broadcasted_iota(
        jnp.int32, (rows, rows), 0
    )
    before = mm(lower.astype(f32).astype(bf16), (one + two).astype(bf16))
    places = lax.broadcasted_iota(jnp.int32, (rows, slots), 1)
    hots = []
    for route, named in ((first, one), (second, two)):
        slot = jnp.sum(before * named, axis=1, keepdims=True).astype(jnp.int32)
        hots.append((places == route * cap + slot).astype(f32))
    hot_ref[...] = (hots[0] + hots[1]).astype(bf16)
    g_ref[:, :width] = mm(hot_ref[...], grad_ref[...], TN).astype(bf16)
    wide = jnp.zeros((rows, 128), f32)
    other = mm(hots[0].astype(bf16), (second.astype(f32) + wide).astype(bf16), TN) + mm(
        hots[1].astype(bf16), (first.astype(f32) + wide).astype(bf16), TN
    )
    g_ref[:, width:] = other.astype(bf16)


def forward_kernel(far_ref, out_ref):
    out_ref[...] = far_ref[far_ref.shape[0] - out_ref.shape[0] :, :]


def attn_forward_kernel(
    w_ref, pack_a_in, pack_b_in, far_c, far_d, col_a_in, col_b_in, table_ref,
    mix_a, mix_b, mix_c, mix_d, small_ref, small_out, mixed_out, probs_out, qkv_out, normed_out, weight_out, token_out,
    ids_out,
    mixed_ref, probs_ref, qkv_ref, normed_ref, weight_ref, token_ref, ids_ref, shift_ref,
    pack_a, pack_b, col_a, col_b, sems, in_sems,
):
    w = w_ref[0]
    fetches = start_copies(
        [(pack_a_in, pack_a), (pack_b_in, pack_b), (col_a_in, col_a), (col_b_in, col_b)], in_sems
    )
    wait_copies(fetches)
    mixes = (mix_a, mix_b, mix_c, mix_d)
    blocks = len(mixes)
    heads, seq, _ = probs_ref.shape
    rows, width = seq // blocks, normed_ref.shape[1]
    shard = width // blocks
    dim = shard // heads
    half, middle = shard // 2, far_c.shape[1] // 2
    weight_ref[w] = col_a[...]
    weight_ref[1 ^ w] = col_b[...]
    weight_ref[2 ^ w, :half] = far_c[:half, : 3 * shard]
    weight_ref[2 ^ w, half:] = far_c[:half, middle : middle + 3 * shard]
    weight_ref[3 ^ w, :half] = far_d[:half, : 3 * shard]
    weight_ref[3 ^ w, half:] = far_d[:half, middle : middle + 3 * shard]
    packs = ((pack_a, 0), (pack_b, 0), (far_c, 2 * half), (far_d, half))
    for k, (ref, at) in enumerate(packs):
        shift_ref[k ^ w] = ref[at + rows :, :shard]
        ids_ref[k ^ w] = ref[at : at + rows, width:]
    for j in range(blocks):
        small_ref[:, j * shard : (j + 1) * shard] = shift_ref[j]
    gain = small_ref[0:1, :].astype(f32)
    weight = weight_ref[...].reshape(width, 3 * shard)
    for k, (ref, at) in enumerate(packs):
        token_ref[k ^ w] = ref[at : at + rows, :width]
        x = ref[at : at + rows, :width].astype(f32)
        normed = (x * norm_scale(x) * gain).astype(bf16)
        place = pl.ds(pl.multiple_of((k ^ w) * rows, rows), rows)
        normed_ref[place, :] = normed
        qkv_ref[place, :] = mm(normed, weight).astype(bf16)
    copies = start_copies(
        [
            (qkv_ref, qkv_out),
            (normed_ref, normed_out),
            (weight_ref, weight_out),
            (token_ref, token_out),
            (ids_ref, ids_out),
            (small_ref, small_out),
        ],
        sems,
    )
    below = lax.broadcasted_iota(jnp.int32, (rows, rows), 1) <= lax.broadcasted_iota(
        jnp.int32, (rows, rows), 0
    )
    for i in range(blocks):
        span = (i + 1) * rows
        ids = ids_ref[i].astype(f32).astype(jnp.int32)
        for h in range(heads):
            query = qkv_ref[i * rows : span, h * dim : (h + 1) * dim]
            keys = qkv_ref[:span, shard + h * dim : shard + (h + 1) * dim]
            values = qkv_ref[:span, 2 * shard + h * dim : 2 * shard + (h + 1) * dim]
            raw = mm(query, keys, NT) * 0.125
            table = jnp.broadcast_to(table_ref[h : h + 1, :], (rows, table_ref.shape[1]))
            bias = [
                jnp.take_along_axis(table, ids[:, j * rows : (j + 1) * rows], axis=1)
                for j in range(i + 1)
            ]
            scores = raw + jnp.concatenate(bias, axis=1) if i else raw + bias[0]
            last = jnp.where(below, scores[:, i * rows :], -1000000000.0)
            scores = jnp.concatenate([scores[:, : i * rows], last], axis=1) if i else last
            raised = jnp.exp(scores - jnp.max(scores, axis=-1, keepdims=True))
            probs = raised / jnp.sum(raised, axis=-1, keepdims=True)
            probs_ref[h, i * rows : span, :span] = probs
            mixed_ref[i, :, h * dim : (h + 1) * dim] = mm(probs.astype(bf16), values).astype(bf16)
        done = slice(i * rows, span)
        copies += start_copies(
            [(probs_ref.at[:, done, :span], probs_out.at[:, done, :span])], sems, 6 + i
        )
    copies += start_copies([(mixed_ref, mixed_out)], sems, 6 + blocks)
    for k in range(blocks):
        mixes[k][...] = mixed_ref[k ^ w]
    wait_copies(copies)


def project_kernel(
    tok_in, small_ref, hot_in, g_in, mix_a, mix_b, mix_c, mix_d, out_a, out_b, out_c, out_d,
    n_ref, residual_out, g_out, tok_ref, hot_ref, residual_ref, sems,
):
    copies = start_copies([(tok_in, tok_ref), (hot_in, hot_ref)], sems)
    g_out[...] = g_in[...]
    residual = 0.0
    for mix, out in ((mix_a, out_a), (mix_b, out_b), (mix_c, out_c), (mix_d, out_d)):
        residual = residual + mm(mix[...], out[...])
    copies[0].wait()
    residual = residual + tok_ref[...].astype(f32)
    residual_ref[...] = residual
    copies += start_copies([(residual_ref, residual_out)], sems, 2)
    normed = (residual * norm_scale(residual) * small_ref[1:2, :].astype(f32)).astype(bf16)
    copies[1].wait()
    n_ref[...] = mm(hot_ref[...], normed, TN).astype(bf16)
    wait_copies(copies[2:])


def expert_kernel(firsts, e_ref, *refs):
    e = e_ref[0]
    count = len(firsts)
    n_refs, g_refs, refs = refs[:count], refs[count : 2 * count], refs[2 * count :]
    (in_ref, out_ref, small_ref), slot_refs, refs = refs[:3], refs[3 : 3 + count], refs[3 + count :]
    hidden_out, pre_out, router_out, hidden_ref, pre_ref, router_ref, sems = refs
    rows, width = n_refs[0].shape
    n = jnp.concatenate([ref[...] for ref in n_refs], axis=0)
    g_all = jnp.concatenate(
        [ref[first : first + rows, :] for first, ref in zip(firsts, g_refs)], axis=0
    )
    g = g_all[:, :width]
    logits = mm(n, small_ref[...], NT)
    lanes = lax.broadcasted_iota(jnp.int32, logits.shape, 1)
    other = g_all[:, width : width + 1].astype(f32).astype(jnp.int32)
    differ = (lanes == 2 + e).astype(f32) - (lanes == 2 + other).astype(f32)
    gate = 1.0 / (1.0 + jnp.exp(-jnp.sum(logits * differ, axis=-1, keepdims=True)))
    pre = mm(n, in_ref[...])
    back = mm(g, out_ref[...], NT)
    square = pre * pre
    bent = jnp.tanh(0.7978845608028654 * pre * (1.0 + 0.044715 * square))
    hidden = 0.5 * pre * (1.0 + bent)
    hidden_ref[...] = (gate * hidden).astype(bf16)
    slope = 0.5 * (1.0 + bent) + 0.5 * pre * (1.0 - bent * bent) * (
        0.7978845608028654 * (1.0 + 3.0 * 0.044715 * square)
    )
    g_gate = jnp.sum(hidden * back, axis=-1, keepdims=True)
    g_logit = (gate * (1.0 - gate) * g_gate * differ).astype(bf16)
    router_ref[...] = mm(g_logit, n, TN)
    g_pre = (gate * back * slope).astype(bf16)
    pre_ref[...] = g_pre
    copies = start_copies(
        [(hidden_ref, hidden_out), (pre_ref, pre_out), (router_ref, router_out)], sems
    )
    slot = mm(g_pre, in_ref[...], NT) + mm(g_logit, small_ref[...])
    for i, ref in enumerate(slot_refs):
        ref[...] = slot[i * rows : (i + 1) * rows].astype(bf16)
    wait_copies(copies)


def result_kernel(in_a, in_b, in_c, in_d, w_ref, *refs):
    outs, held, sems = refs[:4], refs[4:8], refs[8]
    copies = start_copies(list(zip((in_a, in_b, in_c, in_d), held)), sems)
    half = outs[0].shape[0] // 2
    for i in range(4):
        copies[i].wait()
        value = mm(held[i][...], w_ref[...]).astype(bf16)
        if i < 2:
            outs[i][...] = value
        else:
            at = slice((i - 2) * half, (i - 1) * half)
            outs[2][at, :] = value[:half]
            outs[3][at, :] = value[half:]


def expert_grad_kernel(plan, *refs):
    n_count = 1 + max(n for pieces in plan for n, _, _ in pieces)
    g_count = 1 + max(g for pieces in plan for _, g, _ in pieces)
    runs = len(plan)
    n_refs, g_refs, refs = refs[:n_count], refs[n_count : n_count + g_count], refs[n_count + g_count :]
    ins, (g_in, g_out, token_ref), refs = refs[: 2 * runs], refs[2 * runs : 2 * runs + 3], refs[2 * runs + 3 :]
    held, sems = refs[: 2 * runs], refs[-1]
    token_ref[...] = jnp.zeros_like(token_ref)
    copies = start_copies(list(zip(ins, held)), sems)
    width = n_refs[0].shape[1]
    first_term = True
    for i, pieces in enumerate(plan):
        copies[i].wait()
        copies[runs + i].wait()
        at = 0
        for n_at, g_at, first in pieces:
            n = n_refs[n_at][...]
            rows = n.shape[0]
            pre, hidden = held[i][at : at + rows, :], held[runs + i][at : at + rows, :]
            g = g_refs[g_at][first : first + rows, :width]
            at += rows
            for ref, term in ((g_in, mm(n, pre, TN)), (g_out, mm(hidden, g, TN))):
                if first_term:
                    ref[...] = term
                else:
                    ref[...] += term
            first_term = False


def pair_kernel(*refs):
    count = (len(refs) - 1) // 2
    step = refs[0].shape[0]
    for i in range(count):
        total = refs[i][...].astype(f32) + refs[count + i][...].astype(f32)
        refs[-1][i * step : (i + 1) * step, :] = total.astype(bf16)


def total_kernel(own_ref, beside_ref, *refs):
    across, out_ref = refs[:-1], refs[-1]
    step = out_ref.shape[0] // len(across)
    for a, ref in enumerate(across):
        at = slice(a * step, (a + 1) * step)
        total = own_ref[at, :].astype(f32) + beside_ref[at, :].astype(f32) + ref[...].astype(f32)
        out_ref[at, :] = total.astype(bf16)


def second_norm_kernel(
    residual_in, small_in, hot_in, grad_in, got_ref, low_ref, gain_ref, grad_residual_out,
    residual_ref, small_ref, hot_ref, grad_ref, grad_residual_ref, sems,
):
    copies = start_copies(
        [(hot_in, hot_ref), (residual_in, residual_ref), (small_in, small_ref), (grad_in, grad_ref)],
        sems,
    )
    wait_copies(copies)
    g_normed = mm(hot_ref[...], got_ref[...])
    residual = residual_ref[...]
    scale = norm_scale(residual)
    scaled = g_normed * small_ref[1:2, :].astype(f32)
    grad = (
        grad_ref[...].astype(f32)
        + scale * scaled
        - residual * scale * scale * scale * jnp.mean(scaled * residual, axis=-1, keepdims=True)
    )
    grad_residual_ref[...] = grad
    stores = start_copies([(grad_residual_ref, grad_residual_out)], sems, 4)
    low_ref[...] = grad.astype(bf16)
    gain_ref[...] = jnp.sum(g_normed * residual * scale, axis=0, keepdims=True)
    wait_copies(stores)


def block_out_kernel(residual_ref, hot_ref, got_ref, out_ref):
    out_ref[...] = (residual_ref[...] + mm(hot_ref[...], got_ref[...])).astype(bf16)


def attn_backward_kernel(
    ids_ref, grad_a, grad_b, grad_c, grad_d, wout_in, qkv_in, probs_in,
    grads_ref, scores_out, wout_ref, qkv_ref, probs_ref, scores_ref, gmix_ref, part_ref, sems,
):
    w = ids_ref[0]
    packs = (grad_a, grad_b, grad_c, grad_d)
    blocks = len(packs)
    rows = grad_a.shape[0]
    spans = [(slice(i * rows, (i + 1) * rows), (i + 1) * rows) for i in range(blocks)]
    copies = start_copies(
        [(wout_in, wout_ref), (qkv_in, qkv_ref)]
        + [(probs_in.at[:, at, :span], probs_ref.at[:, at, :span]) for at, span in spans],
        sems,
    )
    copies[0].wait()
    rows, width = grad_a.shape
    shard = width // blocks
    heads = probs_ref.shape[0]
    dim = shard // heads
    for k in range(blocks):
        place = pl.ds(pl.multiple_of((k ^ w) * rows, rows), rows)
        gmix_ref[place, :] = mm(packs[k][...], wout_ref[...], NT).astype(bf16)
    part_ref[...] = jnp.zeros_like(part_ref)
    copies[1].wait()
    stores = []
    for i in range(blocks):
        span = (i + 1) * rows
        copies[2 + i].wait()
        for h in range(heads):
            query = qkv_ref[i * rows : span, h * dim : (h + 1) * dim]
            keys = qkv_ref[:span, shard + h * dim : shard + (h + 1) * dim]
            values = qkv_ref[:span, 2 * shard + h * dim : 2 * shard + (h + 1) * dim]
            gmix = gmix_ref[i * rows : span, h * dim : (h + 1) * dim]
            probs = probs_ref[h, i * rows : span, :span]
            gprobs = mm(gmix, values, NT)
            inner = jnp.sum(probs * gprobs, axis=-1, keepdims=True)
            gscores = probs * (gprobs - inner)
            scores_ref[h, i * rows : span, :span] = gscores
            low = gscores.astype(bf16)
            grads_ref[i * rows : span, h * dim : (h + 1) * dim] = (mm(low, keys) * 0.125).astype(
                bf16
            )
            part_ref[0, h, :span, :] += mm(low, query, TN)
            part_ref[1, h, :span, :] += mm(probs.astype(bf16), gmix, TN)
        at = slice(i * rows, span)
        stores += start_copies(
            [(scores_ref.at[:, at, :span], scores_out.at[:, at, :span])], sems, 2 + blocks + i
        )
    for h in range(heads):
        grads_ref[:, shard + h * dim : shard + (h + 1) * dim] = (part_ref[0, h] * 0.125).astype(
            bf16
        )
        grads_ref[:, 2 * shard + h * dim : 2 * shard + (h + 1) * dim] = part_ref[1, h].astype(bf16)
    wait_copies(stores)


def weight_grad_kernel(
    ids_ref, grad_a, grad_b, grad_c, grad_d, normed_in, mixed_in, grads_ref, *refs
):
    *outs, stage_ref, normed_ref, mixed_ref, sems = refs
    w = ids_ref[0]
    copies = start_copies([(mixed_in, mixed_ref), (normed_in, normed_ref)], sems)
    copies[0].wait()
    gout = functools.reduce(
        lambda p, q: p + q,
        [
            mm(mixed_ref[k ^ w], ref[...], TN)
            for k, ref in enumerate((grad_a, grad_b, grad_c, grad_d))
        ],
    )
    copies[1].wait()
    gqkv = mm(normed_ref[...], grads_ref[...], TN)
    if len(outs) == 2:
        outs[0][...] = gqkv
        outs[1][...] = gout
        return
    ne = stage_ref.shape[0]
    shard, width = gout.shape
    nw = width // shard
    piece = shard // ne
    for j in range(nw):
        for s in range(ne):
            row = j * shard + s * piece
            stage_ref[s, j ^ w, :, : 3 * shard] = gqkv[row : row + piece].astype(bf16)
            stage_ref[s, j, :, 3 * shard :] = gout[
                s * piece : (s + 1) * piece, j * shard : (j + 1) * shard
            ].astype(bf16)
    wait_copies(start_copies([(stage_ref, outs[0])], sems, 2))


def weight_sum_kernel(in_ref, *refs):
    outs, gout_ref = refs[:-1], refs[-1]
    for k, out in enumerate(outs):
        total = functools.reduce(
            lambda p, q: p + q, [in_ref[i, k].astype(f32) for i in range(in_ref.shape[0])]
        )
        cut = out.shape[1]
        out[...] = total[:, :cut].astype(bf16)
        gout_ref[k] = total[:, cut:].astype(bf16)


def weight_pack_kernel(a_ref, b_ref, c_ref, d_ref, gout_ref, few_ref, bias_ref, out_ref, stage):
    piece, cut = a_ref.shape
    width = stage.shape[1]
    shard = width - cut
    stage[...] = jnp.zeros_like(stage)
    for k, ref in enumerate((a_ref, b_ref, c_ref, d_ref)):
        stage[k * piece : (k + 1) * piece, :cut] = ref[...].astype(f32)
        stage[k * piece : (k + 1) * piece, cut:] = gout_ref[k].astype(f32)
    at = 4 * piece
    few = few_ref[...]
    high = few.astype(bf16).astype(f32)
    for i, part in enumerate((high[:8], high[8:], (few - high)[:8], (few - high)[8:])):
        if i % 2 == 0:
            stage[at : at + 8, i * shard : (i + 1) * shard] = part
        else:
            stage[at : at + 4, i * shard : (i + 1) * shard] = part[:4]
    bias = bias_ref[...]
    high = bias.astype(bf16).astype(f32)
    stage[at + 4 : at + 8, shard : shard + 128] = high[:4]
    stage[at + 4 : at + 8, 3 * shard : 3 * shard + 128] = (bias - high)[:4]
    out_ref[...] = stage[...].astype(bf16)


def weight_join_kernel(ids_ref, *refs):
    w, e = ids_ref[0], ids_ref[1]
    ins, outs, one_ref, two_ref, router_ref, bias_ref, stage = (
        refs[:-9], refs[-9:-5], refs[-5], refs[-4], refs[-3], refs[-2], refs[-1]
    )
    shard, width = outs[0].shape
    nw, piece = width // shard, stage.shape[1]
    at = nw * piece
    few = 0.0
    for k, ref in enumerate(ins):
        place = pl.ds(pl.multiple_of((k ^ e) * piece, piece), piece)
        value = ref[...].astype(f32)
        for j in range(nw):
            mine = value[j * piece : (j + 1) * piece]
            stage[j ^ w] = mine
            outs[3][place, j * shard : (j + 1) * shard] = mine[:, 3 * shard :]
        for j in range(nw):
            mine = stage[j]
            for i in range(3):
                outs[i][place, j * shard : (j + 1) * shard] = mine[:, i * shard : (i + 1) * shard]
        few += value[at:, : 2 * shard] + value[at:, 2 * shard :]
    one_ref[...] = few[0:1, :shard]
    two_ref[...] = few[1:2, :shard]
    bias = few[4:5, shard:]
    experts = router_ref.shape[0]
    router_ref[:6, :] = few[2:8, :shard]
    router_ref[6:, :] = few[: experts - 6, shard:]
    heads, bins = bias_ref.shape
    for h in range(heads):
        bias_ref[h : h + 1, :] = bias[:, h * bins : (h + 1) * bins]


def input_grad_kernel(
    w_ref, grads_ref, weight_in, token_in, gain_ref, *refs,
):
    *router_in, back_a, back_b, back_c, back_d, few_ref, weight_ref, token_ref, router_ref, sems = (
        refs
    )
    w = w_ref[0]
    wait_copies(
        start_copies(
            [(weight_in, weight_ref), (token_in, token_ref)]
            + [(ref, router_ref.at[i]) for i, ref in enumerate(router_in)],
            sems,
        )
    )
    backs = (back_a, back_b, back_c, back_d)
    blocks, rows, width = token_ref.shape
    shard = width // blocks
    weight = weight_ref[...].reshape(width, 3 * shard)
    total = jnp.zeros((1, width), f32)
    for k in range(blocks):
        place = pl.ds(pl.multiple_of((k ^ w) * rows, rows), rows)
        back = mm(grads_ref[place, :], weight, NT)
        backs[k][:rows, :] = back.astype(bf16)
        x = token_ref[k ^ w].astype(f32)
        total += jnp.sum(back * x * norm_scale(x), axis=0, keepdims=True)
    few = jnp.sum(router_ref[...], axis=0)
    line = lax.broadcasted_iota(jnp.int32, few.shape, 0)
    few = jnp.where(line == 0, total, jnp.where(line == 1, gain_ref[...], few))
    for j in range(blocks):
        few_ref[j] = few[:, j * shard : (j + 1) * shard].astype(bf16)
    for k in range(blocks):
        backs[k][rows:, :] = jnp.zeros((few.shape[0], width), bf16)
        backs[k][rows:, :shard] = few_ref[k ^ w]


def bias_grad_kernel(ids_in, scores_in, out_ref, part_ref, ids_ref, scores_ref, sems):
    wait_copies(start_copies([(ids_in, ids_ref), (scores_in, scores_ref)], sems))
    heads, seq, _ = scores_ref.shape
    blocks, rows, _ = ids_ref.shape
    bins = part_ref.shape[0] // heads
    part_ref[...] = jnp.zeros_like(part_ref)
    for i in range(blocks):
        span = (i + 1) * rows
        ids = ids_ref[i, :, :span].astype(f32).astype(jnp.int32)
        for b in range(bins):
            hit = ids == b
            for h in range(heads):
                picked = jnp.where(hit, scores_ref[h, i * rows : span, :span], 0.0)
                part_ref[h * bins + b : h * bins + b + 1, :] += functools.reduce(
                    lambda p, q: p + q,
                    [
                        jnp.sum(picked[:, j * rows : (j + 1) * rows], axis=0, keepdims=True)
                        for j in range(i + 1)
                    ],
                )
    spread_out = jnp.concatenate(
        [part_ref[...], jnp.zeros((128 - part_ref.shape[0], 128), f32)], axis=0
    )
    out_ref[...] = lax.dot_general(
        jnp.ones((8, 128), f32), spread_out, NT, precision=lax.Precision.HIGHEST,
        preferred_element_type=f32,
    )


def tokens_grad_kernel(
    tok_ref, small_ref, residual_ref, a_ref, b_ref, c_ref, out_ref, few_ref
):
    rows = tok_ref.shape[0]
    shard = few_ref.shape[1]
    total = a_ref[...].astype(f32) + b_ref[...].astype(f32) + c_ref[...].astype(f32)
    grad = total[:rows]
    few_ref[...] = total[rows:, :shard]
    x = tok_ref[...].astype(f32)
    scale = norm_scale(x)
    scaled = grad * small_ref[0:1, :].astype(f32)
    out_ref[...] = (
        residual_ref[...]
        + scale * scaled
        - x * scale * scale * scale * jnp.mean(scaled * x, axis=-1, keepdims=True)
    )


def shaped(shape, dtype=bf16):
    return jax.ShapeDtypeStruct(shape, dtype)


def on_chip(
    kernel, outs, scratch, *args, scalars=(0,), flops=0, stay=(), leave=(), deps=(), limit=32,
    weight=1000,
):
    count = len(args)
    args = [
        pltpu.with_memory_space_constraint(a, pltpu.HBM) if i in stay else a
        for i, a in enumerate(args)
    ]
    places = [
        pltpu.SMEM if i in scalars else pltpu.HBM if i in stay else pltpu.VMEM
        for i in range(count)
    ] + [pl.ANY] * len(deps)

    def run(*refs):
        kernel(*refs[:count], *refs[count + len(deps) :])

    size = sum(a.size * a.dtype.itemsize for a in (*args, *outs))
    return pl.pallas_call(
        run,
        out_shape=[
            pltpu.HBM(a.shape, a.dtype) if i in leave else a for i, a in enumerate(outs)
        ],
        in_specs=[pl.BlockSpec(memory_space=place) for place in places],
        out_specs=[
            pl.BlockSpec(memory_space=pltpu.HBM if i in leave else pltpu.VMEM)
            for i in range(len(outs))
        ],
        scratch_shapes=scratch,
        compiler_params=pltpu.CompilerParams(vmem_limit_bytes=limit * 1024 * 1024),
        cost_estimate=pl.CostEstimate(
            flops=flops + weight * size, bytes_accessed=size * weight // 1000, transcendentals=0
        ),
    )(*args, *deps)


def hold(value, *deps):
    return pl.pallas_call(
        lambda *refs: None,
        out_shape=shaped(value.shape, value.dtype),
        in_specs=[pl.BlockSpec(memory_space=pl.ANY)] * (1 + len(deps)),
        out_specs=pl.BlockSpec(memory_space=pl.ANY),
        input_output_aliases={0: 0},
        cost_estimate=pl.CostEstimate(flops=0, bytes_accessed=0, transcendentals=0),
    )(value, *deps)


def run_expert(pieces, e_arr, w_in, w_out, small, deps=()):
    rows, width = pieces[0][0].shape
    hidden = w_in.shape[1]
    count = len(pieces)
    kept = [
        shaped((rows * count, hidden)), shaped((rows * count, hidden)),
        shaped((small.shape[0], width), f32),
    ]
    return on_chip(
        functools.partial(expert_kernel, [first for _, _, first in pieces]),
        [shaped((rows, width))] * count + kept,
        [pltpu.VMEM(a.shape, a.dtype) for a in kept] + [pltpu.SemaphoreType.DMA((3,))],
        e_arr, *[n for n, _, _ in pieces], *[g for _, g, _ in pieces], w_in, w_out, small,
        leave=range(count, count + 3), deps=deps,
    )


def add_pair(mine, other, deps=()):
    other = send_xor(other, "wshard", 1)
    return on_chip(
        pair_kernel, [shaped(other.shape)], [], mine, other, scalars=(), deps=deps
    )[0]


def scatter_parts(parts, deps=()):
    across = send_xor(add_pair(parts[2], parts[3], deps), "wshard", 2)
    beside = send_xor(parts[1], "wshard", 1)
    return parts[0], beside, across


def body(
    tokens, routes, buckets, gain_one, w_query, w_key, w_value, w_output, pos_bias, gain_two,
    w_router, expert_in, expert_out, grad_out,
):
    rows, width = tokens.shape
    nw, ne = lax.axis_size("wshard"), lax.axis_size("expert")
    w, e = lax.axis_index("wshard"), lax.axis_index("expert")
    w_arr, e_arr = w.astype(jnp.int32).reshape(1), e.astype(jnp.int32).reshape(1)
    ids = jnp.concatenate([w_arr, e_arr])
    shard = width // nw
    heads, bins = pos_bias.shape
    dim = shard // heads
    seq = rows * nw
    experts = w_router.shape[1]
    cap = 3 * rows * TOPK // (2 * experts)
    slots = experts * cap
    few_rows = -(-(2 + experts) // 16) * 16

    far, pack, col_own, col_near = on_chip(
        pack_kernel,
        [
            shaped((shard + rows + few_rows, width + seq)),
            shaped((rows + few_rows, width + seq)),
            shaped((shard, 3 * shard)),
            shaped((shard, 3 * shard)),
        ],
        [
            pltpu.VMEM((rows, width), bf16),
            pltpu.VMEM((rows, seq), jnp.int32),
            pltpu.VMEM((shard, width), bf16),
            pltpu.VMEM((shard, width), bf16),
            pltpu.VMEM((shard, width), bf16),
            pltpu.VMEM((shard,), bf16),
            pltpu.VMEM((shard,), bf16),
            pltpu.VMEM((experts, shard), bf16),
            pltpu.VMEM((shard, 3 * shard), bf16),
            pltpu.SemaphoreType.DMA((9,)),
        ],
        w_arr, gain_one, gain_two, w_router.T, tokens, buckets, w_query, w_key, w_value,
        stay=range(1, 9), leave=(2,),
    )
    far_c = send_xor(far, "wshard", 2)
    pack_b, col_b = send_xor(pack, "wshard", 1), send_xor(col_near, "wshard", 1)
    hot, g_rows = on_chip(
        functools.partial(route_kernel, cap),
        [shaped((rows, slots)), shaped((slots, width + 128))],
        [],
        routes, grad_out, scalars=(), deps=(pack_b, col_b),
    )
    g_got = send_rows(g_rows, experts)
    far_rest = on_chip(
        forward_kernel, [shaped((far.shape[0] - shard // 2, far.shape[1]))], [], far_c,
        scalars=(),
    )[0]
    far_d = send_xor(far_rest, "wshard", 1)
    wout_far, wout_near = send_xor(w_output, "wshard", 2), send_xor(w_output, "wshard", 1)

    table = jnp.zeros((8, 128), f32).at[:heads, :bins].set(pos_bias.astype(f32))
    kept = [
        shaped((few_rows, width)),
        shaped((nw, rows, shard)),
        shaped((heads, seq, seq), f32),
        shaped((seq, 3 * shard)),
        shaped((seq, width)),
        shaped((nw, shard, 3 * shard)),
        shaped((nw, rows, width)),
        shaped((nw, rows, seq)),
    ]
    *mixed, small, small_far, mixed_far, probs, qkv, normed_one, weight, tok_all, bucket_all = on_chip(
        attn_forward_kernel,
        [shaped((rows, shard))] * nw + [shaped((few_rows, width))] + kept,
        [pltpu.VMEM(a.shape, a.dtype) for a in kept[1:]]
        + [
            pltpu.VMEM((nw, few_rows, shard), bf16),
            pltpu.VMEM(pack.shape, bf16),
            pltpu.VMEM(pack.shape, bf16),
            pltpu.VMEM(col_own.shape, bf16),
            pltpu.VMEM(col_own.shape, bf16),
            pltpu.SemaphoreType.DMA((7 + nw,)),
            pltpu.SemaphoreType.DMA((4,)),
        ],
        w_arr, pack, pack_b, far_c, far_d, col_own, col_b, table,
        stay=(1, 2, 5, 6), leave=range(nw + 1, nw + 9), weight=200,
    )
    mixed_got = exchange(mixed, "wshard")
    wout_rest = on_chip(
        forward_kernel, [shaped(w_output.shape)], [], wout_far, scalars=(), deps=(mixed[0], g_got)
    )[0]
    wout_all = [w_output, wout_near, wout_far, send_xor(wout_rest, "wshard", 1)]
    n_rows, residual, g_mine = on_chip(
        project_kernel,
        [shaped((slots, width)), shaped((rows, width), f32), shaped(g_got.shape)],
        [
            pltpu.VMEM((rows, width), bf16),
            pltpu.VMEM((rows, slots), bf16),
            pltpu.VMEM((rows, width), f32),
            pltpu.SemaphoreType.DMA((3,)),
        ],
        tokens, small, hot, g_got, *mixed_got, *wout_all,
        scalars=(), stay=(0, 2), leave=(1,),
    )

    w_in, w_back = expert_in[0], expert_out[0]
    half = slots // 2
    g_parts = gather_w(g_mine)
    n_got = send_rows(n_rows, experts)
    n_far = [send_xor(n_got[a * half : (a + 1) * half], "wshard", 2) for a in range(2)]
    n_near = send_xor(n_got, "wshard", 1)
    plan = [
        [(0, 0, 0)], [(1, 1, 0)], [(2, 2, 0), (3, 3, 0)], [(4, 2, half), (5, 3, half)]
    ]
    n_all = [n_got, n_near]
    runs, order = [], ()
    for step, pieces in enumerate(plan):
        if step >= 2:
            n = n_far[step - 2]
            if step == 2:
                rest = on_chip(forward_kernel, [shaped(n.shape)], [], n, scalars=(), deps=order)[0]
            else:
                rest = n
            n_all += [n, send_xor(rest, "wshard", 1)]
        run = run_expert(
            [(n_all[n], g_parts[g], first) for n, g, first in pieces], e_arr, w_in, w_back, small, order
        )
        runs.append(run)
        order = run[:1]
    hidden, g_pre, g_router = zip(*(run[-3:] for run in runs))
    other = [send_xor(run[1], "wshard", 1) for run in runs[2:]]
    pair = on_chip(
        pair_kernel, [shaped((slots, width))], [], runs[2][0], runs[3][0], *other, scalars=()
    )[0]
    across = send_xor(pair, "wshard", 2)
    beside = send_xor(runs[1][0], "wshard", 1)
    parts = len(runs)
    result = on_chip(
        result_kernel, [shaped((slots, width))] * parts,
        [pltpu.VMEM((slots, width), bf16)] * parts + [pltpu.SemaphoreType.DMA((parts,))],
        *hidden, w_back, scalars=(), stay=range(parts),
    )
    g_total = on_chip(
        total_kernel, [shaped((slots, width))], [], runs[0][0], beside, across,
        scalars=(),
    )[0]
    g_back = send_rows(g_total, experts)

    result_total = on_chip(
        total_kernel, [shaped((slots, width))], [], *scatter_parts(result, deps=(g_total,)),
        scalars=(), deps=(g_back,),
    )[0]
    g_in_w, g_out_w, token = on_chip(
        functools.partial(expert_grad_kernel, plan),
        [
            shaped((width, w_in.shape[1]), f32),
            shaped((w_in.shape[1], width), f32),
            shaped((8, 128), f32),
        ],
        [pltpu.VMEM((slots, w_in.shape[1]), bf16)] * (2 * parts)
        + [pltpu.SemaphoreType.DMA((2 * parts,))],
        *n_all, *g_parts, *g_pre, *hidden,
        scalars=(), stay=range(6 + nw, 6 + nw + 2 * parts), deps=(g_total,), limit=40,
        flops=4 * 4 * slots * width * width,
    )

    grad_low, grad_gain_b, grad_residual = on_chip(
        second_norm_kernel,
        [shaped((rows, width)), shaped((1, width), f32), shaped((rows, width), f32)],
        [
            pltpu.VMEM((rows, width), f32),
            pltpu.VMEM((few_rows, width), bf16),
            pltpu.VMEM((rows, slots), bf16),
            pltpu.VMEM((rows, width), bf16),
            pltpu.VMEM((rows, width), f32),
            pltpu.SemaphoreType.DMA((5,)),
        ],
        residual, small_far, hot, grad_out, g_back,
        scalars=(), stay=range(4), leave=(2,), deps=(token,),
    )
    grad_all = gather_w(grad_low)
    result_got = send_rows(result_total, experts)

    block_out = on_chip(
        block_out_kernel, [shaped((rows, width))], [], residual, hot, result_got, scalars=()
    )[0]
    fast = ne <= 8 and shard % (8 * ne) == 0 and few_rows == 16 and 6 < experts <= 10
    piece = shard // ne
    if fast:
        weight_outs = [shaped((ne, nw, piece, width))]
    else:
        weight_outs = [shaped((width, 3 * shard), f32), shaped((shard, width), f32)]
    grads, scores = on_chip(
        attn_backward_kernel,
        [shaped((seq, 3 * shard)), shaped((heads, seq, seq), f32)],
        [
            pltpu.VMEM((shard, width), bf16),
            pltpu.VMEM((seq, 3 * shard), bf16),
            pltpu.VMEM((heads, seq, seq), f32),
            pltpu.VMEM((heads, seq, seq), f32),
            pltpu.VMEM((seq, shard), bf16),
            pltpu.VMEM((2, heads, seq, dim), f32),
            pltpu.SemaphoreType.DMA((2 + 2 * nw,)),
        ],
        ids, *grad_all, w_output, qkv, probs, stay=range(1 + nw, 4 + nw), leave=(1,),
        weight=650,
    )
    chunks = on_chip(
        weight_grad_kernel,
        weight_outs,
        [
            pltpu.VMEM((ne, nw, piece, width) if fast else (8, 128), bf16),
            pltpu.VMEM((seq, width), bf16),
            pltpu.VMEM((nw, rows, shard), bf16),
            pltpu.SemaphoreType.DMA((3,)),
        ],
        ids, *grad_all, normed_one, mixed_far, grads, stay=(1 + nw, 2 + nw),
        leave=(0,) if fast else (), weight=650,
    )
    chunks = [hold(chunks[0], result_got), *chunks[1:]]
    back = on_chip(
        input_grad_kernel,
        [shaped((rows + few_rows, width))] * nw,
        [
            pltpu.VMEM((nw, few_rows, shard), bf16),
            pltpu.VMEM((nw, shard, 3 * shard), bf16),
            pltpu.VMEM((nw, rows, width), bf16),
            pltpu.VMEM((parts, few_rows, width), f32),
            pltpu.SemaphoreType.DMA((2 + parts,)),
        ],
        w_arr, grads, weight, tok_all, grad_gain_b, *g_router,
        stay=(2, 3, *range(5, 5 + parts)), deps=chunks[:1],
    )
    bias = on_chip(
        bias_grad_kernel,
        [shaped((8, 128), f32)],
        [
            pltpu.VMEM((heads * bins, 128), f32),
            pltpu.VMEM((nw, rows, seq), bf16),
            pltpu.VMEM((heads, seq, seq), f32),
            pltpu.SemaphoreType.DMA((2,)),
        ],
        bucket_all, scores, scalars=(), stay=(0, 1), deps=chunks[:1],
    )[0]
    grad_tokens, few = on_chip(
        tokens_grad_kernel, [shaped((rows, width), f32), shaped((few_rows, shard), f32)], [],
        tokens, small, grad_residual, *scatter_parts(back), scalars=(),
    )
    if fast:
        got = lax.all_to_all(chunks[0], "expert", 0, 0, tiled=True)
        *sums, gout = on_chip(
            weight_sum_kernel,
            [shaped((piece, 3 * shard))] * nw + [shaped((nw, piece, shard))],
            [],
            got, scalars=(),
        )
        swapped = exchange(sums, "wshard")
        joined = on_chip(
            weight_pack_kernel, [shaped((nw * piece + 8, width))],
            [pltpu.VMEM((nw * piece + 8, width), f32)],
            *swapped, gout, few, bias, scalars=(),
        )[0]
        *weights, gain_a, gain_b, router, bias = on_chip(
            weight_join_kernel,
            [shaped((shard, width), f32)] * 4
            + [shaped(shape, f32) for shape in ((1, shard), (1, shard), (experts, shard), (heads, bins))],
            [pltpu.VMEM((nw, piece, width), f32)],
            ids, *spread(joined, "expert"),
        )
    else:
        gqkv, gout = chunks
        pieces_w = to_xor(to_xor(gqkv.reshape(nw, ne, piece, 3 * shard), "expert", 1), "wshard")
        pieces_w = pieces_w.astype(bf16)
        pieces_o = to_xor(gout.reshape(ne, piece, width), "expert").astype(bf16)
        add = lambda parts: functools.reduce(lambda a, b: a + b, [c.astype(f32) for c in parts])
        total = add(exchange([pieces_w[:, k] for k in range(ne)], "expert")).astype(bf16)
        total_out = add(exchange([pieces_o[k] for k in range(ne)], "expert")).astype(bf16)
        swapped = jnp.stack(exchange([total[k] for k in range(nw)], "wshard"))
        swapped = to_xor(swapped, "wshard").reshape(nw, piece, 3, shard).transpose(1, 2, 0, 3)
        joined = jnp.concatenate([swapped.reshape(piece, 3 * width), total_out], axis=1)
        whole = to_xor(jnp.stack(spread(joined, "expert")), "expert").reshape(shard, 4 * width)
        whole = whole.astype(f32)
        weights = [whole[:, i * width : (i + 1) * width] for i in range(4)]
        few, bias = lax.psum((few, bias), "expert")
        gain_a, gain_b, router = few[0], few[1], few[2 : 2 + experts]
        bias = bias[0, : heads * bins].reshape(heads, bins)
    return (
        block_out,
        grad_tokens,
        gain_a.reshape(shard),
        *weights,
        bias,
        gain_b.reshape(shard),
        router.T,
        g_in_w[None],
        g_out_w[None],
    )


def solution(mesh):
    placed = (
        P(("expert", "wshard"), None),
        P(("expert", "wshard"), None),
        P(("expert", "wshard"), None),
        P("wshard"),
        P("wshard", None),
        P("wshard", None),
        P("wshard", None),
        P("wshard", None),
        P("wshard", None),
        P("wshard"),
        P("wshard", None),
        P("expert", None, "wshard"),
        P("expert", "wshard", None),
        P(("expert", "wshard"), None),
    )
    return jax.shard_map(
        body,
        mesh=mesh,
        in_specs=placed,
        out_specs=(
            P(("expert", "wshard"), None),
            P(("expert", "wshard"), None),
            P("wshard"),
            P("wshard", None),
            P("wshard", None),
            P("wshard", None),
            P("wshard", None),
            P("wshard", None),
            P("wshard"),
            P("wshard", None),
            P("expert", None, "wshard"),
            P("expert", "wshard", None),
        ),
        check_vma=False,
    )
```

```python
import functools

import jax
import jax.numpy as jnp
from jax import lax
from jax.experimental import pallas as pl
from jax.experimental.pallas import tpu as pltpu
from jax.sharding import PartitionSpec as P

TOPK = 2
epsilon = 1e-06
bf16 = jnp.bfloat16
f32 = jnp.float32
NN = (((1,), (0,)), ((), ()))
NT = (((1,), (1,)), ((), ()))
TN = (((0,), (0,)), ((), ()))


def mm(left, right, dims=NN):
    return lax.dot_general(left, right, dims, preferred_element_type=f32)


def send_xor(value, axis, k):
    n = lax.axis_size(axis)
    return lax.ppermute(value, axis, [(i, i ^ k) for i in range(n)])


def to_xor(stacked, axis, dim=0):
    n = stacked.shape[dim]
    return jnp.take(stacked, jnp.arange(n) ^ lax.axis_index(axis), axis=dim)


def exchange(parts, axis):
    n = len(parts)
    if n <= 8:
        got = [send_xor(parts[k], axis, k) for k in range(n - 1, 0, -1)]
        return [parts[0]] + got[::-1]
    got = lax.all_to_all(to_xor(jnp.stack(parts), axis), axis, 0, 0, tiled=True)
    got = to_xor(got, axis)
    return [got[k] for k in range(n)]


def spread(value, axis):
    n = lax.axis_size(axis)
    if n <= 8:
        return exchange([value] * n, axis)
    got = to_xor(lax.all_gather(value, axis), axis)
    return [got[k] for k in range(n)]


def gather_w(value):
    across = send_xor(value, "wshard", 2)
    beside = send_xor(value, "wshard", 1)
    return [value, beside, across, send_xor(across, "wshard", 1)]


def send_rows(value, experts):
    blocks = value.reshape(experts, -1, value.shape[-1])
    return lax.all_to_all(blocks, "expert", 0, 0, tiled=True).reshape(value.shape)


def start_copies(pairs, sems, first=0):
    copies = [
        pltpu.make_async_copy(src, dst, sems.at[first + i]) for i, (src, dst) in enumerate(pairs)
    ]
    for copy in copies:
        copy.start()
    return copies


def wait_copies(copies):
    for copy in copies:
        copy.wait()


def norm_scale(x):
    return lax.rsqrt(jnp.mean(x * x, axis=-1, keepdims=True) + epsilon)


def pack_kernel(
    w_ref, one_ref, two_ref, router_ref, tok_ref, bucket_ref, wq_ref, wk_ref, wv_ref,
    far_ref, pack_ref, own_out, near_ref,
    tok, bucket, wq, wk, wv, one, two, router, own_ref, sems,
):
    w = w_ref[0]
    copies = start_copies(
        [
            (tok_ref, tok), (bucket_ref, bucket), (wq_ref, wq), (wk_ref, wk), (wv_ref, wv),
            (one_ref, one), (two_ref, two), (router_ref, router),
        ],
        sems,
    )
    wait_copies(copies)
    experts = router.shape[0]
    few_rows = pack_ref.shape[0] - tok.shape[0]
    small = jnp.concatenate(
        [
            one[...].astype(f32).reshape(1, -1),
            two[...].astype(f32).reshape(1, -1),
            router[...].astype(f32),
            jnp.zeros((few_rows - 2 - experts, router.shape[1]), f32),
        ],
        axis=0,
    ).astype(bf16)
    rows, width = tok.shape
    shard = wq.shape[0]
    blocks = width // shard
    half = shard // 2
    parts = [
        (j, slice(i * shard, (i + 1) * shard), ref[:, j * shard : (j + 1) * shard])
        for j in range(blocks)
        for i, ref in enumerate((wq, wk, wv))
    ]
    for j, at, block in parts:

        @pl.when(w == j)
        def _():
            own_ref[:, at] = block

    stores = start_copies([(own_ref, own_out)], sems, 8)
    pack_ref[:rows, :width] = tok[...]
    pack_ref[:rows, width:] = bucket[...].astype(f32).astype(bf16)
    pack_ref[rows:, :] = jnp.zeros((pack_ref.shape[0] - rows, pack_ref.shape[1]), bf16)
    pack_ref[rows:, :shard] = small
    middle = far_ref.shape[1] // 2
    far_ref[: 2 * half, :] = jnp.zeros((2 * half, far_ref.shape[1]), bf16)
    far_ref[2 * half :, :] = pack_ref[...]
    for j, at, block in parts:

        @pl.when(w ^ 1 == j)
        def _():
            near_ref[:, at] = block

        for k in (2, 3):

            @pl.when(w ^ k == j)
            def _():
                place = slice((k - 2) * half, (k - 1) * half)
                far_ref[place, at] = block[:half]
                far_ref[place, middle + at.start : middle + at.stop] = block[half:]

    wait_copies(stores)


def route_kernel(cap, routes_ref, grad_ref, hot_ref, g_ref):
    rows, width = grad_ref.shape
    slots = hot_ref.shape[1]
    first, second = routes_ref[:, 0:1], routes_ref[:, 1:2]
    lanes = lax.broadcasted_iota(jnp.int32, (rows, 128), 1)
    one, two = (lanes == first).astype(f32), (lanes == second).astype(f32)
    lower = lax.broadcasted_iota(jnp.int32, (rows, rows), 1) < lax.broadcasted_iota(
        jnp.int32, (rows, rows), 0
    )
    before = mm(lower.astype(f32).astype(bf16), (one + two).astype(bf16))
    places = lax.broadcasted_iota(jnp.int32, (rows, slots), 1)
    hots = []
    for route, named in ((first, one), (second, two)):
        slot = jnp.sum(before * named, axis=1, keepdims=True).astype(jnp.int32)
        hots.append((places == route * cap + slot).astype(f32))
    hot_ref[...] = (hots[0] + hots[1]).astype(bf16)
    g_ref[:, :width] = mm(hot_ref[...], grad_ref[...], TN).astype(bf16)
    wide = jnp.zeros((rows, 128), f32)
    other = mm(hots[0].astype(bf16), (second.astype(f32) + wide).astype(bf16), TN) + mm(
        hots[1].astype(bf16), (first.astype(f32) + wide).astype(bf16), TN
    )
    g_ref[:, width:] = other.astype(bf16)


def forward_kernel(far_ref, out_ref):
    out_ref[...] = far_ref[far_ref.shape[0] - out_ref.shape[0] :, :]


def attn_forward_kernel(
    w_ref, pack_a_in, pack_b_in, far_c, far_d, col_a_in, col_b_in, table_ref,
    mix_a, mix_b, mix_c, mix_d, small_ref, small_out, mixed_out, probs_out, qkv_out, normed_out, weight_out, token_out,
    ids_out,
    mixed_ref, probs_ref, qkv_ref, normed_ref, weight_ref, token_ref, ids_ref, shift_ref,
    pack_a, pack_b, col_a, col_b, sems, in_sems,
):
    w = w_ref[0]
    fetches = start_copies(
        [(pack_a_in, pack_a), (pack_b_in, pack_b), (col_a_in, col_a), (col_b_in, col_b)], in_sems
    )
    mixes = (mix_a, mix_b, mix_c, mix_d)
    blocks = len(mixes)
    heads, seq, _ = probs_ref.shape
    rows, width = seq // blocks, normed_ref.shape[1]
    shard = width // blocks
    dim = shard // heads
    half, middle = shard // 2, far_c.shape[1] // 2
    weight_ref[2 ^ w, :half] = far_c[:half, : 3 * shard]
    weight_ref[2 ^ w, half:] = far_c[:half, middle : middle + 3 * shard]
    weight_ref[3 ^ w, :half] = far_d[:half, : 3 * shard]
    weight_ref[3 ^ w, half:] = far_d[:half, middle : middle + 3 * shard]
    wait_copies(fetches)
    weight_ref[w] = col_a[...]
    weight_ref[1 ^ w] = col_b[...]
    packs = ((pack_a, 0), (pack_b, 0), (far_c, 2 * half), (far_d, half))
    for k, (ref, at) in enumerate(packs):
        shift_ref[k ^ w] = ref[at + rows :, :shard]
        ids_ref[k ^ w] = ref[at : at + rows, width:]
    for j in range(blocks):
        small_ref[:, j * shard : (j + 1) * shard] = shift_ref[j]
    gain = small_ref[0:1, :].astype(f32)
    weight = weight_ref[...].reshape(width, 3 * shard)
    for k, (ref, at) in enumerate(packs):
        token_ref[k ^ w] = ref[at : at + rows, :width]
        x = ref[at : at + rows, :width].astype(f32)
        normed = (x * norm_scale(x) * gain).astype(bf16)
        place = pl.ds(pl.multiple_of((k ^ w) * rows, rows), rows)
        normed_ref[place, :] = normed
        qkv_ref[place, :] = mm(normed, weight).astype(bf16)
    copies = start_copies(
        [
            (qkv_ref, qkv_out),
            (normed_ref, normed_out),
            (weight_ref, weight_out),
            (token_ref, token_out),
            (ids_ref, ids_out),
            (small_ref, small_out),
        ],
        sems,
    )
    below = lax.broadcasted_iota(jnp.int32, (rows, rows), 1) <= lax.broadcasted_iota(
        jnp.int32, (rows, rows), 0
    )
    for i in range(blocks):
        span = (i + 1) * rows
        ids = ids_ref[i].astype(f32).astype(jnp.int32)
        for h in range(heads):
            query = qkv_ref[i * rows : span, h * dim : (h + 1) * dim]
            keys = qkv_ref[:span, shard + h * dim : shard + (h + 1) * dim]
            values = qkv_ref[:span, 2 * shard + h * dim : 2 * shard + (h + 1) * dim]
            raw = mm(query, keys, NT) * 0.125
            table = jnp.broadcast_to(table_ref[h : h + 1, :], (rows, table_ref.shape[1]))
            bias = [
                jnp.take_along_axis(table, ids[:, j * rows : (j + 1) * rows], axis=1)
                for j in range(i + 1)
            ]
            scores = raw + jnp.concatenate(bias, axis=1) if i else raw + bias[0]
            last = jnp.where(below, scores[:, i * rows :], -1000000000.0)
            scores = jnp.concatenate([scores[:, : i * rows], last], axis=1) if i else last
            raised = jnp.exp(scores - jnp.max(scores, axis=-1, keepdims=True))
            probs = raised / jnp.sum(raised, axis=-1, keepdims=True)
            probs_ref[h, i * rows : span, :span] = probs
            mixed_ref[i, :, h * dim : (h + 1) * dim] = mm(probs.astype(bf16), values).astype(bf16)
        done = slice(i * rows, span)
        copies += start_copies(
            [(probs_ref.at[:, done, :span], probs_out.at[:, done, :span])], sems, 6 + i
        )
    copies += start_copies([(mixed_ref, mixed_out)], sems, 6 + blocks)
    for k in range(blocks):
        mixes[k][...] = mixed_ref[k ^ w]
    wait_copies(copies)


def project_kernel(
    tok_in, small_ref, hot_in, g_in, mix_a, mix_b, mix_c, mix_d, out_a, out_b, out_c, out_d,
    n_ref, residual_out, g_out, tok_ref, hot_ref, residual_ref, sems,
):
    copies = start_copies([(tok_in, tok_ref), (hot_in, hot_ref)], sems)
    g_out[...] = g_in[...]
    residual = 0.0
    for mix, out in ((mix_a, out_a), (mix_b, out_b), (mix_c, out_c), (mix_d, out_d)):
        residual = residual + mm(mix[...], out[...])
    copies[0].wait()
    residual = residual + tok_ref[...].astype(f32)
    residual_ref[...] = residual
    copies += start_copies([(residual_ref, residual_out)], sems, 2)
    normed = (residual * norm_scale(residual) * small_ref[1:2, :].astype(f32)).astype(bf16)
    copies[1].wait()
    n_ref[...] = mm(hot_ref[...], normed, TN).astype(bf16)
    wait_copies(copies[2:])


def expert_kernel(firsts, e_ref, *refs):
    e = e_ref[0]
    count = len(firsts)
    n_refs, g_refs, refs = refs[:count], refs[count : 2 * count], refs[2 * count :]
    (in_ref, out_ref, small_ref), slot_refs, refs = refs[:3], refs[3 : 3 + count], refs[3 + count :]
    hidden_out, pre_out, router_out, hidden_ref, pre_ref, router_ref, sems = refs
    rows, width = n_refs[0].shape
    n = jnp.concatenate([ref[...] for ref in n_refs], axis=0)
    g_all = jnp.concatenate(
        [ref[first : first + rows, :] for first, ref in zip(firsts, g_refs)], axis=0
    )
    g = g_all[:, :width]
    logits = mm(n, small_ref[...], NT)
    lanes = lax.broadcasted_iota(jnp.int32, logits.shape, 1)
    other = g_all[:, width : width + 1].astype(f32).astype(jnp.int32)
    differ = (lanes == 2 + e).astype(f32) - (lanes == 2 + other).astype(f32)
    gate = 1.0 / (1.0 + jnp.exp(-jnp.sum(logits * differ, axis=-1, keepdims=True)))
    pre = mm(n, in_ref[...])
    back = mm(g, out_ref[...], NT)
    square = pre * pre
    bent = jnp.tanh(0.7978845608028654 * pre * (1.0 + 0.044715 * square))
    hidden = 0.5 * pre * (1.0 + bent)
    hidden_ref[...] = (gate * hidden).astype(bf16)
    slope = 0.5 * (1.0 + bent) + 0.5 * pre * (1.0 - bent * bent) * (
        0.7978845608028654 * (1.0 + 3.0 * 0.044715 * square)
    )
    g_gate = jnp.sum(hidden * back, axis=-1, keepdims=True)
    g_logit = (gate * (1.0 - gate) * g_gate * differ).astype(bf16)
    router_ref[...] = mm(g_logit, n, TN)
    g_pre = (gate * back * slope).astype(bf16)
    pre_ref[...] = g_pre
    copies = start_copies(
        [(hidden_ref, hidden_out), (pre_ref, pre_out), (router_ref, router_out)], sems
    )
    slot = mm(g_pre, in_ref[...], NT) + mm(g_logit, small_ref[...])
    for i, ref in enumerate(slot_refs):
        ref[...] = slot[i * rows : (i + 1) * rows].astype(bf16)
    wait_copies(copies)


def result_kernel(in_a, in_b, in_c, in_d, w_ref, *refs):
    outs, held, sems = refs[:4], refs[4:8], refs[8]
    copies = start_copies(list(zip((in_a, in_b, in_c, in_d), held)), sems)
    half = outs[0].shape[0] // 2
    for i in range(4):
        copies[i].wait()
        value = mm(held[i][...], w_ref[...]).astype(bf16)
        if i < 2:
            outs[i][...] = value
        else:
            at = slice((i - 2) * half, (i - 1) * half)
            outs[2][at, :] = value[:half]
            outs[3][at, :] = value[half:]


def expert_grad_kernel(plan, *refs):
    n_count = 1 + max(n for pieces in plan for n, _, _ in pieces)
    g_count = 1 + max(g for pieces in plan for _, g, _ in pieces)
    runs = len(plan)
    n_refs, g_refs, refs = refs[:n_count], refs[n_count : n_count + g_count], refs[n_count + g_count :]
    ins, (g_in, g_out, token_ref), refs = refs[: 2 * runs], refs[2 * runs : 2 * runs + 3], refs[2 * runs + 3 :]
    held, sems = refs[: 2 * runs], refs[-1]
    token_ref[...] = jnp.zeros_like(token_ref)
    copies = start_copies(list(zip(ins, held)), sems)
    width = n_refs[0].shape[1]
    first_term = True
    for i, pieces in enumerate(plan):
        copies[i].wait()
        copies[runs + i].wait()
        at = 0
        for n_at, g_at, first in pieces:
            n = n_refs[n_at][...]
            rows = n.shape[0]
            pre, hidden = held[i][at : at + rows, :], held[runs + i][at : at + rows, :]
            g = g_refs[g_at][first : first + rows, :width]
            at += rows
            for ref, term in ((g_in, mm(n, pre, TN)), (g_out, mm(hidden, g, TN))):
                if first_term:
                    ref[...] = term
                else:
                    ref[...] += term
            first_term = False


def pair_kernel(*refs):
    count = (len(refs) - 1) // 2
    step = refs[0].shape[0]
    for i in range(count):
        total = refs[i][...].astype(f32) + refs[count + i][...].astype(f32)
        refs[-1][i * step : (i + 1) * step, :] = total.astype(bf16)


def total_kernel(own_ref, beside_ref, *refs):
    across, out_ref = refs[:-1], refs[-1]
    step = out_ref.shape[0] // len(across)
    for a, ref in enumerate(across):
        at = slice(a * step, (a + 1) * step)
        total = own_ref[at, :].astype(f32) + beside_ref[at, :].astype(f32) + ref[...].astype(f32)
        out_ref[at, :] = total.astype(bf16)


def second_norm_kernel(
    residual_in, small_in, hot_in, grad_in, got_ref, low_ref, gain_ref, grad_residual_out,
    residual_ref, small_ref, hot_ref, grad_ref, grad_residual_ref, sems,
):
    copies = start_copies(
        [(hot_in, hot_ref), (residual_in, residual_ref), (small_in, small_ref), (grad_in, grad_ref)],
        sems,
    )
    wait_copies(copies)
    g_normed = mm(hot_ref[...], got_ref[...])
    residual = residual_ref[...]
    scale = norm_scale(residual)
    scaled = g_normed * small_ref[1:2, :].astype(f32)
    grad = (
        grad_ref[...].astype(f32)
        + scale * scaled
        - residual * scale * scale * scale * jnp.mean(scaled * residual, axis=-1, keepdims=True)
    )
    grad_residual_ref[...] = grad
    stores = start_copies([(grad_residual_ref, grad_residual_out)], sems, 4)
    low_ref[...] = grad.astype(bf16)
    gain_ref[...] = jnp.sum(g_normed * residual * scale, axis=0, keepdims=True)
    wait_copies(stores)


def block_out_kernel(residual_ref, hot_ref, got_ref, out_ref):
    out_ref[...] = (residual_ref[...] + mm(hot_ref[...], got_ref[...])).astype(bf16)


def attn_backward_kernel(
    ids_ref, grad_a, grad_b, grad_c, grad_d, wout_in, qkv_in, probs_in,
    grads_ref, scores_out, wout_ref, qkv_ref, probs_ref, scores_ref, gmix_ref, part_ref, sems,
):
    w = ids_ref[0]
    packs = (grad_a, grad_b, grad_c, grad_d)
    blocks = len(packs)
    rows = grad_a.shape[0]
    spans = [(slice(i * rows, (i + 1) * rows), (i + 1) * rows) for i in range(blocks)]
    copies = start_copies(
        [(wout_in, wout_ref), (qkv_in, qkv_ref)]
        + [(probs_in.at[:, at, :span], probs_ref.at[:, at, :span]) for at, span in spans],
        sems,
    )
    copies[0].wait()
    rows, width = grad_a.shape
    shard = width // blocks
    heads = probs_ref.shape[0]
    dim = shard // heads
    for k in range(blocks):
        place = pl.ds(pl.multiple_of((k ^ w) * rows, rows), rows)
        gmix_ref[place, :] = mm(packs[k][...], wout_ref[...], NT).astype(bf16)
    part_ref[...] = jnp.zeros_like(part_ref)
    copies[1].wait()
    stores = []
    for i in range(blocks):
        span = (i + 1) * rows
        copies[2 + i].wait()
        for h in range(heads):
            query = qkv_ref[i * rows : span, h * dim : (h + 1) * dim]
            keys = qkv_ref[:span, shard + h * dim : shard + (h + 1) * dim]
            values = qkv_ref[:span, 2 * shard + h * dim : 2 * shard + (h + 1) * dim]
            gmix = gmix_ref[i * rows : span, h * dim : (h + 1) * dim]
            probs = probs_ref[h, i * rows : span, :span]
            gprobs = mm(gmix, values, NT)
            inner = jnp.sum(probs * gprobs, axis=-1, keepdims=True)
            gscores = probs * (gprobs - inner)
            scores_ref[h, i * rows : span, :span] = gscores
            low = gscores.astype(bf16)
            grads_ref[i * rows : span, h * dim : (h + 1) * dim] = (mm(low, keys) * 0.125).astype(
                bf16
            )
            part_ref[0, h, :span, :] += mm(low, query, TN)
            part_ref[1, h, :span, :] += mm(probs.astype(bf16), gmix, TN)
        at = slice(i * rows, span)
        stores += start_copies(
            [(scores_ref.at[:, at, :span], scores_out.at[:, at, :span])], sems, 2 + blocks + i
        )
    for h in range(heads):
        grads_ref[:, shard + h * dim : shard + (h + 1) * dim] = (part_ref[0, h] * 0.125).astype(
            bf16
        )
        grads_ref[:, 2 * shard + h * dim : 2 * shard + (h + 1) * dim] = part_ref[1, h].astype(bf16)
    wait_copies(stores)


def weight_grad_kernel(
    ids_ref, grad_a, grad_b, grad_c, grad_d, normed_in, mixed_in, grads_ref, *refs
):
    *outs, stage_ref, normed_ref, mixed_ref, sems = refs
    w = ids_ref[0]
    copies = start_copies([(mixed_in, mixed_ref), (normed_in, normed_ref)], sems)
    copies[0].wait()
    gout = functools.reduce(
        lambda p, q: p + q,
        [
            mm(mixed_ref[k ^ w], ref[...], TN)
            for k, ref in enumerate((grad_a, grad_b, grad_c, grad_d))
        ],
    )
    copies[1].wait()
    gqkv = mm(normed_ref[...], grads_ref[...], TN)
    if len(outs) == 2:
        outs[0][...] = gqkv
        outs[1][...] = gout
        return
    ne = stage_ref.shape[0]
    shard, width = gout.shape
    nw = width // shard
    piece = shard // ne
    for j in range(nw):
        for s in range(ne):
            row = j * shard + s * piece
            stage_ref[s, j ^ w, :, : 3 * shard] = gqkv[row : row + piece].astype(bf16)
            stage_ref[s, j, :, 3 * shard :] = gout[
                s * piece : (s + 1) * piece, j * shard : (j + 1) * shard
            ].astype(bf16)
    wait_copies(start_copies([(stage_ref, outs[0])], sems, 2))


def weight_sum_kernel(in_ref, *refs):
    outs, gout_ref = refs[:-1], refs[-1]
    for k, out in enumerate(outs):
        total = functools.reduce(
            lambda p, q: p + q, [in_ref[i, k].astype(f32) for i in range(in_ref.shape[0])]
        )
        cut = out.shape[1]
        out[...] = total[:, :cut].astype(bf16)
        gout_ref[k] = total[:, cut:].astype(bf16)


def weight_pack_kernel(a_ref, b_ref, c_ref, d_ref, gout_ref, few_ref, bias_ref, out_ref, stage):
    piece, cut = a_ref.shape
    width = stage.shape[1]
    shard = width - cut
    stage[...] = jnp.zeros_like(stage)
    for k, ref in enumerate((a_ref, b_ref, c_ref, d_ref)):
        stage[k * piece : (k + 1) * piece, :cut] = ref[...].astype(f32)
        stage[k * piece : (k + 1) * piece, cut:] = gout_ref[k].astype(f32)
    at = 4 * piece
    few = few_ref[...]
    high = few.astype(bf16).astype(f32)
    for i, part in enumerate((high[:8], high[8:], (few - high)[:8], (few - high)[8:])):
        if i % 2 == 0:
            stage[at : at + 8, i * shard : (i + 1) * shard] = part
        else:
            stage[at : at + 4, i * shard : (i + 1) * shard] = part[:4]
    bias = bias_ref[...]
    high = bias.astype(bf16).astype(f32)
    stage[at + 4 : at + 8, shard : shard + 128] = high[:4]
    stage[at + 4 : at + 8, 3 * shard : 3 * shard + 128] = (bias - high)[:4]
    out_ref[...] = stage[...].astype(bf16)


def weight_join_kernel(ids_ref, *refs):
    w, e = ids_ref[0], ids_ref[1]
    ins, outs, one_ref, two_ref, router_ref, bias_ref, stage = (
        refs[:-9], refs[-9:-5], refs[-5], refs[-4], refs[-3], refs[-2], refs[-1]
    )
    shard, width = outs[0].shape
    nw, piece = width // shard, stage.shape[1]
    at = nw * piece
    few = 0.0
    for k, ref in enumerate(ins):
        place = pl.ds(pl.multiple_of((k ^ e) * piece, piece), piece)
        value = ref[...].astype(f32)
        for j in range(nw):
            mine = value[j * piece : (j + 1) * piece]
            stage[j ^ w] = mine
            outs[3][place, j * shard : (j + 1) * shard] = mine[:, 3 * shard :]
        for j in range(nw):
            mine = stage[j]
            for i in range(3):
                outs[i][place, j * shard : (j + 1) * shard] = mine[:, i * shard : (i + 1) * shard]
        few += value[at:, : 2 * shard] + value[at:, 2 * shard :]
    one_ref[...] = few[0:1, :shard]
    two_ref[...] = few[1:2, :shard]
    bias = few[4:5, shard:]
    experts = router_ref.shape[0]
    router_ref[:6, :] = few[2:8, :shard]
    router_ref[6:, :] = few[: experts - 6, shard:]
    heads, bins = bias_ref.shape
    for h in range(heads):
        bias_ref[h : h + 1, :] = bias[:, h * bins : (h + 1) * bins]


def input_grad_kernel(
    w_ref, grads_ref, weight_in, token_in, gain_ref, *refs,
):
    *router_in, back_a, back_b, back_c, back_d, few_ref, weight_ref, token_ref, router_ref, sems = (
        refs
    )
    w = w_ref[0]
    wait_copies(
        start_copies(
            [(weight_in, weight_ref), (token_in, token_ref)]
            + [(ref, router_ref.at[i]) for i, ref in enumerate(router_in)],
            sems,
        )
    )
    backs = (back_a, back_b, back_c, back_d)
    blocks, rows, width = token_ref.shape
    shard = width // blocks
    weight = weight_ref[...].reshape(width, 3 * shard)
    total = jnp.zeros((1, width), f32)
    for k in range(blocks):
        place = pl.ds(pl.multiple_of((k ^ w) * rows, rows), rows)
        back = mm(grads_ref[place, :], weight, NT)
        backs[k][:rows, :] = back.astype(bf16)
        x = token_ref[k ^ w].astype(f32)
        total += jnp.sum(back * x * norm_scale(x), axis=0, keepdims=True)
    few = jnp.sum(router_ref[...], axis=0)
    line = lax.broadcasted_iota(jnp.int32, few.shape, 0)
    few = jnp.where(line == 0, total, jnp.where(line == 1, gain_ref[...], few))
    for j in range(blocks):
        few_ref[j] = few[:, j * shard : (j + 1) * shard].astype(bf16)
    for k in range(blocks):
        backs[k][rows:, :] = jnp.zeros((few.shape[0], width), bf16)
        backs[k][rows:, :shard] = few_ref[k ^ w]


def bias_grad_kernel(ids_in, scores_in, out_ref, part_ref, ids_ref, scores_ref, sems):
    wait_copies(start_copies([(ids_in, ids_ref), (scores_in, scores_ref)], sems))
    heads, seq, _ = scores_ref.shape
    blocks, rows, _ = ids_ref.shape
    bins = part_ref.shape[0] // heads
    part_ref[...] = jnp.zeros_like(part_ref)
    for i in range(blocks):
        span = (i + 1) * rows
        ids = ids_ref[i, :, :span].astype(f32).astype(jnp.int32)
        for b in range(bins):
            hit = ids == b
            for h in range(heads):
                picked = jnp.where(hit, scores_ref[h, i * rows : span, :span], 0.0)
                part_ref[h * bins + b : h * bins + b + 1, :] += functools.reduce(
                    lambda p, q: p + q,
                    [
                        jnp.sum(picked[:, j * rows : (j + 1) * rows], axis=0, keepdims=True)
                        for j in range(i + 1)
                    ],
                )
    spread_out = jnp.concatenate(
        [part_ref[...], jnp.zeros((128 - part_ref.shape[0], 128), f32)], axis=0
    )
    out_ref[...] = lax.dot_general(
        jnp.ones((8, 128), f32), spread_out, NT, precision=lax.Precision.HIGHEST,
        preferred_element_type=f32,
    )


def tokens_grad_kernel(
    tok_ref, small_ref, residual_ref, a_ref, b_ref, c_ref, out_ref, few_ref
):
    rows = tok_ref.shape[0]
    shard = few_ref.shape[1]
    total = a_ref[...].astype(f32) + b_ref[...].astype(f32) + c_ref[...].astype(f32)
    grad = total[:rows]
    few_ref[...] = total[rows:, :shard]
    x = tok_ref[...].astype(f32)
    scale = norm_scale(x)
    scaled = grad * small_ref[0:1, :].astype(f32)
    out_ref[...] = (
        residual_ref[...]
        + scale * scaled
        - x * scale * scale * scale * jnp.mean(scaled * x, axis=-1, keepdims=True)
    )


def shaped(shape, dtype=bf16):
    return jax.ShapeDtypeStruct(shape, dtype)


def on_chip(
    kernel, outs, scratch, *args, scalars=(0,), flops=0, stay=(), leave=(), deps=(), limit=32,
    weight=1000,
):
    count = len(args)
    args = [
        pltpu.with_memory_space_constraint(a, pltpu.HBM) if i in stay else a
        for i, a in enumerate(args)
    ]
    places = [
        pltpu.SMEM if i in scalars else pltpu.HBM if i in stay else pltpu.VMEM
        for i in range(count)
    ] + [pl.ANY] * len(deps)

    def run(*refs):
        kernel(*refs[:count], *refs[count + len(deps) :])

    size = sum(a.size * a.dtype.itemsize for a in (*args, *outs))
    return pl.pallas_call(
        run,
        out_shape=[
            pltpu.HBM(a.shape, a.dtype) if i in leave else a for i, a in enumerate(outs)
        ],
        in_specs=[pl.BlockSpec(memory_space=place) for place in places],
        out_specs=[
            pl.BlockSpec(memory_space=pltpu.HBM if i in leave else pltpu.VMEM)
            for i in range(len(outs))
        ],
        scratch_shapes=scratch,
        compiler_params=pltpu.CompilerParams(vmem_limit_bytes=limit * 1024 * 1024),
        cost_estimate=pl.CostEstimate(
            flops=flops + weight * size, bytes_accessed=size * weight // 1000, transcendentals=0
        ),
    )(*args, *deps)


def hold(value, *deps):
    return pl.pallas_call(
        lambda *refs: None,
        out_shape=shaped(value.shape, value.dtype),
        in_specs=[pl.BlockSpec(memory_space=pl.ANY)] * (1 + len(deps)),
        out_specs=pl.BlockSpec(memory_space=pl.ANY),
        input_output_aliases={0: 0},
        cost_estimate=pl.CostEstimate(flops=0, bytes_accessed=0, transcendentals=0),
    )(value, *deps)


def run_expert(pieces, e_arr, w_in, w_out, small, deps=()):
    rows, width = pieces[0][0].shape
    hidden = w_in.shape[1]
    count = len(pieces)
    kept = [
        shaped((rows * count, hidden)), shaped((rows * count, hidden)),
        shaped((small.shape[0], width), f32),
    ]
    return on_chip(
        functools.partial(expert_kernel, [first for _, _, first in pieces]),
        [shaped((rows, width))] * count + kept,
        [pltpu.VMEM(a.shape, a.dtype) for a in kept] + [pltpu.SemaphoreType.DMA((3,))],
        e_arr, *[n for n, _, _ in pieces], *[g for _, g, _ in pieces], w_in, w_out, small,
        leave=range(count, count + 3), deps=deps,
    )


def add_pair(mine, other, deps=()):
    other = send_xor(other, "wshard", 1)
    return on_chip(
        pair_kernel, [shaped(other.shape)], [], mine, other, scalars=(), deps=deps
    )[0]


def scatter_parts(parts, deps=()):
    across = send_xor(add_pair(parts[2], parts[3], deps), "wshard", 2)
    beside = send_xor(parts[1], "wshard", 1)
    return parts[0], beside, across


def body(
    tokens, routes, buckets, gain_one, w_query, w_key, w_value, w_output, pos_bias, gain_two,
    w_router, expert_in, expert_out, grad_out,
):
    rows, width = tokens.shape
    nw, ne = lax.axis_size("wshard"), lax.axis_size("expert")
    w, e = lax.axis_index("wshard"), lax.axis_index("expert")
    w_arr, e_arr = w.astype(jnp.int32).reshape(1), e.astype(jnp.int32).reshape(1)
    ids = jnp.concatenate([w_arr, e_arr])
    shard = width // nw
    heads, bins = pos_bias.shape
    dim = shard // heads
    seq = rows * nw
    experts = w_router.shape[1]
    cap = 3 * rows * TOPK // (2 * experts)
    slots = experts * cap
    few_rows = -(-(2 + experts) // 16) * 16

    far, pack, col_own, col_near = on_chip(
        pack_kernel,
        [
            shaped((shard + rows + few_rows, width + seq)),
            shaped((rows + few_rows, width + seq)),
            shaped((shard, 3 * shard)),
            shaped((shard, 3 * shard)),
        ],
        [
            pltpu.VMEM((rows, width), bf16),
            pltpu.VMEM((rows, seq), jnp.int32),
            pltpu.VMEM((shard, width), bf16),
            pltpu.VMEM((shard, width), bf16),
            pltpu.VMEM((shard, width), bf16),
            pltpu.VMEM((shard,), bf16),
            pltpu.VMEM((shard,), bf16),
            pltpu.VMEM((experts, shard), bf16),
            pltpu.VMEM((shard, 3 * shard), bf16),
            pltpu.SemaphoreType.DMA((9,)),
        ],
        w_arr, gain_one, gain_two, w_router.T, tokens, buckets, w_query, w_key, w_value,
        stay=range(1, 9), leave=(2,),
    )
    far_c = send_xor(far, "wshard", 2)
    pack_b, col_b = send_xor(pack, "wshard", 1), send_xor(col_near, "wshard", 1)
    hot, g_rows = on_chip(
        functools.partial(route_kernel, cap),
        [shaped((rows, slots)), shaped((slots, width + 128))],
        [],
        routes, grad_out, scalars=(), deps=(pack_b, col_b),
    )
    g_got = send_rows(g_rows, experts)
    far_rest = on_chip(
        forward_kernel, [shaped((far.shape[0] - shard // 2, far.shape[1]))], [], far_c,
        scalars=(),
    )[0]
    far_d = send_xor(far_rest, "wshard", 1)
    wout_far, wout_near = send_xor(w_output, "wshard", 2), send_xor(w_output, "wshard", 1)

    table = jnp.zeros((8, 128), f32).at[:heads, :bins].set(pos_bias.astype(f32))
    kept = [
        shaped((few_rows, width)),
        shaped((nw, rows, shard)),
        shaped((heads, seq, seq), f32),
        shaped((seq, 3 * shard)),
        shaped((seq, width)),
        shaped((nw, shard, 3 * shard)),
        shaped((nw, rows, width)),
        shaped((nw, rows, seq)),
    ]
    *mixed, small, small_far, mixed_far, probs, qkv, normed_one, weight, tok_all, bucket_all = on_chip(
        attn_forward_kernel,
        [shaped((rows, shard))] * nw + [shaped((few_rows, width))] + kept,
        [pltpu.VMEM(a.shape, a.dtype) for a in kept[1:]]
        + [
            pltpu.VMEM((nw, few_rows, shard), bf16),
            pltpu.VMEM(pack.shape, bf16),
            pltpu.VMEM(pack.shape, bf16),
            pltpu.VMEM(col_own.shape, bf16),
            pltpu.VMEM(col_own.shape, bf16),
            pltpu.SemaphoreType.DMA((7 + nw,)),
            pltpu.SemaphoreType.DMA((4,)),
        ],
        w_arr, pack, pack_b, far_c, far_d, col_own, col_b, table,
        stay=(1, 2, 5, 6), leave=range(nw + 1, nw + 9), weight=200,
    )
    mixed_got = exchange(mixed, "wshard")
    wout_rest = on_chip(
        forward_kernel, [shaped(w_output.shape)], [], wout_far, scalars=(), deps=(mixed[0], g_got)
    )[0]
    wout_all = [w_output, wout_near, wout_far, send_xor(wout_rest, "wshard", 1)]
    n_rows, residual, g_mine = on_chip(
        project_kernel,
        [shaped((slots, width)), shaped((rows, width), f32), shaped(g_got.shape)],
        [
            pltpu.VMEM((rows, width), bf16),
            pltpu.VMEM((rows, slots), bf16),
            pltpu.VMEM((rows, width), f32),
            pltpu.SemaphoreType.DMA((3,)),
        ],
        tokens, small, hot, g_got, *mixed_got, *wout_all,
        scalars=(), stay=(0, 2), leave=(1,),
    )

    w_in, w_back = expert_in[0], expert_out[0]
    half = slots // 2
    g_parts = gather_w(g_mine)
    n_got = send_rows(n_rows, experts)
    n_far = [send_xor(n_got[a * half : (a + 1) * half], "wshard", 2) for a in range(2)]
    n_near = send_xor(n_got, "wshard", 1)
    plan = [
        [(0, 0, 0)], [(1, 1, 0)], [(2, 2, 0), (3, 3, 0)], [(4, 2, half), (5, 3, half)]
    ]
    n_all = [n_got, n_near]
    runs, order = [], ()
    for step, pieces in enumerate(plan):
        if step >= 2:
            n = n_far[step - 2]
            if step == 2:
                rest = on_chip(forward_kernel, [shaped(n.shape)], [], n, scalars=(), deps=order)[0]
            else:
                rest = n
            n_all += [n, send_xor(rest, "wshard", 1)]
        run = run_expert(
            [(n_all[n], g_parts[g], first) for n, g, first in pieces], e_arr, w_in, w_back, small, order
        )
        runs.append(run)
        order = run[:1]
    hidden, g_pre, g_router = zip(*(run[-3:] for run in runs))
    other = [send_xor(run[1], "wshard", 1) for run in runs[2:]]
    pair = on_chip(
        pair_kernel, [shaped((slots, width))], [], runs[2][0], runs[3][0], *other, scalars=()
    )[0]
    across = send_xor(pair, "wshard", 2)
    beside = send_xor(runs[1][0], "wshard", 1)
    parts = len(runs)
    result = on_chip(
        result_kernel, [shaped((slots, width))] * parts,
        [pltpu.VMEM((slots, width), bf16)] * parts + [pltpu.SemaphoreType.DMA((parts,))],
        *hidden, w_back, scalars=(), stay=range(parts),
    )
    g_total = on_chip(
        total_kernel, [shaped((slots, width))], [], runs[0][0], beside, across,
        scalars=(),
    )[0]
    g_back = send_rows(g_total, experts)

    result_total = on_chip(
        total_kernel, [shaped((slots, width))], [], *scatter_parts(result, deps=(g_total,)),
        scalars=(), deps=(g_back,),
    )[0]
    g_in_w, g_out_w, token = on_chip(
        functools.partial(expert_grad_kernel, plan),
        [
            shaped((width, w_in.shape[1]), f32),
            shaped((w_in.shape[1], width), f32),
            shaped((8, 128), f32),
        ],
        [pltpu.VMEM((slots, w_in.shape[1]), bf16)] * (2 * parts)
        + [pltpu.SemaphoreType.DMA((2 * parts,))],
        *n_all, *g_parts, *g_pre, *hidden,
        scalars=(), stay=range(6 + nw, 6 + nw + 2 * parts), deps=(g_total,), limit=40,
        flops=4 * 4 * slots * width * width,
    )

    grad_low, grad_gain_b, grad_residual = on_chip(
        second_norm_kernel,
        [shaped((rows, width)), shaped((1, width), f32), shaped((rows, width), f32)],
        [
            pltpu.VMEM((rows, width), f32),
            pltpu.VMEM((few_rows, width), bf16),
            pltpu.VMEM((rows, slots), bf16),
            pltpu.VMEM((rows, width), bf16),
            pltpu.VMEM((rows, width), f32),
            pltpu.SemaphoreType.DMA((5,)),
        ],
        residual, small_far, hot, grad_out, g_back,
        scalars=(), stay=range(4), leave=(2,), deps=(token,),
    )
    grad_all = gather_w(grad_low)
    result_got = send_rows(result_total, experts)

    block_out = on_chip(
        block_out_kernel, [shaped((rows, width))], [], residual, hot, result_got, scalars=()
    )[0]
    fast = ne <= 8 and shard % (8 * ne) == 0 and few_rows == 16 and 6 < experts <= 10
    piece = shard // ne
    if fast:
        weight_outs = [shaped((ne, nw, piece, width))]
    else:
        weight_outs = [shaped((width, 3 * shard), f32), shaped((shard, width), f32)]
    grads, scores = on_chip(
        attn_backward_kernel,
        [shaped((seq, 3 * shard)), shaped((heads, seq, seq), f32)],
        [
            pltpu.VMEM((shard, width), bf16),
            pltpu.VMEM((seq, 3 * shard), bf16),
            pltpu.VMEM((heads, seq, seq), f32),
            pltpu.VMEM((heads, seq, seq), f32),
            pltpu.VMEM((seq, shard), bf16),
            pltpu.VMEM((2, heads, seq, dim), f32),
            pltpu.SemaphoreType.DMA((2 + 2 * nw,)),
        ],
        ids, *grad_all, w_output, qkv, probs, stay=range(1 + nw, 4 + nw), leave=(1,),
        weight=650,
    )
    chunks = on_chip(
        weight_grad_kernel,
        weight_outs,
        [
            pltpu.VMEM((ne, nw, piece, width) if fast else (8, 128), bf16),
            pltpu.VMEM((seq, width), bf16),
            pltpu.VMEM((nw, rows, shard), bf16),
            pltpu.SemaphoreType.DMA((3,)),
        ],
        ids, *grad_all, normed_one, mixed_far, grads, stay=(1 + nw, 2 + nw),
        leave=(0,) if fast else (), weight=650,
    )
    chunks = [hold(chunks[0], result_got), *chunks[1:]]
    back = on_chip(
        input_grad_kernel,
        [shaped((rows + few_rows, width))] * nw,
        [
            pltpu.VMEM((nw, few_rows, shard), bf16),
            pltpu.VMEM((nw, shard, 3 * shard), bf16),
            pltpu.VMEM((nw, rows, width), bf16),
            pltpu.VMEM((parts, few_rows, width), f32),
            pltpu.SemaphoreType.DMA((2 + parts,)),
        ],
        w_arr, grads, weight, tok_all, grad_gain_b, *g_router,
        stay=(2, 3, *range(5, 5 + parts)), deps=chunks[:1],
    )
    bias = on_chip(
        bias_grad_kernel,
        [shaped((8, 128), f32)],
        [
            pltpu.VMEM((heads * bins, 128), f32),
            pltpu.VMEM((nw, rows, seq), bf16),
            pltpu.VMEM((heads, seq, seq), f32),
            pltpu.SemaphoreType.DMA((2,)),
        ],
        bucket_all, scores, scalars=(), stay=(0, 1), deps=chunks[:1],
    )[0]
    grad_tokens, few = on_chip(
        tokens_grad_kernel, [shaped((rows, width), f32), shaped((few_rows, shard), f32)], [],
        tokens, small, grad_residual, *scatter_parts(back), scalars=(),
    )
    if fast:
        got = lax.all_to_all(chunks[0], "expert", 0, 0, tiled=True)
        *sums, gout = on_chip(
            weight_sum_kernel,
            [shaped((piece, 3 * shard))] * nw + [shaped((nw, piece, shard))],
            [],
            got, scalars=(),
        )
        swapped = exchange(sums, "wshard")
        joined = on_chip(
            weight_pack_kernel, [shaped((nw * piece + 8, width))],
            [pltpu.VMEM((nw * piece + 8, width), f32)],
            *swapped, gout, few, bias, scalars=(),
        )[0]
        *weights, gain_a, gain_b, router, bias = on_chip(
            weight_join_kernel,
            [shaped((shard, width), f32)] * 4
            + [shaped(shape, f32) for shape in ((1, shard), (1, shard), (experts, shard), (heads, bins))],
            [pltpu.VMEM((nw, piece, width), f32)],
            ids, *spread(joined, "expert"),
        )
    else:
        gqkv, gout = chunks
        pieces_w = to_xor(to_xor(gqkv.reshape(nw, ne, piece, 3 * shard), "expert", 1), "wshard")
        pieces_w = pieces_w.astype(bf16)
        pieces_o = to_xor(gout.reshape(ne, piece, width), "expert").astype(bf16)
        add = lambda parts: functools.reduce(lambda a, b: a + b, [c.astype(f32) for c in parts])
        total = add(exchange([pieces_w[:, k] for k in range(ne)], "expert")).astype(bf16)
        total_out = add(exchange([pieces_o[k] for k in range(ne)], "expert")).astype(bf16)
        swapped = jnp.stack(exchange([total[k] for k in range(nw)], "wshard"))
        swapped = to_xor(swapped, "wshard").reshape(nw, piece, 3, shard).transpose(1, 2, 0, 3)
        joined = jnp.concatenate([swapped.reshape(piece, 3 * width), total_out], axis=1)
        whole = to_xor(jnp.stack(spread(joined, "expert")), "expert").reshape(shard, 4 * width)
        whole = whole.astype(f32)
        weights = [whole[:, i * width : (i + 1) * width] for i in range(4)]
        few, bias = lax.psum((few, bias), "expert")
        gain_a, gain_b, router = few[0], few[1], few[2 : 2 + experts]
        bias = bias[0, : heads * bins].reshape(heads, bins)
    return (
        block_out,
        grad_tokens,
        gain_a.reshape(shard),
        *weights,
        bias,
        gain_b.reshape(shard),
        router.T,
        g_in_w[None],
        g_out_w[None],
    )


def solution(mesh):
    placed = (
        P(("expert", "wshard"), None),
        P(("expert", "wshard"), None),
        P(("expert", "wshard"), None),
        P("wshard"),
        P("wshard", None),
        P("wshard", None),
        P("wshard", None),
        P("wshard", None),
        P("wshard", None),
        P("wshard"),
        P("wshard", None),
        P("expert", None, "wshard"),
        P("expert", "wshard", None),
        P(("expert", "wshard"), None),
    )
    return jax.shard_map(
        body,
        mesh=mesh,
        in_specs=placed,
        out_specs=(
            P(("expert", "wshard"), None),
            P(("expert", "wshard"), None),
            P("wshard"),
            P("wshard", None),
            P("wshard", None),
            P("wshard", None),
            P("wshard", None),
            P("wshard", None),
            P("wshard"),
            P("wshard", None),
            P("expert", None, "wshard"),
            P("expert", "wshard", None),
        ),
        check_vma=False,
    )
```
